32 devices in a mesh: dp: 4 (over y, core), space: 8 (over z, x).
Axes of the slice: x: 2, y: 2, z: 4, core: 2. Of those that a mesh axis runs over, the one named last changes fastest.
Arguments:
- snapshot: bfloat16 [4, 32, 64, 1024], P('dp', 'space'), may hold values from -6 to 6
- conv_one: bfloat16 [864, 128], replicated, may hold values from -0.21875 to 0.21875
- conv_two: bfloat16 [3456, 256], replicated, may hold values from -0.0546875 to 0.0546875
- cotangent: bfloat16 [4, 256, 8, 128], P('dp', 'space'), may hold values from -0.046875 to 0.046875
Outputs:
- latent: bfloat16 [4, 256, 8, 128], P('dp', 'space')
- grad_one: float32 [128, 864], P('space')
- grad_two: float32 [256, 3456], P('space')
The draws below stay inside these ranges and needn't reach their ends.
All inputs are finite; a program needn't handle non-finite values.
Results may differ from the reference program's by a relative error of at most 0.0049.
Values may be sent and summed in bfloat16 or wider, within the bound.
No kernel may reach another device: no remote copies, remote signals or barrier semaphores. Data moves between devices by JAX's collectives and lax.ppermute only.
A program may use at most 64 MiB of HBM per device.

```python
import jax
import jax.numpy as jnp
from jax import lax

CH_IN = 32
CH_MID = 128
CH_OUT = 256
Y_CELLS = 64
Z_CELLS = 32
SAMPLES = 4
NX = 32
NX_LATENT = 8
YZ_LATENT = 128


def spiked(drawn, own_key, source, target, shards_of, factor):
    owner, partner = [(jnp.arange(drawn.shape[axis_at]) // (drawn.shape[axis_at] // shards_of)).reshape([-1 if axis == axis_at else 1 for axis in range(drawn.ndim)]) for axis_at in (source, target)]
    chosen = jax.random.permutation(own_key, shards_of)[partner]
    strong = (owner == chosen) | (owner == (partner + shards_of // 2) % shards_of)
    return jnp.where(strong, factor * drawn, drawn)


def steps_of(own_key, extent, cuts, smallest, high):
    factor_of, own = 1.0, jax.random.fold_in(own_key, 6)
    for dim, blocks in cuts:
        steps = jnp.exp(jax.random.uniform(jax.random.fold_in(own, dim), (blocks,), jnp.float32, smallest / len(cuts), high / len(cuts)))
        factor_of = factor_of * jnp.repeat(steps, extent[dim] // blocks).reshape([-1 if axis == dim else 1 for axis in range(len(extent))])
    return factor_of


def bell_draw(rng, extent, scale, bound, shards=(), dtype=jnp.bfloat16):
    result = jax.random.normal(rng, extent, jnp.float32) * scale
    if len(shards) > 0:
        result = steps_of(rng, extent, shards, -0.22, 0.18) * result
    return jnp.clip(result, min=-bound, max=bound).astype(dtype)


def heavy_noise(rng, dims, spread, bound, shards, heavy, dtype=jnp.bfloat16):
    array = spread * jax.random.normal(rng, dims, jnp.float32)
    if shards:
        array = array * steps_of(rng, dims, shards, -0.22, 0.18)
    return jnp.clip(spiked(array, jax.random.fold_in(rng, 3), *heavy), -bound, bound).astype(dtype)


def setup_inputs(seed: int = 0) -> dict:
    splits = jax.random.split(jax.random.key(seed), 5)
    snapshot = bell_draw(splits[0], (SAMPLES, NX, Y_CELLS, Z_CELLS * CH_IN), 1.0, 6.0, ((0, 4), (1, 8)))
    conv_one = bell_draw(splits[1], (27 * CH_IN, CH_MID), (27 * CH_IN) ** -0.5, 0.21875)
    conv_two = bell_draw(splits[2], (27 * CH_MID, CH_OUT), (4 * 27 * CH_MID) ** -0.5, 0.0546875)
    cotangent = heavy_noise(splits[3], (SAMPLES, CH_OUT, NX_LATENT, YZ_LATENT), 0.006, 0.046875, ((0, 4), (1, 8)), (0, 1, 4, 2.0))
    return {"snapshot": snapshot, "conv_one": conv_one, "conv_two": conv_two, "cotangent": cotangent}


def patches(padded, out_x, out_y, out_z):
    channels = padded.shape[3]
    grown = jnp.pad(padded, ((0, 1), (0, 1), (0, 1), (0, 0)))
    phased = grown.reshape(out_x + 1, 2, out_y + 1, 2, out_z + 1, 2, channels)
    pieces = []
    for tap_x in range(3):
        for tap_y in range(3):
            for tap_z in range(3):
                start = (tap_x // 2, tap_x % 2, tap_y // 2, tap_y % 2, tap_z // 2, tap_z % 2, 0)
                limit = (tap_x // 2 + out_x, tap_x % 2 + 1, tap_y // 2 + out_y, tap_y % 2 + 1, tap_z // 2 + out_z, tap_z % 2 + 1, channels)
                pieces.append(lax.slice(phased, start, limit).reshape(out_x, out_y, out_z, channels))
    stacked = jnp.concatenate(pieces, axis=3)
    return stacked.reshape(out_x * out_y * out_z, 27 * channels)


def fold_axis(blocks, space, tap):
    first_tap = lax.index_in_dim(blocks, 0, tap, keepdims=False)
    middle_tap = lax.index_in_dim(blocks, 1, tap, keepdims=False)
    last_tap = lax.index_in_dim(blocks, 2, tap, keepdims=False)
    after = [(0, 0)] * first_tap.ndim
    before = [(0, 0)] * first_tap.ndim
    after[space] = (0, 1)
    before[space] = (1, 0)
    even_cells = jnp.pad(first_tap, after) + jnp.pad(last_tap, before)
    odd_cells = jnp.pad(middle_tap, after)
    joined = jnp.stack([even_cells, odd_cells], axis=space + 1)
    shape = list(even_cells.shape)
    shape[space] = 2 * shape[space]
    return joined.reshape(shape)


def spread_taps(back_rows, out_x, out_y, out_z):
    channels = back_rows.shape[1] // 27
    blocks = back_rows.reshape(out_x, out_y, out_z, 3, 3, 3, channels)
    blocks = fold_axis(blocks, 2, 5)
    blocks = fold_axis(blocks, 1, 4)
    blocks = fold_axis(blocks, 0, 3)
    return blocks[:2 * out_x + 1, :2 * out_y + 1, :2 * out_z + 1]


def silu_slope(values):
    logistic = jax.nn.sigmoid(values)
    return logistic * (1.0 + values * (1.0 - logistic))


def sample_pass(field_cells, upstream, conv_one, conv_two):
    in_width = conv_one.shape[0] // 27
    mid_width = conv_one.shape[1]
    out_width = conv_two.shape[1]
    fine_grid = field_cells.reshape(field_cells.shape[0], field_cells.shape[1], -1, in_width)
    extent_x, extent_y, extent_z = fine_grid.shape[0], fine_grid.shape[1], fine_grid.shape[2]
    padded = jnp.pad(fine_grid, ((1, 0), (1, 0), (1, 0), (0, 0)))
    patch_one = patches(padded, extent_x // 2, extent_y // 2, extent_z // 2)
    hidden_pre = jnp.dot(patch_one, conv_one, preferred_element_type=jnp.float32)
    hidden = jax.nn.silu(hidden_pre).astype(jnp.bfloat16)
    act_grid = hidden.reshape(extent_x // 2, extent_y // 2, extent_z // 2, mid_width)
    act_pad = jnp.pad(act_grid, ((1, 0), (1, 0), (1, 0), (0, 0)))
    patch_two = patches(act_pad, extent_x // 4, extent_y // 4, extent_z // 4)
    latent_rows = jnp.dot(patch_two, conv_two, preferred_element_type=jnp.float32).astype(jnp.bfloat16)
    latent = latent_rows.reshape(extent_x // 4, -1, out_width).transpose(2, 0, 1)
    grad_rows = upstream.transpose(1, 2, 0).reshape(-1, out_width)
    grad_two = lax.dot_general(patch_two, grad_rows, (((0,), (0,)), ((), ())), preferred_element_type=jnp.float32).T
    back_rows = lax.dot_general(grad_rows, conv_two, (((1,), (1,)), ((), ())), preferred_element_type=jnp.float32)
    grad_pad = spread_taps(back_rows, extent_x // 4, extent_y // 4, extent_z // 4)
    grad_act = grad_pad[1:, 1:, 1:].reshape(-1, mid_width)
    grad_pre = (grad_act * silu_slope(hidden_pre)).astype(jnp.bfloat16)
    grad_one = lax.dot_general(patch_one, grad_pre, (((0,), (0,)), ((), ())), preferred_element_type=jnp.float32).T
    return latent, grad_one, grad_two


def reference(snapshot, conv_one, conv_two, cotangent):
    def per_sample(sample_pair):
        return sample_pass(sample_pair[0], sample_pair[1], conv_one, conv_two)

    latent, grads_one, grads_two = lax.map(per_sample, (snapshot, cotangent))
    return latent, jnp.sum(grads_one, axis=0), jnp.sum(grads_two, axis=0)
```

```python
import functools

import jax
import jax.numpy as jnp
from jax import lax
from jax.experimental import pallas as pl
from jax.experimental.pallas import tpu as pltpu
from jax.sharding import PartitionSpec as P

F32 = jnp.float32
BF16 = jnp.bfloat16
VMEM_LIMIT = 40 * 1024 * 1024

NJ, NK, CELLS = 16, 8, 128
TAP_PHASE = {0: (1, 1), 1: (0, 0), 2: (1, 0)}


def dot(a, b):
    return jnp.dot(a, b, preferred_element_type=F32)


def iota(shape, axis):
    return lax.broadcasted_iota(jnp.int32, shape, axis)


def one_hot(mask):
    return jnp.where(mask, 1.0, 0.0).astype(BF16)


def cell_order(shifted):
    width = CELLS * (4 if shifted else 1)
    row, col = iota((CELLS, width), 0), iota((CELLS, width), 1)
    v, cell = col // CELLS, col % CELLS
    to_j, to_k = cell % NJ + v // 2, cell // NJ + v % 2
    return one_hot((to_k < NK) & (row == to_j * NK + to_k))


def kernel_a(snap, halo, w1, h0, h1, slope_t, p1, w_ext):
    row, col = iota((80, 64), 0), iota((80, 64), 1)
    pick = one_hot(col == 4 * (row % NJ) + row // NJ - 1)
    for plane in range(5):
        rows = halo[0] if plane == 0 else snap[plane - 1]
        picked = dot(pick, rows).astype(BF16)
        for i in range(2):
            a = plane - 2 * i
            if not 0 <= a <= 2:
                continue
            for p in range(2):
                for b in range(3):
                    rho = 2 * p + b
                    for k in range(NK):
                        at = (2 * i + p) * CELLS + k * NJ
                        p1[at : at + NJ, (3 * a + b) * 128 : (3 * a + b + 1) * 128] = picked[
                            rho * NJ : (rho + 1) * NJ, k * 128 : (k + 1) * 128
                        ]
    for t in range(9):
        base, src = t * 128, t * 96
        zeros = jnp.zeros((128, 128), BF16)
        w_ext[base : base + 64, 0:128] = w1[src + 32 : src + 96, :]
        w_ext[base + 64 : base + 128, 0:128] = zeros[:64]
        w_ext[base : base + 32, 128:256] = zeros[:32]
        w_ext[base + 32 : base + 128, 128:256] = w1[src : src + 96, :]
        w_ext[base : base + 96, 256:384] = zeros[:96]
        w_ext[base + 96 : base + 128, 256:384] = w1[src : src + 32, :]
    for i in range(2):
        hidden = h0 if i == 0 else h1
        for p in range(2):
            at = (2 * i + p) * CELLS
            full = dot(p1[at : at + CELLS, :], w_ext[...])
            before = jnp.concatenate(
                [jnp.zeros((NJ, 128), F32), full[: CELLS - NJ, 256:384]], axis=0
            )
            for q, pre in enumerate((full[:, 0:128] + before, full[:, 128:256])):
                logistic = 1.0 / (1.0 + jnp.exp(-pre))
                hidden[2 * p + q] = (pre * logistic).astype(BF16)
                slope = logistic * (1.0 + pre * (1.0 - logistic))
                slope_t[4 * i + 2 * p + q] = slope.T


def kernel_b(pieces, rows_per, place, cot, w2, slope_t, p1, *rest):
    outs, (grad_t,) = rest[:-1], rest[-1:]
    sources = cot.shape[0]
    moved = dot(cot[...].reshape(-1, CELLS), cell_order(True))
    moved = moved.reshape(sources * pieces, 2, rows_per, 4 * CELLS)
    planes = [moved[:, s].reshape(-1, 4 * CELLS).astype(BF16) for s in range(2)]
    for i in range(2):
        for p in range(2):
            for q in range(2):
                total = None
                for a in (1,) if i == 0 else (2, 0):
                    source = planes[1 if a == 0 else 0]
                    for b in (1,) if p == 0 else (2, 0):
                        for c in (1,) if q == 0 else (2, 0):
                            v = 2 * (b == 0) + (c == 0)
                            tap = 9 * a + 3 * b + c
                            term = dot(
                                w2[tap * 128 : (tap + 1) * 128, :],
                                source[:, v * CELLS : (v + 1) * CELLS],
                            )
                            total = term if total is None else total + term
                pre_t = total * slope_t[4 * i + 2 * p + q]
                at = (2 * i + p) * CELLS
                grad_t[q * 128 : (q + 1) * 128, at : at + CELLS] = pre_t.astype(BF16)
                if q == 0:
                    ahead = pltpu.roll(pre_t, CELLS - NJ, axis=1)
                    ahead = jnp.where(iota((128, CELLS), 1) < CELLS - NJ, ahead, 0.0)
                    grad_t[256:384, at : at + CELLS] = ahead.astype(BF16)
    lane = iota((128, 128), 1)
    frames = []
    for t in range(9):
        full = dot(grad_t[...], p1[:, t * 128 : (t + 1) * 128])
        side = jnp.where(lane < 64, full[0:128], full[256:384])
        side = jnp.where((lane < 64) | (lane >= 96), side, 0.0)
        own = jnp.where(lane < 32, 0.0, full[128:256])
        frames.append(own + pltpu.roll(side, 64, axis=1))
    if pieces == 1:
        for t in range(9):
            outs[0][:, t * 128 : (t + 1) * 128] = frames[t]
        return
    owned = 128 // sources
    share = owned // pieces
    frames = [frame.astype(BF16) for frame in frames]
    for k in range(pieces):
        q = place[0] ^ k
        height = sources * 2 * share
        row, col = iota((height, 128), 0), iota((height, 128), 1)
        chosen = one_hot(col == row // (2 * share) * owned + q * share + row % share)
        for t in range(5):
            low = dot(chosen, frames[t])
            high = dot(chosen, frames[t + 5]) if t < 4 else jnp.zeros_like(low)
            half = iota(low.shape, 0) % (2 * share) // share
            outs[k][:, t * 128 : (t + 1) * 128] = jnp.where(half == 0, low, high).astype(BF16)


def kernel_latent(h0, h1, below, w2, out):
    totals = {}
    for b in range(3):
        p, sj = TAP_PHASE[b]
        for c in range(3):
            q, sk = TAP_PHASE[c]
            for a, plane in enumerate((below, h0, h1)):
                tap = 9 * a + 3 * b + c
                term = dot(plane[2 * p + q], w2[tap * 128 : (tap + 1) * 128, :])
                v = 2 * sj + sk
                totals[v] = totals[v] + term if v in totals else term
    width = totals[0].shape[1]
    zero = jnp.zeros((NJ, width), F32)

    def later(value):
        return jnp.concatenate([zero, value[: CELLS - NJ]], axis=0)

    inner = totals[2] + later(totals[3])
    inner = jnp.where(iota(inner.shape, 0) % NJ == 0, 0.0, pltpu.roll(inner, 1, axis=0))
    rows = totals[0] + later(totals[1]) + inner
    row, col = iota((CELLS, CELLS), 0), iota((CELLS, CELLS), 1)
    back = one_hot((row // NJ == col % NK) & (row % NJ == col // NK))
    out[...] = dot(rows.T.astype(BF16), back).astype(BF16)


def kernel_two(samples, rows_per, *refs):
    cots, refs = refs[:samples], refs[samples:]
    hidden_0, refs = refs[:samples], refs[samples:]
    hidden_1, refs = refs[:samples], refs[samples:]
    packed = len(refs) > 1
    out = refs[-1]
    order = cell_order(True)
    moved = []
    for cot in cots:
        value = dot(cot[...].reshape(-1, CELLS), order)
        value = value.reshape(-1, 2, rows_per, 4 * CELLS)
        moved.append([value[:, s].reshape(-1, 4 * CELLS).astype(BF16) for s in range(2)])
    left = {}
    for s in range(2):
        for v in range(4):
            left[s, v] = jnp.concatenate(
                [m[s][:, v * CELLS : (v + 1) * CELLS] for m in moved], axis=1
            )
    height = left[0, 0].shape[0]
    for p in range(2):
        for q in range(2):
            phase = 2 * p + q
            right_0 = jnp.concatenate([h[phase] for h in hidden_0], axis=0)
            right_1 = jnp.concatenate([h[phase] for h in hidden_1], axis=0)
            both = jnp.concatenate([right_0, right_1], axis=1)
            taps = [
                (b, c)
                for b in range(3)
                for c in range(3)
                if TAP_PHASE[b][0] == p and TAP_PHASE[c][0] == q
            ]
            shifts = [2 * TAP_PHASE[b][1] + TAP_PHASE[c][1] for b, c in taps]
            same = dot(jnp.concatenate([left[0, v] for v in shifts], axis=0), both)
            above = dot(jnp.concatenate([left[1, v] for v in shifts], axis=0), right_1)
            for n, (b, c) in enumerate(taps):
                rows = slice(n * height, (n + 1) * height)
                for a, value in (
                    (0, above[rows]),
                    (1, same[rows, 0:128]),
                    (2, same[rows, 128:256]),
                ):
                    at = (9 * a + 3 * b + c) * 128
                    if packed:
                        value = value.reshape(-1, rows_per, 128)
                        out[:, :, at : at + 128] = value.astype(out.dtype)
                    else:
                        out[:, at : at + 128] = value
    if packed:
        *parts, latent, _ = refs
        total = parts[0][...].astype(F32)
        for part in parts[1:]:
            total = total + part[...].astype(F32)
        wide = 27 * 128
        out[:, :, wide : wide + 640] = total.reshape(-1, rows_per, 640).astype(BF16)
        cells = latent[...].astype(F32).reshape(out.shape[0], -1, rows_per, CELLS)
        for w in range(cells.shape[1]):
            at = wide + 640 + w * 128
            out[:, :, at : at + 128] = cells[:, w].astype(BF16)


def kernel_sum(got, total_out, latent):
    sources, rows_per, _ = got.shape
    wide = 27 * 128 + 640
    for at in range(0, wide, 512):
        total = got[0, :, at : at + 512].astype(F32)
        for src in range(1, sources):
            total = total + got[src, :, at : at + 512].astype(F32)
        total_out[:, at : at + 512] = total.astype(BF16)
    height = sources * rows_per
    row, col = iota((height, height), 0), iota((height, height), 1)
    swap = one_hot((row // sources == col % rows_per) & (row % sources == col // rows_per))
    for w in range(latent.shape[0] // rows_per):
        at = wide + w * 128
        cells = got[:, :, at : at + 128].astype(F32).reshape(height, 128).astype(BF16)
        moved = dot(swap, cells).reshape(rows_per, sources, 128).astype(BF16)
        latent[w * rows_per : (w + 1) * rows_per] = moved


def kernel_final(pieces, place, *refs):
    parts, (one, two, joined) = refs[:pieces], refs[pieces:]
    rows_per = parts[0].shape[0]
    wide = 27 * 128
    share = rows_per // 2
    for k in range(pieces):
        q = place[0] ^ k
        at = pl.multiple_of(q * rows_per, rows_per)
        two[pl.ds(at, rows_per), :] = parts[k][:, :wide].astype(F32)
        joined[pl.ds(at, rows_per), :] = parts[k][:, wide : wide + 640].astype(F32)
    owned = pieces * share
    row, col = iota((owned, 2 * owned), 0), iota((owned, 2 * owned), 1)
    for half in range(2):
        chosen = one_hot(col == row // share * rows_per + half * share + row % share)
        value = dot(chosen, joined[...].astype(BF16))
        for t in range(5 - half):
            at = (5 * half + t) * 96
            one[:, at : at + 96] = value[:, t * 128 + 32 : (t + 1) * 128]


def call(kernel, out_shape, *args, scalars=0, scratch=(), flops=0):
    vmem = pl.BlockSpec(memory_space=pltpu.VMEM)
    smem = pl.BlockSpec(memory_space=pltpu.SMEM)
    single = isinstance(out_shape, jax.ShapeDtypeStruct)
    moved = sum(x.size * x.dtype.itemsize for x in args)
    return pl.pallas_call(
        kernel,
        out_shape=out_shape,
        in_specs=[smem] * scalars + [vmem] * (len(args) - scalars),
        out_specs=vmem if single else [vmem] * len(out_shape),
        scratch_shapes=list(scratch),
        cost_estimate=pl.CostEstimate(flops=flops, bytes_accessed=moved, transcendentals=0),
        compiler_params=pltpu.CompilerParams(vmem_limit_bytes=VMEM_LIMIT),
    )(*args)


def shape(dims, dtype):
    return jax.ShapeDtypeStruct(dims, dtype)


def swap_ranks(block, axis, k):
    return lax.ppermute(block, axis, [(i, i ^ k) for i in range(lax.axis_size(axis))])


def from_below(block, axis):
    return lax.ppermute(block, axis, [(i - 1, i) for i in range(1, lax.axis_size(axis))])


def on_device(snapshot, conv_one, conv_two, cotangent):
    slabs, samples = lax.axis_size("space"), lax.axis_size("dp")
    group = cotangent.shape[1]
    shared = samples == 4 and slabs == 8
    pieces = samples if shared else 1
    rows_per = group // pieces
    place = lax.axis_index("dp").astype(jnp.int32).reshape(1)

    slab = snapshot[0]
    halo = from_below(slab[3:], "space")
    by_plane = cotangent[0].transpose(1, 0, 2).reshape(slabs, pieces, 1, rows_per, CELLS)
    next_plane = jnp.pad(by_plane[1:], ((0, 1), (0, 0), (0, 0), (0, 0), (0, 0)))
    parcels = jnp.concatenate([by_plane, next_plane], axis=2).reshape(slabs, 2 * group, CELLS)
    cot = lax.all_to_all(parcels, "space", split_axis=0, concat_axis=0, tiled=True)

    h0, h1, slope_t, p1 = call(
        kernel_a,
        (
            shape((4, CELLS, 128), BF16),
            shape((4, CELLS, 128), BF16),
            shape((8, 128, CELLS), F32),
            shape((4 * CELLS, 9 * 128), BF16),
        ),
        slab,
        halo,
        conv_one,
        scratch=[pltpu.VMEM((9 * 128, 384), BF16)],
        flops=10**9,
    )
    below = from_below(h1, "space")

    if shared:
        one_shape = [shape((slabs * rows_per, 640), BF16)] * pieces
    else:
        one_shape = [shape((128, 9 * 128), F32)]
    ones = call(
        functools.partial(kernel_b, pieces, rows_per),
        one_shape,
        place,
        cot,
        conv_two,
        slope_t,
        p1,
        scalars=1,
        scratch=[pltpu.VMEM((384, 4 * CELLS), BF16)],
        flops=10**9,
    )
    latent_t = call(
        kernel_latent, shape((256, CELLS), BF16), h0, h1, below, conv_two, flops=10**9
    )

    if not shared:
        spread = latent_t.reshape(slabs, group, CELLS)
        latent = lax.all_to_all(spread, "space", split_axis=0, concat_axis=0, tiled=True)
        two = call(
            functools.partial(kernel_two, 1, rows_per),
            shape((256, 27 * 128), F32),
            cot,
            h0,
            h1,
            flops=10**9,
        )
        one = ones[0].reshape(128, 9, 128)[:, :, 32:].reshape(128, 864)
        one, two = lax.psum((one, two), "dp")
        one = lax.psum_scatter(one, "space", scatter_dimension=0, tiled=True)
        two = lax.psum_scatter(two, "space", scatter_dimension=0, tiled=True)
        return latent.transpose(1, 0, 2)[None], one, two

    def exchange(block):
        across = swap_ranks(block, "dp", 2)
        beside = swap_ranks(block, "dp", 1)
        return [block, beside, across, swap_ranks(across, "dp", 1)]

    all_h1 = exchange(h1)
    all_h0 = exchange(h0)
    cots, part_ones = [], []
    for k in range(pieces):
        piece = lax.dynamic_slice_in_dim(cot, (place[0] ^ k) * 2 * rows_per, 2 * rows_per, 1)
        cots.append(swap_ranks(piece, "dp", k) if k else piece)
        part_ones.append(swap_ranks(ones[k], "dp", k) if k else ones[k])
    width = 27 * 128 + 640 + group // rows_per * CELLS
    parcel = call(
        functools.partial(kernel_two, samples, rows_per),
        shape((slabs, rows_per, width), BF16),
        *cots,
        *all_h0,
        *all_h1,
        *part_ones,
        latent_t,
        flops=10**9,
    )
    got = lax.all_to_all(parcel, "space", split_axis=0, concat_axis=0, tiled=True)
    total, latent = call(
        kernel_sum,
        (shape((rows_per, 27 * 128 + 640), BF16), shape((group, slabs, CELLS), BF16)),
        got,
        flops=10**6,
    )
    totals = [swap_ranks(total, "dp", k) if k else total for k in range(pieces)]
    one, two = call(
        functools.partial(kernel_final, pieces),
        (shape((16, 864), F32), shape((32, 27 * 128), F32)),
        place,
        *totals,
        scalars=1,
        scratch=[pltpu.VMEM((4 * rows_per, 640), F32)],
        flops=10**6,
    )
    return latent[None], one, two


def solution(mesh):
    placed = (P("dp", "space", None, None), P(), P(), P("dp", "space", None, None))
    return jax.shard_map(
        on_device,
        mesh=mesh,
        in_specs=placed,
        out_specs=(P("dp", "space", None, None), P("space", None), P("space", None)),
        check_vma=False,
    )
```

```python
import functools

import jax
import jax.numpy as jnp
from jax import lax
from jax.experimental import pallas as pl
from jax.experimental.pallas import tpu as pltpu
from jax.sharding import PartitionSpec as P

F32 = jnp.float32
BF16 = jnp.bfloat16
VMEM_LIMIT = 40 * 1024 * 1024

NJ, NK, CELLS = 16, 8, 128
TAP_PHASE = {0: (1, 1), 1: (0, 0), 2: (1, 0)}


def dot(a, b):
    return jnp.dot(a, b, preferred_element_type=F32)


def iota(shape, axis):
    return lax.broadcasted_iota(jnp.int32, shape, axis)


def one_hot(mask):
    return jnp.where(mask, 1.0, 0.0).astype(BF16)


def cell_order(shifted):
    width = CELLS * (4 if shifted else 1)
    row, col = iota((CELLS, width), 0), iota((CELLS, width), 1)
    v, cell = col // CELLS, col % CELLS
    to_j, to_k = cell % NJ + v // 2, cell // NJ + v % 2
    return one_hot((to_k < NK) & (row == to_j * NK + to_k))


def fill_patches(planes, p1):
    row, col = iota((80, 64), 0), iota((80, 64), 1)
    pick = one_hot(col == 4 * (row % NJ) + row // NJ - 1)
    for a, rows in enumerate(planes):
        picked = dot(pick, rows).astype(BF16)
        for p in range(2):
            for b in range(3):
                rho = 2 * p + b
                for k in range(NK):
                    at = p * CELLS + k * NJ
                    p1[at : at + NJ, (3 * a + b) * 128 : (3 * a + b + 1) * 128] = picked[
                        rho * NJ : (rho + 1) * NJ, k * 128 : (k + 1) * 128
                    ]


def widen(w1, w_ext):
    for t in range(9):
        base, src = t * 128, t * 96
        zeros = jnp.zeros((128, 128), BF16)
        w_ext[base : base + 64, 0:128] = w1[src + 32 : src + 96, :]
        w_ext[base + 64 : base + 128, 0:128] = zeros[:64]
        w_ext[base : base + 32, 128:256] = zeros[:32]
        w_ext[base + 32 : base + 128, 128:256] = w1[src : src + 96, :]
        w_ext[base : base + 96, 256:384] = zeros[:96]
        w_ext[base + 96 : base + 128, 256:384] = w1[src : src + 32, :]


def fill_hidden(p1, w_ext, hidden, slope_t):
    for p in range(2):
        full = dot(p1[p * CELLS : (p + 1) * CELLS, :], w_ext[...])
        before = jnp.concatenate(
            [jnp.zeros((NJ, 128), F32), full[: CELLS - NJ, 256:384]], axis=0
        )
        for q, pre in enumerate((full[:, 0:128] + before, full[:, 128:256])):
            logistic = 1.0 / (1.0 + jnp.exp(-pre))
            hidden[2 * p + q] = (pre * logistic).astype(BF16)
            slope = logistic * (1.0 + pre * (1.0 - logistic))
            slope_t[2 * p + q] = slope.T


def kernel_upper(pieces, cot, snap, w1, parcels, halo, hidden, slope_t, p1, w_ext):
    group, slabs = cot.shape[:2]
    rows_per = group // pieces
    halo[0] = snap[3]
    flat = cot[...].astype(F32).reshape(-1, CELLS).astype(BF16)
    row, col = iota((2 * group * slabs, group * slabs), 0), iota((2 * group * slabs, group * slabs), 1)
    slab = row // (2 * group) + row // rows_per % 2
    channel = row % (2 * group) // (2 * rows_per) * rows_per + row % rows_per
    chosen = one_hot((slab < slabs) & (col == channel * slabs + slab))
    parcels[...] = dot(chosen, flat).astype(BF16).reshape(slabs, 2 * group, CELLS)
    fill_patches([snap[1], snap[2], snap[3]], p1)
    widen(w1, w_ext)
    fill_hidden(p1, w_ext, hidden, slope_t)


def kernel_lower(snap, halo, w1, hidden, slope_t, p1, w_ext):
    fill_patches([halo[0], snap[0], snap[1]], p1)
    widen(w1, w_ext)
    fill_hidden(p1, w_ext, hidden, slope_t)


def kernel_b(pieces, rows_per, place, cot, w2, slope_0, slope_1, p1_0, p1_1, *rest):
    outs, (grad_t,) = rest[:-1], rest[-1:]
    sources = cot.shape[0]
    moved = dot(cot[...].reshape(-1, CELLS), cell_order(True))
    moved = moved.reshape(sources * pieces, 2, rows_per, 4 * CELLS)
    planes = [moved[:, s].reshape(-1, 4 * CELLS).astype(BF16) for s in range(2)]
    for i in range(2):
        for p in range(2):
            for q in range(2):
                total = None
                for a in (1,) if i == 0 else (2, 0):
                    source = planes[1 if a == 0 else 0]
                    for b in (1,) if p == 0 else (2, 0):
                        for c in (1,) if q == 0 else (2, 0):
                            v = 2 * (b == 0) + (c == 0)
                            tap = 9 * a + 3 * b + c
                            term = dot(
                                w2[tap * 128 : (tap + 1) * 128, :],
                                source[:, v * CELLS : (v + 1) * CELLS],
                            )
                            total = term if total is None else total + term
                pre_t = total * (slope_0, slope_1)[i][2 * p + q]
                at = (2 * i + p) * CELLS
                grad_t[q * 128 : (q + 1) * 128, at : at + CELLS] = pre_t.astype(BF16)
                if q == 0:
                    ahead = pltpu.roll(pre_t, CELLS - NJ, axis=1)
                    ahead = jnp.where(iota((128, CELLS), 1) < CELLS - NJ, ahead, 0.0)
                    grad_t[256:384, at : at + CELLS] = ahead.astype(BF16)
    lane = iota((128, 128), 1)
    frames = []
    for t in range(9):
        cols = slice(t * 128, (t + 1) * 128)
        full = dot(grad_t[:, : 2 * CELLS], p1_0[:, cols])
        full = full + dot(grad_t[:, 2 * CELLS :], p1_1[:, cols])
        side = jnp.where(lane < 64, full[0:128], full[256:384])
        side = jnp.where((lane < 64) | (lane >= 96), side, 0.0)
        own = jnp.where(lane < 32, 0.0, full[128:256])
        frames.append(own + pltpu.roll(side, 64, axis=1))
    if pieces == 1:
        for t in range(9):
            outs[0][:, t * 128 : (t + 1) * 128] = frames[t]
        return
    owned = 128 // sources
    share = owned // pieces
    frames = [frame.astype(BF16) for frame in frames]
    for k in range(pieces):
        q = place[0] ^ k
        height = sources * 2 * share
        row, col = iota((height, 128), 0), iota((height, 128), 1)
        chosen = one_hot(col == row // (2 * share) * owned + q * share + row % share)
        for t in range(5):
            low = dot(chosen, frames[t])
            high = dot(chosen, frames[t + 5]) if t < 4 else jnp.zeros_like(low)
            half = iota(low.shape, 0) % (2 * share) // share
            outs[k][:, t * 128 : (t + 1) * 128] = jnp.where(half == 0, low, high).astype(BF16)


def kernel_latent(h0, h1, below, w2, out):
    totals = {}
    for b in range(3):
        p, sj = TAP_PHASE[b]
        for c in range(3):
            q, sk = TAP_PHASE[c]
            for a, plane in enumerate((below, h0, h1)):
                tap = 9 * a + 3 * b + c
                term = dot(plane[2 * p + q], w2[tap * 128 : (tap + 1) * 128, :])
                v = 2 * sj + sk
                totals[v] = totals[v] + term if v in totals else term
    width = totals[0].shape[1]
    zero = jnp.zeros((NJ, width), F32)

    def later(value):
        return jnp.concatenate([zero, value[: CELLS - NJ]], axis=0)

    inner = totals[2] + later(totals[3])
    inner = jnp.where(iota(inner.shape, 0) % NJ == 0, 0.0, pltpu.roll(inner, 1, axis=0))
    rows = totals[0] + later(totals[1]) + inner
    row, col = iota((CELLS, CELLS), 0), iota((CELLS, CELLS), 1)
    back = one_hot((row // NJ == col % NK) & (row % NJ == col // NK))
    out[...] = dot(rows.T.astype(BF16), back).astype(BF16)


def moved_rows(cots, rows_per, plane):
    order = cell_order(True)
    moved = []
    for cot in cots:
        value = dot(cot[...].reshape(-1, CELLS), order)
        value = value.reshape(-1, 2, rows_per, 4 * CELLS)
        moved.append(value[:, plane].reshape(-1, 4 * CELLS).astype(BF16))
    return [
        jnp.concatenate([m[:, v * CELLS : (v + 1) * CELLS] for m in moved], axis=1)
        for v in range(4)
    ]


def kernel_two(samples, rows_per, upper, packed, *refs):
    cots, hidden, refs = refs[:samples], refs[samples : 2 * samples], refs[2 * samples :]
    out = refs[-1]
    taps_x = (0, 2) if upper else (1,)
    left = {a: moved_rows(cots, rows_per, 1 if a == 0 else 0) for a in taps_x}
    height = left[taps_x[0]][0].shape[0]
    for p in range(2):
        for q in range(2):
            right = jnp.concatenate([h[2 * p + q] for h in hidden], axis=0)
            taps = [
                (n, b, c)
                for n in range(len(taps_x))
                for b in range(3)
                for c in range(3)
                if TAP_PHASE[b][0] == p and TAP_PHASE[c][0] == q
            ]
            rows = [left[taps_x[n]][2 * TAP_PHASE[b][1] + TAP_PHASE[c][1]] for n, b, c in taps]
            value = dot(jnp.concatenate(rows, axis=0), right)
            for at, (n, b, c) in enumerate(taps):
                part = value[at * height : (at + 1) * height]
                to = (9 * n + 3 * b + c) * 128
                if packed:
                    out[:, :, to : to + 128] = part.reshape(-1, rows_per, 128).astype(BF16)
                else:
                    out[:, to : to + 128] = part
    if packed and not upper:
        *parts, latent, _ = refs
        total = parts[0][...].astype(F32)
        for part in parts[1:]:
            total = total + part[...].astype(F32)
        out[:, :, 1152:1792] = total.reshape(-1, rows_per, 640).astype(BF16)
        cells = latent[...].astype(F32).reshape(out.shape[0], -1, rows_per, CELLS)
        for w in range(cells.shape[1]):
            at = 1792 + w * 128
            out[:, :, at : at + 128] = cells[:, w].astype(BF16)


def add_sources(got, total_out):
    sources, width = got.shape[0], total_out.shape[1]
    for at in range(0, width, 256):
        total = got[0, :, at : at + 256].astype(F32)
        for src in range(1, sources):
            total = total + got[src, :, at : at + 256].astype(F32)
        total_out[:, at : at + 256] = total.astype(BF16)


def kernel_sum_upper(got, total_out):
    add_sources(got, total_out)


def kernel_sum_lower(got, total_out, latent):
    sources, rows_per, _ = got.shape
    add_sources(got, total_out)
    height = sources * rows_per
    row, col = iota((height, height), 0), iota((height, height), 1)
    swap = one_hot((row // sources == col % rows_per) & (row % sources == col // rows_per))
    for w in range(latent.shape[0] // rows_per):
        at = 1792 + w * 128
        cells = got[:, :, at : at + 128].astype(F32).reshape(height, 128).astype(BF16)
        moved = dot(swap, cells).reshape(rows_per, sources, 128).astype(BF16)
        latent[w * rows_per : (w + 1) * rows_per] = moved


def kernel_final(pieces, place, *refs):
    uppers, lowers, (one, two, joined) = (
        refs[:pieces],
        refs[pieces : 2 * pieces],
        refs[2 * pieces :],
    )
    rows_per = uppers[0].shape[0]
    share = rows_per // 2
    for k in range(pieces):
        q = place[0] ^ k
        at = pl.multiple_of(q * rows_per, rows_per)
        two[pl.ds(at, rows_per), 0:1152] = uppers[k][:, 0:1152].astype(F32)
        two[pl.ds(at, rows_per), 1152:2304] = lowers[k][:, 0:1152].astype(F32)
        two[pl.ds(at, rows_per), 2304:3456] = uppers[k][:, 1152:2304].astype(F32)
        joined[pl.ds(at, rows_per), :] = lowers[k][:, 1152:1792].astype(F32)
    owned = pieces * share
    row, col = iota((owned, 2 * owned), 0), iota((owned, 2 * owned), 1)
    for half in range(2):
        chosen = one_hot(col == row // share * rows_per + half * share + row % share)
        value = dot(chosen, joined[...].astype(BF16))
        for t in range(5 - half):
            at = (5 * half + t) * 96
            one[:, at : at + 96] = value[:, t * 128 + 32 : (t + 1) * 128]


def call(kernel, out_shape, *args, scalars=0, scratch=(), flops=0):
    vmem = pl.BlockSpec(memory_space=pltpu.VMEM)
    smem = pl.BlockSpec(memory_space=pltpu.SMEM)
    single = isinstance(out_shape, jax.ShapeDtypeStruct)
    moved = sum(x.size * x.dtype.itemsize for x in args)
    return pl.pallas_call(
        kernel,
        out_shape=out_shape,
        in_specs=[smem] * scalars + [vmem] * (len(args) - scalars),
        out_specs=vmem if single else [vmem] * len(out_shape),
        scratch_shapes=list(scratch),
        cost_estimate=pl.CostEstimate(flops=flops, bytes_accessed=moved, transcendentals=0),
        compiler_params=pltpu.CompilerParams(vmem_limit_bytes=VMEM_LIMIT),
    )(*args)


def shape(dims, dtype):
    return jax.ShapeDtypeStruct(dims, dtype)


def swap_ranks(block, axis, k):
    return lax.ppermute(block, axis, [(i, i ^ k) for i in range(lax.axis_size(axis))])


def from_below(block, axis):
    return lax.ppermute(block, axis, [(i - 1, i) for i in range(1, lax.axis_size(axis))])


def on_device(snapshot, conv_one, conv_two, cotangent):
    slabs, samples = lax.axis_size("space"), lax.axis_size("dp")
    group = cotangent.shape[1]
    shared = samples == 4 and slabs == 8
    pieces = samples if shared else 1
    rows_per = group // pieces
    place = lax.axis_index("dp").astype(jnp.int32).reshape(1)

    slab = snapshot[0]
    plane_shapes = (
        shape((4, CELLS, 128), BF16),
        shape((4, 128, CELLS), F32),
        shape((2 * CELLS, 9 * 128), BF16),
    )
    wide = [pltpu.VMEM((9 * 128, 384), BF16)]
    parcels, last, h1, slope_1, p1_1 = call(
        functools.partial(kernel_upper, pieces),
        (shape((slabs, 2 * group, CELLS), BF16), shape((1,) + slab.shape[1:], BF16)) + plane_shapes,
        cotangent[0],
        slab,
        conv_one,
        scratch=wide,
        flops=10**9,
    )
    halo = from_below(last, "space")
    cot = lax.all_to_all(parcels, "space", split_axis=0, concat_axis=0, tiled=True)
    below = from_below(h1, "space")
    h0, slope_0, p1_0 = call(
        kernel_lower, plane_shapes, slab, halo, conv_one, scratch=wide, flops=10**9
    )

    if shared:
        one_shape = [shape((slabs * rows_per, 640), BF16)] * pieces
    else:
        one_shape = [shape((128, 9 * 128), F32)]
    ones = call(
        functools.partial(kernel_b, pieces, rows_per),
        one_shape,
        place,
        cot,
        conv_two,
        slope_0,
        slope_1,
        p1_0,
        p1_1,
        scalars=1,
        scratch=[pltpu.VMEM((384, 4 * CELLS), BF16)],
        flops=10**9,
    )
    latent_t = call(
        kernel_latent, shape((256, CELLS), BF16), h0, h1, below, conv_two, flops=10**9
    )

    if not shared:
        spread = latent_t.reshape(slabs, group, CELLS)
        latent = lax.all_to_all(spread, "space", split_axis=0, concat_axis=0, tiled=True)
        halves = [
            call(
                functools.partial(kernel_two, 1, rows_per, upper, False),
                shape((256, (18 if upper else 9) * 128), F32),
                cot,
                hidden,
                flops=10**9,
            )
            for upper, hidden in ((True, h1), (False, h0))
        ]
        two = jnp.concatenate([halves[0][:, :1152], halves[1], halves[0][:, 1152:]], axis=1)
        one = ones[0].reshape(128, 9, 128)[:, :, 32:].reshape(128, 864)
        one, two = lax.psum((one, two), "dp")
        one = lax.psum_scatter(one, "space", scatter_dimension=0, tiled=True)
        two = lax.psum_scatter(two, "space", scatter_dimension=0, tiled=True)
        return latent.transpose(1, 0, 2)[None], one, two

    def exchange(block):
        across = swap_ranks(block, "dp", 2)
        beside = swap_ranks(block, "dp", 1)
        return [block, beside, across, swap_ranks(across, "dp", 1)]

    all_h1 = exchange(h1)
    all_h0 = exchange(h0)
    cots, part_ones = [], []
    for k in range(pieces):
        piece = lax.dynamic_slice_in_dim(cot, (place[0] ^ k) * 2 * rows_per, 2 * rows_per, 1)
        cots.append(swap_ranks(piece, "dp", k) if k else piece)
        part_ones.append(swap_ranks(ones[k], "dp", k) if k else ones[k])
    parcel_shape = shape((slabs, rows_per, 18 * 128), BF16)
    upper = call(
        functools.partial(kernel_two, samples, rows_per, True, True),
        parcel_shape,
        *cots,
        *all_h1,
        flops=10**9,
    )
    got_upper = lax.all_to_all(upper, "space", split_axis=0, concat_axis=0, tiled=True)
    lower = call(
        functools.partial(kernel_two, samples, rows_per, False, True),
        parcel_shape,
        *cots,
        *all_h0,
        *part_ones,
        latent_t,
        flops=10**9,
    )
    got_lower = lax.all_to_all(lower, "space", split_axis=0, concat_axis=0, tiled=True)
    total_upper = call(
        kernel_sum_upper, shape((rows_per, 18 * 128), BF16), got_upper, flops=10**6
    )
    total_lower, latent = call(
        kernel_sum_lower,
        (shape((rows_per, 14 * 128), BF16), shape((group, slabs, CELLS), BF16)),
        got_lower,
        flops=10**6,
    )
    totals = [
        swap_ranks(total, "dp", k) if k else total
        for total in (total_upper, total_lower)
        for k in range(pieces)
    ]
    one, two = call(
        functools.partial(kernel_final, pieces),
        (shape((16, 864), F32), shape((32, 27 * 128), F32)),
        place,
        *totals,
        scalars=1,
        scratch=[pltpu.VMEM((4 * rows_per, 640), F32)],
        flops=10**6,
    )
    return latent[None], one, two


def solution(mesh):
    placed = (P("dp", "space", None, None), P(), P(), P("dp", "space", None, None))
    return jax.shard_map(
        on_device,
        mesh=mesh,
        in_specs=placed,
        out_specs=(P("dp", "space", None, None), P("space", None), P("space", None)),
        check_vma=False,
    )
```

```python
import functools

import jax
import jax.numpy as jnp
from jax import lax
from jax.experimental import pallas as pl
from jax.experimental.pallas import tpu as pltpu
from jax.sharding import PartitionSpec as P

F32 = jnp.float32
BF16 = jnp.bfloat16
VMEM_LIMIT = 16 * 1024 * 1024

FLOPS_PACK, FLOPS_BACK = 10**9, 10**9

NJ, NK, CELLS = 16, 8, 128
ONE_AT, ONE_END, LATENT_AT, NEXT_AT, WIDTH = 3456, 4320, 4352, 4864, 5376
HIDDEN_AT, PACK = (0, 8), 16
TAP_PHASE = {0: (1, 1), 1: (0, 0), 2: (1, 0)}


def dot(a, b):
    return jnp.dot(a, b, preferred_element_type=F32)


def iota(shape, axis):
    return lax.broadcasted_iota(jnp.int32, shape, axis)


def one_hot(mask):
    return jnp.where(mask, 1.0, 0.0).astype(BF16)


def cell_order(shifted):
    width = CELLS * (4 if shifted else 1)
    row, col = iota((CELLS, width), 0), iota((CELLS, width), 1)
    v, cell = col // CELLS, col % CELLS
    to_j, to_k = cell % NJ + v // 2, cell // NJ + v % 2
    return one_hot((to_k < NK) & (row == to_j * NK + to_k))


def fill_patches(planes, p1):
    row, col = iota((80, 64), 0), iota((80, 64), 1)
    pick = one_hot(col == 4 * (row % NJ) + row // NJ - 1)
    for a, rows in enumerate(planes):
        picked = dot(pick, rows).astype(BF16)
        for p in range(2):
            for b in range(3):
                rho = 2 * p + b
                for k in range(NK):
                    at = p * CELLS + k * NJ
                    p1[at : at + NJ, (3 * a + b) * 128 : (3 * a + b + 1) * 128] = picked[
                        rho * NJ : (rho + 1) * NJ, k * 128 : (k + 1) * 128
                    ]


def widen(w1, w_ext):
    for t in range(9):
        base, src = t * 128, t * 96
        zeros = jnp.zeros((128, 128), BF16)
        w_ext[base : base + 64, 0:128] = w1[src + 32 : src + 96, :]
        w_ext[base + 64 : base + 128, 0:128] = zeros[:64]
        w_ext[base : base + 32, 128:256] = zeros[:32]
        w_ext[base + 32 : base + 128, 128:256] = w1[src : src + 96, :]
        w_ext[base : base + 96, 256:384] = zeros[:96]
        w_ext[base + 96 : base + 128, 256:384] = w1[src : src + 32, :]


def fill_hidden(p1, w_ext, hidden, slope_t):
    for p in range(2):
        full = dot(p1[p * CELLS : (p + 1) * CELLS, :], w_ext[...])
        before = jnp.concatenate(
            [jnp.zeros((NJ, 128), F32), full[: CELLS - NJ, 256:384]], axis=0
        )
        for q, pre in enumerate((full[:, 0:128] + before, full[:, 128:256])):
            logistic = 1.0 / (1.0 + jnp.exp(-pre))
            hidden[2 * p + q] = (pre * logistic).astype(BF16)
            if slope_t is not None:
                slope = logistic * (1.0 + pre * (1.0 - logistic))
                slope_t[2 * p + q] = slope.T


def kernel_parcels(pieces, cot_hbm, snap, parcels, halo, cot, sems):
    last = pltpu.make_async_copy(snap.at[pl.ds(3, 1)], halo, sems.at[0])
    whole = pltpu.make_async_copy(cot_hbm, cot, sems.at[1])
    whole.start()
    last.start()
    group, slabs = cot.shape[:2]
    rows_per = group // pieces
    row, col = iota((2 * group * slabs, group * slabs), 0), iota((2 * group * slabs, group * slabs), 1)
    slab = row // (2 * group) + row // rows_per % 2
    channel = row % (2 * group) // (2 * rows_per) * rows_per + row % rows_per
    chosen = one_hot((slab < slabs) & (col == channel * slabs + slab))
    whole.wait()
    flat = cot[...].astype(F32).reshape(-1, CELLS).astype(BF16)
    parcels[...] = dot(chosen, flat).astype(BF16).reshape(slabs, 2 * group, CELLS)
    last.wait()


class Phases:
    def __init__(self, pack, i):
        self.pack, self.at = pack, HIDDEN_AT[i]

    def __setitem__(self, phase, value):
        at = self.at + 2 * phase
        self.pack[at : at + 2] = value.reshape(2, 64, 128)

    def __getitem__(self, phase):
        at = self.at + 2 * phase
        return self.pack[at : at + 2].reshape(CELLS, 128)


def hidden_planes(snap, halo, w_ext, p1, hidden, slope_t):
    for i, planes in enumerate(([halo[0], snap[0], snap[1]], [snap[1], snap[2], snap[3]])):
        fill_patches(planes, p1.at[i])
        fill_hidden(p1.at[i], w_ext, hidden(i), None if slope_t is None else slope_t.at[i])


def kernel_pack(snap_hbm, halo, w1_hbm, pack, snap, w1, p1, w_ext, sems):
    copies = [
        pltpu.make_async_copy(w1_hbm, w1, sems.at[0]),
        pltpu.make_async_copy(snap_hbm, snap, sems.at[1]),
    ]
    for copy in copies:
        copy.start()
    copies[0].wait()
    widen(w1, w_ext)
    copies[1].wait()
    hidden_planes(snap, halo, w_ext, p1, lambda i: Phases(pack, i), None)


def kernel_back(pieces, rows_per, place, snap_hbm, halo, w1_hbm, w2_hbm, cot, *rest):
    *outs, parts, snap, w1, p1, w_ext, w2, hidden, slope_t, grad_t, sems = rest
    copies = [
        pltpu.make_async_copy(w1_hbm, w1, sems.at[0]),
        pltpu.make_async_copy(snap_hbm, snap, sems.at[1]),
        pltpu.make_async_copy(w2_hbm, w2, sems.at[2]),
    ]
    for copy in copies:
        copy.start()
    copies[0].wait()
    widen(w1, w_ext)
    copies[1].wait()
    hidden_planes(snap, halo, w_ext, p1, lambda i: hidden.at[i], slope_t)
    copies[2].wait()
    grad_one_share(pieces, rows_per, place, w2, cot, outs, p1, slope_t, grad_t)
    latent_parts(hidden, w2, parts)


def grad_one_share(pieces, rows_per, place, w2, cot, outs, p1, slope_t, grad_t):
    sources = cot.shape[0]
    moved = dot(cot[...].reshape(-1, CELLS), cell_order(True))
    moved = moved.reshape(sources * pieces, 2, rows_per, 4 * CELLS)
    planes = [moved[:, s].reshape(-1, 4 * CELLS).astype(BF16) for s in range(2)]
    for i in range(2):
        for p in range(2):
            for q in range(2):
                total = None
                for a in (1,) if i == 0 else (2, 0):
                    source = planes[1 if a == 0 else 0]
                    for b in (1,) if p == 0 else (2, 0):
                        for c in (1,) if q == 0 else (2, 0):
                            v = 2 * (b == 0) + (c == 0)
                            tap = 9 * a + 3 * b + c
                            term = dot(
                                w2[tap * 128 : (tap + 1) * 128, :],
                                source[:, v * CELLS : (v + 1) * CELLS],
                            )
                            total = term if total is None else total + term
                pre_t = total * slope_t[i, 2 * p + q]
                at = (2 * i + p) * CELLS
                grad_t[q * 128 : (q + 1) * 128, at : at + CELLS] = pre_t.astype(BF16)
                if q == 0:
                    ahead = pltpu.roll(pre_t, CELLS - NJ, axis=1)
                    ahead = jnp.where(iota((128, CELLS), 1) < CELLS - NJ, ahead, 0.0)
                    grad_t[256:384, at : at + CELLS] = ahead.astype(BF16)
    lane = iota((128, 128), 1)
    frames = []
    for t in range(9):
        cols = slice(t * 128, (t + 1) * 128)
        full = dot(grad_t[:, : 2 * CELLS], p1[0, :, cols])
        full = full + dot(grad_t[:, 2 * CELLS :], p1[1, :, cols])
        side = jnp.where(lane < 64, full[0:128], full[256:384])
        side = jnp.where((lane < 64) | (lane >= 96), side, 0.0)
        own = jnp.where(lane < 32, 0.0, full[128:256])
        frames.append(own + pltpu.roll(side, 64, axis=1))
    if pieces == 1:
        for t in range(9):
            outs[0][:, t * 96 : (t + 1) * 96] = frames[t][:, 32:]
        return
    owned = 128 // sources
    share = owned // 2
    row, col = iota((128 // 2, 128), 0), iota((128 // 2, 128), 1)
    frames = [frame.astype(BF16) for frame in frames]
    for k in range(2):
        half = (place[0] ^ k) & 1
        chosen = one_hot(col == row // share * owned + half * share + row % share)
        for t in range(9):
            value = dot(chosen, frames[t])
            outs[k][:, t * 96 : (t + 1) * 96] = value[:, 32:].astype(BF16)


def latent_parts(hidden, w2, parts):
    row, col = iota((CELLS, CELLS), 0), iota((CELLS, CELLS), 1)
    back = one_hot((row // NJ == col % NK) & (row % NJ == col // NK))
    for part, taps_x in enumerate(((1, 2), (0,))):
        totals = {}
        for b in range(3):
            p, sj = TAP_PHASE[b]
            for c in range(3):
                q, sk = TAP_PHASE[c]
                for a in taps_x:
                    tap = 9 * a + 3 * b + c
                    plane = 0 if a == 1 else 1
                    term = dot(hidden[plane, 2 * p + q], w2[tap * 128 : (tap + 1) * 128, :])
                    v = 2 * sj + sk
                    totals[v] = totals[v] + term if v in totals else term
        zero = jnp.zeros((NJ, totals[0].shape[1]), F32)

        def later(value):
            return jnp.concatenate([zero, value[: CELLS - NJ]], axis=0)

        inner = totals[2] + later(totals[3])
        inner = jnp.where(iota(inner.shape, 0) % NJ == 0, 0.0, pltpu.roll(inner, 1, axis=0))
        rows = totals[0] + later(totals[1]) + inner
        parts[part] = dot(rows.T.astype(BF16), back).astype(BF16)


def moved_rows(cots, rows_per, order):
    moved = []
    for cot in cots:
        value = dot(cot[...].reshape(-1, CELLS), order).reshape(-1, 2, rows_per, 4 * CELLS)
        moved.append([value[:, s].reshape(-1, 4 * CELLS).astype(BF16) for s in range(2)])
    return [
        [
            jnp.concatenate([m[s][:, v * CELLS : (v + 1) * CELLS] for m in moved], axis=1)
            for v in range(4)
        ]
        for s in range(2)
    ]


def kernel_two(samples, rows_per, *refs):
    packs, cots, refs = refs[:samples], refs[samples : 2 * samples], refs[2 * samples :]
    packed = samples > 1
    out = refs[-1]
    left = moved_rows(cots, rows_per, cell_order(True))
    height = left[0][0].shape[0]
    for p in range(2):
        for q in range(2):
            right_0, right_1 = [
                jnp.concatenate([Phases(pack, i)[2 * p + q] for pack in packs], axis=0)
                for i in range(2)
            ]
            both = jnp.concatenate([right_0, right_1], axis=1)
            taps = [
                (b, c)
                for b in range(3)
                for c in range(3)
                if TAP_PHASE[b][0] == p and TAP_PHASE[c][0] == q
            ]
            shifts = [2 * TAP_PHASE[b][1] + TAP_PHASE[c][1] for b, c in taps]
            same = dot(jnp.concatenate([left[0][v] for v in shifts], axis=0), both)
            above = dot(jnp.concatenate([left[1][v] for v in shifts], axis=0), right_1)
            for n, (b, c) in enumerate(taps):
                rows = slice(n * height, (n + 1) * height)
                parts = (above[rows], same[rows, 0:128], same[rows, 128:256])
                for a, value in enumerate(parts):
                    to = (9 * a + 3 * b + c) * 128
                    if packed:
                        out[:, :, to : to + 128] = value.reshape(-1, rows_per, 128).astype(BF16)
                    else:
                        out[:, to : to + 128] = value
    if packed:
        own, other, latent, _ = refs
        total = own[...].astype(F32) + other[...].astype(F32)
        out[:, :, ONE_AT:ONE_END] = total.reshape(-1, rows_per, 864).astype(BF16)
        out[:, :, ONE_END:LATENT_AT] = jnp.zeros(
            (out.shape[0], rows_per, LATENT_AT - ONE_END), BF16
        )
        for part, start in enumerate((LATENT_AT, NEXT_AT)):
            cells = latent[part].astype(F32).reshape(out.shape[0], -1, rows_per, CELLS)
            for w in range(cells.shape[1]):
                to = start + w * 128
                out[:, :, to : to + 128] = cells[:, w].astype(BF16)


def kernel_sum(got, total_out, latent):
    sources, rows_per, _ = got.shape
    for at in range(0, LATENT_AT, 256):
        total = got[0, :, at : at + 256].astype(F32)
        for src in range(1, sources):
            total = total + got[src, :, at : at + 256].astype(F32)
        total_out[:, at : at + 256] = total.astype(BF16)
    height = sources * rows_per
    row, col = iota((height, height), 0), iota((height, height), 1)
    swap = one_hot((row // sources == col % rows_per) & (row % sources == col // rows_per))
    for w in range(latent.shape[0] // rows_per):
        own, next_ = [
            got[:, :, at : at + 128].astype(F32)
            for at in (LATENT_AT + w * 128, NEXT_AT + w * 128)
        ]
        cells = own + jnp.concatenate([jnp.zeros_like(next_[:1]), next_[:-1]], axis=0)
        cells = cells.reshape(height, 128).astype(BF16)
        moved = dot(swap, cells).reshape(rows_per, sources, 128).astype(BF16)
        latent[w * rows_per : (w + 1) * rows_per] = moved


def kernel_final(pieces, place, *refs):
    parts, (one, two) = refs[:pieces], refs[pieces:]
    rows_per = parts[0].shape[0]
    for k in range(pieces):
        at = pl.multiple_of((place[0] ^ k) * rows_per, rows_per)
        two[pl.ds(at, rows_per), :] = parts[k][:, 0:ONE_AT].astype(F32)
    for k in range(2):
        at = pl.multiple_of(((place[0] ^ k) & 1) * rows_per, rows_per)
        shares = [parts[n][:, ONE_AT:ONE_END].astype(F32) for n in (k, k ^ 2)]
        one[pl.ds(at, rows_per), :] = shares[0] + shares[1]


def call(kernel, out_shape, *args, spaces=None, scratch=(), flops=10**9):
    spaces = spaces or {}
    single = isinstance(out_shape, jax.ShapeDtypeStruct)
    vmem = pl.BlockSpec(memory_space=pltpu.VMEM)
    moved = sum(x.size * x.dtype.itemsize for x in args)
    return pl.pallas_call(
        kernel,
        out_shape=out_shape,
        in_specs=[
            pl.BlockSpec(memory_space=spaces.get(n, pltpu.VMEM)) for n in range(len(args))
        ],
        out_specs=vmem if single else [vmem] * len(out_shape),
        scratch_shapes=list(scratch),
        cost_estimate=pl.CostEstimate(flops=flops, bytes_accessed=moved, transcendentals=0),
        compiler_params=pltpu.CompilerParams(vmem_limit_bytes=VMEM_LIMIT),
    )(*args)


def shape(dims, dtype):
    return jax.ShapeDtypeStruct(dims, dtype)


def swap_ranks(block, axis, k):
    return lax.ppermute(block, axis, [(i, i ^ k) for i in range(lax.axis_size(axis))])


def first_of(value, *others):
    return lax.optimization_barrier((value, *others))[0]


def from_below(block, axis):
    return lax.ppermute(block, axis, [(i - 1, i) for i in range(1, lax.axis_size(axis))])


def on_device(snapshot, conv_one, conv_two, cotangent):
    slabs, samples = lax.axis_size("space"), lax.axis_size("dp")
    group = cotangent.shape[1]
    shared = samples == 4 and slabs == 8
    pieces = samples if shared else 1
    rows_per = group // pieces
    place = lax.axis_index("dp").astype(jnp.int32).reshape(1)

    slab = snapshot[0]
    parcels, last = call(
        functools.partial(kernel_parcels, pieces),
        (shape((slabs, 2 * group, CELLS), BF16), shape((1,) + slab.shape[1:], BF16)),
        cotangent[0],
        slab,
        spaces={0: pltpu.HBM, 1: pltpu.HBM},
        scratch=[pltpu.VMEM((group, slabs, CELLS), BF16), pltpu.SemaphoreType.DMA((2,))],
    )
    halo = from_below(last, "space")
    cot = lax.all_to_all(parcels, "space", split_axis=0, concat_axis=0, tiled=True)
    forward = [
        pltpu.VMEM(slab.shape, BF16),
        pltpu.VMEM(conv_one.shape, BF16),
        pltpu.VMEM((2, 2 * CELLS, 9 * 128), BF16),
        pltpu.VMEM((9 * 128, 384), BF16),
    ]
    pack = call(
        kernel_pack,
        shape((PACK, 64, CELLS), BF16),
        slab,
        halo,
        conv_one,
        spaces={0: pltpu.HBM, 2: pltpu.HBM},
        scratch=forward + [pltpu.SemaphoreType.DMA((2,))],
        flops=FLOPS_PACK,
    )
    if shared:
        one_shape = (shape((64, 864), BF16),) * 2
    else:
        one_shape = (shape((128, 864), F32),)
    *ones, parts = call(
        functools.partial(kernel_back, pieces, rows_per),
        one_shape + (shape((2, 256, CELLS), BF16),),
        place,
        slab,
        halo,
        conv_one,
        conv_two,
        cot,
        spaces={0: pltpu.SMEM, 1: pltpu.HBM, 3: pltpu.HBM, 4: pltpu.HBM},
        scratch=forward
        + [
            pltpu.VMEM(conv_two.shape, BF16),
            pltpu.VMEM((2, 4, CELLS, 128), BF16),
            pltpu.VMEM((2, 4, 128, CELLS), F32),
            pltpu.VMEM((384, 4 * CELLS), BF16),
            pltpu.SemaphoreType.DMA((3,)),
        ],
        flops=FLOPS_BACK,
    )

    if not shared:
        spread = parts.reshape(2, slabs, group, CELLS).transpose(1, 0, 2, 3)
        spread = lax.all_to_all(spread, "space", split_axis=0, concat_axis=0, tiled=True)
        next_ = jnp.pad(spread[:-1, 1].astype(F32), ((1, 0), (0, 0), (0, 0)))
        latent = (spread[:, 0].astype(F32) + next_).astype(BF16)
        two = call(
            functools.partial(kernel_two, 1, rows_per),
            shape((256, 27 * 128), F32),
            pack,
            cot,
        )
        one, two = lax.psum((ones[0], two), "dp")
        one = lax.psum_scatter(one, "space", scatter_dimension=0, tiled=True)
        two = lax.psum_scatter(two, "space", scatter_dimension=0, tiled=True)
        return latent.transpose(1, 0, 2)[None], one, two

    across = swap_ranks(pack, "dp", 2)
    beside = swap_ranks(pack, "dp", 1)
    cots = []
    for k in range(pieces):
        piece = lax.dynamic_slice_in_dim(cot, (place[0] ^ k) * 2 * rows_per, 2 * rows_per, 1)
        cots.append(swap_ranks(piece, "dp", k) if k else piece)
    parcel = call(
        functools.partial(kernel_two, samples, rows_per),
        shape((slabs, rows_per, WIDTH), BF16),
        pack,
        beside,
        across,
        swap_ranks(first_of(across, *ones, *cots[1:]), "dp", 1),
        *cots,
        ones[0],
        swap_ranks(ones[1], "dp", 1),
        parts,
    )
    got = lax.all_to_all(parcel, "space", split_axis=0, concat_axis=0, tiled=True)
    total, latent = call(
        kernel_sum,
        (shape((rows_per, LATENT_AT), BF16), shape((group, slabs, CELLS), BF16)),
        got,
    )
    totals = [swap_ranks(total, "dp", k) if k else total for k in range(pieces)]
    one, two = call(
        functools.partial(kernel_final, pieces),
        (shape((16, 864), F32), shape((32, 27 * 128), F32)),
        place,
        *totals,
        spaces={0: pltpu.SMEM},
    )
    return latent[None], one, two


def solution(mesh):
    placed = (P("dp", "space", None, None), P(), P(), P("dp", "space", None, None))
    return jax.shard_map(
        on_device,
        mesh=mesh,
        in_specs=placed,
        out_specs=(P("dp", "space", None, None), P("space", None), P("space", None)),
        check_vma=False,
    )
```

```python
import functools

import jax
import jax.numpy as jnp
from jax import lax
from jax.experimental import pallas as pl
from jax.experimental.pallas import tpu as pltpu
from jax.sharding import PartitionSpec as P

F32 = jnp.float32
BF16 = jnp.bfloat16
VMEM_LIMIT = 16 * 1024 * 1024

NJ, NK, CELLS = 16, 8, 128
ONE_AT, WIDTH = 3456, 4320
HIDDEN_AT, PACK = (0, 8), 16
TAP_PHASE = {0: (1, 1), 1: (0, 0), 2: (1, 0)}


def dot(a, b):
    return jnp.dot(a, b, preferred_element_type=F32)


def iota(shape, axis):
    return lax.broadcasted_iota(jnp.int32, shape, axis)


def one_hot(mask):
    return jnp.where(mask, 1.0, 0.0).astype(BF16)


def cell_order(shifted):
    width = CELLS * (4 if shifted else 1)
    row, col = iota((CELLS, width), 0), iota((CELLS, width), 1)
    v, cell = col // CELLS, col % CELLS
    to_j, to_k = cell % NJ + v // 2, cell // NJ + v % 2
    return one_hot((to_k < NK) & (row == to_j * NK + to_k))


def fill_patches(planes, p1):
    row, col = iota((80, 64), 0), iota((80, 64), 1)
    pick = one_hot(col == 4 * (row % NJ) + row // NJ - 1)
    for a, rows in enumerate(planes):
        picked = dot(pick, rows).astype(BF16)
        for p in range(2):
            for b in range(3):
                rho = 2 * p + b
                for k in range(NK):
                    at = p * CELLS + k * NJ
                    p1[at : at + NJ, (3 * a + b) * 128 : (3 * a + b + 1) * 128] = picked[
                        rho * NJ : (rho + 1) * NJ, k * 128 : (k + 1) * 128
                    ]


def widen(w1, w_ext):
    for t in range(9):
        base, src = t * 128, t * 96
        zeros = jnp.zeros((128, 128), BF16)
        w_ext[base : base + 64, 0:128] = w1[src + 32 : src + 96, :]
        w_ext[base + 64 : base + 128, 0:128] = zeros[:64]
        w_ext[base : base + 32, 128:256] = zeros[:32]
        w_ext[base + 32 : base + 128, 128:256] = w1[src : src + 96, :]
        w_ext[base : base + 96, 256:384] = zeros[:96]
        w_ext[base + 96 : base + 128, 256:384] = w1[src : src + 32, :]


def fill_hidden(p1, w_ext, hidden, slope_t):
    for p in range(2):
        full = dot(p1[p * CELLS : (p + 1) * CELLS, :], w_ext[...])
        before = jnp.concatenate(
            [jnp.zeros((NJ, 128), F32), full[: CELLS - NJ, 256:384]], axis=0
        )
        for q, pre in enumerate((full[:, 0:128] + before, full[:, 128:256])):
            logistic = 1.0 / (1.0 + jnp.exp(-pre))
            hidden[2 * p + q] = (pre * logistic).astype(BF16)
            slope = logistic * (1.0 + pre * (1.0 - logistic))
            slope_t[2 * p + q] = slope.T


def kernel_parcels(pieces, _, __, cot_hbm, snap, parcels, halo, cot, sems):
    last = pltpu.make_async_copy(snap.at[pl.ds(3, 1)], halo, sems.at[0])
    whole = pltpu.make_async_copy(cot_hbm, cot, sems.at[1])
    whole.start()
    last.start()
    group, slabs = cot.shape[:2]
    rows_per = group // pieces
    row, col = iota((2 * group * slabs, group * slabs), 0), iota((2 * group * slabs, group * slabs), 1)
    slab = row // (2 * group) + row // rows_per % 2
    channel = row % (2 * group) // (2 * rows_per) * rows_per + row % rows_per
    chosen = one_hot((slab < slabs) & (col == channel * slabs + slab))
    whole.wait()
    flat = cot[...].astype(F32).reshape(-1, CELLS).astype(BF16)
    parcels[...] = dot(chosen, flat).astype(BF16).reshape(slabs, 2 * group, CELLS)
    last.wait()


class Phases:
    def __init__(self, pack, i):
        self.pack, self.at = pack, HIDDEN_AT[i]

    def __setitem__(self, phase, value):
        at = self.at + 2 * phase
        self.pack[at : at + 2] = value.reshape(2, 64, 128)

    def __getitem__(self, phase):
        at = self.at + 2 * phase
        return self.pack[at : at + 2].reshape(CELLS, 128)


def kernel_pack(snap, halo, w1, pack, slope_t, p1, w_ext):
    widen(w1, w_ext)
    for i, planes in enumerate(([halo[0], snap[0], snap[1]], [snap[1], snap[2], snap[3]])):
        fill_patches(planes, p1.at[i])
        fill_hidden(p1.at[i], w_ext, Phases(pack, i), slope_t.at[i])


def kernel_pieces(place, slot, cot, *outs):
    height = outs[0].shape[1]
    for k, out in enumerate(outs):
        at = pl.multiple_of((place[0] ^ k) * height, height)
        for n in range(out.shape[0]):
            out[n] = cot[slot[0] ^ n, pl.ds(at, height), :]


def kernel_back(pieces, rows_per, place, slot, slope_t, p1, w2, cot, *rest):
    *outs, grad_t = rest
    grad_one_share(pieces, rows_per, place, slot, w2, cot, outs, p1, slope_t, grad_t)


def grad_one_share(pieces, rows_per, place, slot, w2, cot, outs, p1, slope_t, grad_t):
    sources = cot.shape[0]
    moved = dot(cot[...].reshape(-1, CELLS), cell_order(True))
    moved = moved.reshape(sources * pieces, 2, rows_per, 4 * CELLS)
    planes = [moved[:, s].reshape(-1, 4 * CELLS).astype(BF16) for s in range(2)]
    for i in range(2):
        for p in range(2):
            for q in range(2):
                total = None
                for a in (1,) if i == 0 else (2, 0):
                    source = planes[1 if a == 0 else 0]
                    for b in (1,) if p == 0 else (2, 0):
                        for c in (1,) if q == 0 else (2, 0):
                            v = 2 * (b == 0) + (c == 0)
                            tap = 9 * a + 3 * b + c
                            term = dot(
                                w2[tap * 128 : (tap + 1) * 128, :],
                                source[:, v * CELLS : (v + 1) * CELLS],
                            )
                            total = term if total is None else total + term
                pre_t = total * slope_t[i, 2 * p + q]
                at = (2 * i + p) * CELLS
                grad_t[q * 128 : (q + 1) * 128, at : at + CELLS] = pre_t.astype(BF16)
                if q == 0:
                    ahead = pltpu.roll(pre_t, CELLS - NJ, axis=1)
                    ahead = jnp.where(iota((128, CELLS), 1) < CELLS - NJ, ahead, 0.0)
                    grad_t[256:384, at : at + CELLS] = ahead.astype(BF16)
    lane = iota((128, 128), 1)
    frames = []
    for t in range(9):
        cols = slice(t * 128, (t + 1) * 128)
        full = dot(grad_t[:, : 2 * CELLS], p1[0, :, cols])
        full = full + dot(grad_t[:, 2 * CELLS :], p1[1, :, cols])
        side = jnp.where(lane < 64, full[0:128], full[256:384])
        side = jnp.where((lane < 64) | (lane >= 96), side, 0.0)
        own = jnp.where(lane < 32, 0.0, full[128:256])
        frames.append(own + pltpu.roll(side, 64, axis=1))
    if pieces == 1:
        for t in range(9):
            outs[0][:, t * 96 : (t + 1) * 96] = frames[t][:, 32:]
        return
    owned = 128 // sources
    share = owned // 2
    row, col = iota((128 // 2, 128), 0), iota((128 // 2, 128), 1)
    frames = [frame.astype(BF16) for frame in frames]
    for k in range(2):
        half = (place[0] ^ k) & 1
        chosen = one_hot(col == (row // share ^ slot[0]) * owned + half * share + row % share)
        for t in range(9):
            value = dot(chosen, frames[t])
            outs[k][:, t * 96 : (t + 1) * 96] = value[:, 32:].astype(BF16)


def kernel_latent(pack, w2, parts):
    owners = parts.shape[0]
    group = parts.shape[1] // 2
    row, col = iota((CELLS, CELLS), 0), iota((CELLS, CELLS), 1)
    back = one_hot((row // NJ == col % NK) & (row % NJ == col // NK))
    for part, taps_x in enumerate(((1, 2), (0,))):
        totals = {}
        for b in range(3):
            p, sj = TAP_PHASE[b]
            for c in range(3):
                q, sk = TAP_PHASE[c]
                for a in taps_x:
                    tap = 9 * a + 3 * b + c
                    hidden = Phases(pack, 0 if a == 1 else 1)[2 * p + q]
                    term = dot(hidden, w2[tap * 128 : (tap + 1) * 128, :])
                    v = 2 * sj + sk
                    totals[v] = totals[v] + term if v in totals else term
        zero = jnp.zeros((NJ, totals[0].shape[1]), F32)

        def later(value):
            return jnp.concatenate([zero, value[: CELLS - NJ]], axis=0)

        inner = totals[2] + later(totals[3])
        inner = jnp.where(iota(inner.shape, 0) % NJ == 0, 0.0, pltpu.roll(inner, 1, axis=0))
        rows = totals[0] + later(totals[1]) + inner
        value = dot(rows.T.astype(BF16), back).reshape(owners, group, CELLS)
        parts[:, part * group : (part + 1) * group] = value.astype(BF16)


def moved_rows(cots, rows_per, order):
    moved = []
    for cot in cots:
        value = dot(cot[...].reshape(-1, CELLS), order).reshape(-1, 2, rows_per, 4 * CELLS)
        moved.append([value[:, s].reshape(-1, 4 * CELLS).astype(BF16) for s in range(2)])
    return [
        [
            jnp.concatenate([m[s][:, v * CELLS : (v + 1) * CELLS] for m in moved], axis=1)
            for v in range(4)
        ]
        for s in range(2)
    ]


def kernel_two(samples, rows_per, *refs):
    packs, cots, refs = refs[:samples], refs[samples : 2 * samples], refs[2 * samples :]
    packed = samples > 1
    if packed:
        ones, outs = refs[:2], refs[2:]
    left = moved_rows(cots, rows_per, cell_order(True))
    height = left[0][0].shape[0]
    for p in range(2):
        for q in range(2):
            right_0, right_1 = [
                jnp.concatenate([Phases(pack, i)[2 * p + q] for pack in packs], axis=0)
                for i in range(2)
            ]
            both = jnp.concatenate([right_0, right_1], axis=1)
            taps = [
                (b, c)
                for b in range(3)
                for c in range(3)
                if TAP_PHASE[b][0] == p and TAP_PHASE[c][0] == q
            ]
            shifts = [2 * TAP_PHASE[b][1] + TAP_PHASE[c][1] for b, c in taps]
            same = dot(jnp.concatenate([left[0][v] for v in shifts], axis=0), both)
            above = dot(jnp.concatenate([left[1][v] for v in shifts], axis=0), right_1)
            for n, (b, c) in enumerate(taps):
                rows = slice(n * height, (n + 1) * height)
                parts = (above[rows], same[rows, 0:128], same[rows, 128:256])
                for a, value in enumerate(parts):
                    to = (9 * a + 3 * b + c) * 128
                    if packed:
                        spread(value.reshape(-1, rows_per, 128), outs, to)
                    else:
                        refs[0][:, to : to + 128] = value
    if packed:
        total = ones[0][...].astype(F32) + ones[1][...].astype(F32)
        spread(total.reshape(-1, rows_per, WIDTH - ONE_AT), outs, ONE_AT)


def spread(value, outs, at):
    kept, near_1, near_2, near_3, lent, own_far = outs
    lanes = slice(at, at + value.shape[2])
    kept[:, lanes] = value[0]
    for n, near in enumerate((near_1, near_2, near_3), 1):
        near[:, lanes] = value[n].astype(BF16)
    for n in range(2):
        own_far[n, :, lanes] = value[4 + 2 * n]
        lent[n, :, lanes] = value[5 + 2 * n].astype(BF16)


def kernel_far(lent, own_far, *outs):
    for n, out in enumerate(outs):
        out[...] = (own_far[n] + lent[n].astype(F32)).astype(BF16)


def kernel_sum(kept, *refs):
    *others, total_out = refs
    total = kept[...]
    for other in others:
        total = total + other[...].astype(F32)
    total_out[...] = total.astype(BF16)


def kernel_join(got, latent):
    slabs, group = got.shape[0], got.shape[1] // 2
    next_ = got[:, group:].astype(F32)
    next_ = jnp.concatenate([jnp.zeros_like(next_[:1]), next_[:-1]], axis=0)
    cells = (got[:, :group].astype(F32) + next_).reshape(-1, CELLS).astype(BF16)
    height = slabs * group
    row, col = iota((height, height), 0), iota((height, height), 1)
    swap = one_hot((row // slabs == col % group) & (row % slabs == col // group))
    latent[...] = dot(swap, cells).reshape(group, slabs, CELLS).astype(BF16)


def kernel_final(pieces, place, *refs):
    parts, (one, two) = refs[:pieces], refs[pieces:]
    rows_per = parts[0].shape[0]
    for k in range(pieces):
        at = pl.multiple_of((place[0] ^ k) * rows_per, rows_per)
        two[pl.ds(at, rows_per), :] = parts[k][:, 0:ONE_AT].astype(F32)
    for k in range(2):
        at = pl.multiple_of(((place[0] ^ k) & 1) * rows_per, rows_per)
        shares = [parts[n][:, ONE_AT:WIDTH].astype(F32) for n in (k, k ^ 2)]
        one[pl.ds(at, rows_per), :] = shares[0] + shares[1]


def call(kernel, out_shape, *args, spaces=None, out_spaces=None, scratch=(), vmem=VMEM_LIMIT):
    spaces, out_spaces = spaces or {}, out_spaces or {}
    single = isinstance(out_shape, jax.ShapeDtypeStruct)

    def spec(n, of):
        return pl.BlockSpec(memory_space=of.get(n, pltpu.VMEM))

    moved = sum(x.size * x.dtype.itemsize for x in args)
    return pl.pallas_call(
        kernel,
        out_shape=out_shape,
        in_specs=[spec(n, spaces) for n in range(len(args))],
        out_specs=spec(0, {}) if single else [spec(n, out_spaces) for n in range(len(out_shape))],
        scratch_shapes=list(scratch),
        cost_estimate=pl.CostEstimate(flops=10**9, bytes_accessed=moved, transcendentals=0),
        compiler_params=pltpu.CompilerParams(vmem_limit_bytes=vmem),
    )(*args)


def shape(dims, dtype):
    return jax.ShapeDtypeStruct(dims, dtype)


def swap_ranks(block, axis, k):
    return lax.ppermute(block, axis, [(i, i ^ k) for i in range(lax.axis_size(axis))])


def first_of(value, *others):
    return lax.optimization_barrier((value, *others))[0]


def from_below(block, axis):
    return lax.ppermute(block, axis, [(i - 1, i) for i in range(1, lax.axis_size(axis))])


def on_device(snapshot, conv_one, conv_two, cotangent):
    slabs, samples = lax.axis_size("space"), lax.axis_size("dp")
    group = cotangent.shape[1]
    shared = samples == 4 and slabs == 8
    pieces = samples if shared else 1
    rows_per = group // pieces

    slab = snapshot[0]
    place, slot = [
        lax.axis_index(axis).astype(jnp.int32).reshape(1) for axis in ("dp", "space")
    ]
    parcels, last = call(
        functools.partial(kernel_parcels, pieces),
        (shape((slabs, 2 * group, CELLS), BF16), shape((1,) + slab.shape[1:], BF16)),
        place,
        slot,
        cotangent[0],
        slab,
        spaces={0: pltpu.SMEM, 1: pltpu.SMEM, 2: pltpu.HBM, 3: pltpu.HBM},
        scratch=[pltpu.VMEM((group, slabs, CELLS), BF16), pltpu.SemaphoreType.DMA((2,))],
        vmem=60 * 1024 * 1024,
    )
    halo = from_below(last, "space")
    cot = lax.all_to_all(parcels, "space", split_axis=0, concat_axis=0, tiled=True)
    pack, slope_t, p1 = call(
        kernel_pack,
        (
            shape((PACK, 64, CELLS), BF16),
            shape((2, 4, 128, CELLS), F32),
            shape((2, 2 * CELLS, 9 * 128), BF16),
        ),
        slab,
        halo,
        conv_one,
        scratch=[pltpu.VMEM((9 * 128, 384), BF16)],
    )
    ones = call(
        functools.partial(kernel_back, pieces, rows_per),
        (shape((64, 864), BF16),) * 2 if shared else (shape((128, 864), F32),),
        place,
        slot,
        slope_t,
        p1,
        conv_two,
        cot,
        spaces={0: pltpu.SMEM, 1: pltpu.SMEM},
        scratch=[pltpu.VMEM((384, 4 * CELLS), BF16)],
    )

    def latent_of(pack):
        return call(kernel_latent, shape((slabs, 2 * group, CELLS), BF16), pack, conv_two)

    def joined(parts):
        got = lax.all_to_all(parts, "space", split_axis=0, concat_axis=0, tiled=True)
        return call(kernel_join, shape((group, slabs, CELLS), BF16), got)[None]

    if not shared:
        two = call(
            functools.partial(kernel_two, 1, rows_per), shape((256, 27 * 128), F32), pack, cot
        )
        one, two = lax.psum((ones[0], two), "dp")
        one = lax.psum_scatter(one, "space", scatter_dimension=0, tiled=True)
        two = lax.psum_scatter(two, "space", scatter_dimension=0, tiled=True)
        return joined(latent_of(pack)), one, two

    across = swap_ranks(pack, "dp", 2)
    beside = swap_ranks(pack, "dp", 1)
    own, *cots = call(
        kernel_pieces,
        (shape((slabs, 2 * rows_per, CELLS), BF16),) * pieces,
        place,
        slot,
        cot,
        spaces={0: pltpu.SMEM, 1: pltpu.SMEM},
    )
    cots = [own] + [swap_ranks(piece, "dp", k) for k, piece in enumerate(cots, 1)]
    one_block = shape((rows_per, WIDTH), BF16)
    kept, near_1, near_2, near_3, lent, own_far = call(
        functools.partial(kernel_two, samples, rows_per),
        (
            shape((rows_per, WIDTH), F32),
            one_block,
            one_block,
            one_block,
            shape((2, rows_per, WIDTH), BF16),
            shape((2, rows_per, WIDTH), F32),
        ),
        pack,
        beside,
        across,
        swap_ranks(first_of(across, *ones, *cots[1:]), "dp", 1),
        *cots,
        ones[0],
        swap_ranks(ones[1], "dp", 1),
    )
    parts = latent_of(first_of(pack, lent))
    lent = swap_ranks(lent, "space", 1)
    far = call(kernel_far, (one_block, one_block), lent, own_far)
    others = [
        swap_ranks(block, "space", k)
        for k, block in ((1, near_1), (2, near_2), (3, near_3), (4, far[0]), (6, far[1]))
    ]
    latent = joined(first_of(parts, *far))
    total = call(kernel_sum, one_block, kept, *others)
    totals = [swap_ranks(total, "dp", k) if k else total for k in range(pieces)]
    one, two = call(
        functools.partial(kernel_final, pieces),
        (shape((16, 864), F32), shape((32, 27 * 128), F32)),
        place,
        *totals,
        spaces={0: pltpu.SMEM},
    )
    return latent, one, two


def solution(mesh):
    placed = (P("dp", "space", None, None), P(), P(), P("dp", "space", None, None))
    return jax.shard_map(
        on_device,
        mesh=mesh,
        in_specs=placed,
        out_specs=(P("dp", "space", None, None), P("space", None), P("space", None)),
        check_vma=False,
    )
```

```python
import functools

import jax
import jax.numpy as jnp
from jax import lax
from jax.experimental import pallas as pl
from jax.experimental.pallas import tpu as pltpu
from jax.sharding import PartitionSpec as P

F32 = jnp.float32
BF16 = jnp.bfloat16
VMEM_LIMIT = 16 * 1024 * 1024

NJ, NK, CELLS = 16, 8, 128
ONE_AT, WIDTH = 3456, 4320
HIDDEN_AT, PACK = (0, 8), 16
TAP_PHASE = {0: (1, 1), 1: (0, 0), 2: (1, 0)}


def dot(a, b):
    return jnp.dot(a, b, preferred_element_type=F32)


def iota(shape, axis):
    return lax.broadcasted_iota(jnp.int32, shape, axis)


def one_hot(mask):
    return jnp.where(mask, 1.0, 0.0).astype(BF16)


def cell_order(shifted):
    width = CELLS * (4 if shifted else 1)
    row, col = iota((CELLS, width), 0), iota((CELLS, width), 1)
    v, cell = col // CELLS, col % CELLS
    to_j, to_k = cell % NJ + v // 2, cell // NJ + v % 2
    return one_hot((to_k < NK) & (row == to_j * NK + to_k))


def fill_picked(planes, picked):
    row, col = iota((80, 64), 0), iota((80, 64), 1)
    pick = one_hot(col == 4 * (row % NJ) + row // NJ - 1)
    for x, rows in enumerate(planes):
        value = dot(pick, rows).astype(BF16)
        for rho in range(5):
            for k in range(NK):
                picked[x, rho, k * NJ : (k + 1) * NJ] = value[
                    rho * NJ : (rho + 1) * NJ, k * 128 : (k + 1) * 128
                ]


def widen(w1, w_ext):
    for t in range(9):
        base, src = t * 128, t * 96
        zeros = jnp.zeros((128, 128), BF16)
        w_ext[base : base + 64, 0:128] = w1[src + 32 : src + 96, :]
        w_ext[base + 64 : base + 128, 0:128] = zeros[:64]
        w_ext[base : base + 32, 128:256] = zeros[:32]
        w_ext[base + 32 : base + 128, 128:256] = w1[src : src + 96, :]
        w_ext[base : base + 96, 256:384] = zeros[:96]
        w_ext[base + 96 : base + 128, 256:384] = w1[src : src + 32, :]


def fill_hidden(picked, i, w_ext, hidden, slope_t):
    for p in range(2):
        patches = [picked[2 * i + a, 2 * p + b] for a in range(3) for b in range(3)]
        full = dot(jnp.concatenate(patches, axis=1), w_ext[...])
        before = jnp.concatenate(
            [jnp.zeros((NJ, 128), F32), full[: CELLS - NJ, 256:384]], axis=0
        )
        for q, pre in enumerate((full[:, 0:128] + before, full[:, 128:256])):
            logistic = 1.0 / (1.0 + jnp.exp(-pre))
            hidden[2 * p + q] = (pre * logistic).astype(BF16)
            slope = logistic * (1.0 + pre * (1.0 - logistic))
            slope_t[2 * p + q] = slope.T


def kernel_parcels(pieces, _, __, cot_hbm, snap, parcels, halo, cot, sems):
    last = pltpu.make_async_copy(snap.at[pl.ds(3, 1)], halo, sems.at[0])
    whole = pltpu.make_async_copy(cot_hbm, cot, sems.at[1])
    whole.start()
    last.start()
    group, slabs = cot.shape[:2]
    rows_per = group // pieces
    row, col = iota((2 * group * slabs, group * slabs), 0), iota((2 * group * slabs, group * slabs), 1)
    slab = row // (2 * group) + row // rows_per % 2
    channel = row % (2 * group) // (2 * rows_per) * rows_per + row % rows_per
    chosen = one_hot((slab < slabs) & (col == channel * slabs + slab))
    whole.wait()
    flat = cot[...].astype(F32).reshape(-1, CELLS).astype(BF16)
    parcels[...] = dot(chosen, flat).astype(BF16).reshape(slabs, 2 * group, CELLS)
    last.wait()


class Phases:
    def __init__(self, pack, i):
        self.pack, self.at = pack, HIDDEN_AT[i]

    def __setitem__(self, phase, value):
        at = self.at + 2 * phase
        self.pack[at : at + 2] = value.reshape(2, 64, 128)

    def __getitem__(self, phase):
        at = self.at + 2 * phase
        return self.pack[at : at + 2].reshape(CELLS, 128)


def kernel_pack(snap, halo, w1, pack, slope_t, picked, w_ext):
    widen(w1, w_ext)
    fill_picked([halo[0], snap[0], snap[1], snap[2], snap[3]], picked)
    for i in range(2):
        fill_hidden(picked, i, w_ext, Phases(pack, i), slope_t.at[i])


def kernel_pieces(place, slot, cot, *outs):
    height = outs[0].shape[1]
    for k, out in enumerate(outs):
        at = pl.multiple_of((place[0] ^ k) * height, height)
        for n in range(out.shape[0]):
            out[n] = cot[slot[0] ^ n, pl.ds(at, height), :]


def kernel_back(pieces, rows_per, place, slot, slope_t, picked, w2, cot, *rest):
    *outs, grad_t = rest
    grad_one_share(pieces, rows_per, place, slot, w2, cot, outs, picked, slope_t, grad_t)


def grad_one_share(pieces, rows_per, place, slot, w2, cot, outs, picked, slope_t, grad_t):
    sources = cot.shape[0]
    moved = dot(cot[...].reshape(-1, CELLS), cell_order(True))
    moved = moved.reshape(sources * pieces, 2, rows_per, 4 * CELLS)
    planes = [moved[:, s].reshape(-1, 4 * CELLS).astype(BF16) for s in range(2)]
    for i in range(2):
        for p in range(2):
            for q in range(2):
                total = None
                for a in (1,) if i == 0 else (2, 0):
                    source = planes[1 if a == 0 else 0]
                    for b in (1,) if p == 0 else (2, 0):
                        for c in (1,) if q == 0 else (2, 0):
                            v = 2 * (b == 0) + (c == 0)
                            tap = 9 * a + 3 * b + c
                            term = dot(
                                w2[tap * 128 : (tap + 1) * 128, :],
                                source[:, v * CELLS : (v + 1) * CELLS],
                            )
                            total = term if total is None else total + term
                pre_t = total * slope_t[i, 2 * p + q]
                at = (2 * i + p) * CELLS
                grad_t[q * 128 : (q + 1) * 128, at : at + CELLS] = pre_t.astype(BF16)
                if q == 0:
                    ahead = pltpu.roll(pre_t, CELLS - NJ, axis=1)
                    ahead = jnp.where(iota((128, CELLS), 1) < CELLS - NJ, ahead, 0.0)
                    grad_t[256:384, at : at + CELLS] = ahead.astype(BF16)
    lane = iota((128, 128), 1)
    frames = []
    for t in range(9):
        blocks = [picked[2 * i + t // 3, 2 * p + t % 3] for i in range(2) for p in range(2)]
        full = dot(grad_t[...], jnp.concatenate(blocks, axis=0))
        side = jnp.where(lane < 64, full[0:128], full[256:384])
        side = jnp.where((lane < 64) | (lane >= 96), side, 0.0)
        own = jnp.where(lane < 32, 0.0, full[128:256])
        frames.append(own + pltpu.roll(side, 64, axis=1))
    if pieces == 1:
        for t in range(9):
            outs[0][:, t * 96 : (t + 1) * 96] = frames[t][:, 32:]
        return
    owned = 128 // sources
    share = owned // 2
    row, col = iota((128 // 2, 128), 0), iota((128 // 2, 128), 1)
    frames = [frame.astype(BF16) for frame in frames]
    for k in range(2):
        half = (place[0] ^ k) & 1
        chosen = one_hot(col == (row // share ^ slot[0]) * owned + half * share + row % share)
        for t in range(9):
            value = dot(chosen, frames[t])
            outs[k][:, t * 96 : (t + 1) * 96] = value[:, 32:].astype(BF16)


def kernel_latent(pack, w2, parts):
    owners = parts.shape[0]
    group = parts.shape[1] // 2
    row, col = iota((CELLS, CELLS), 0), iota((CELLS, CELLS), 1)
    back = one_hot((row // NJ == col % NK) & (row % NJ == col // NK))
    for part, taps_x in enumerate(((1, 2), (0,))):
        totals = {}
        for b in range(3):
            p, sj = TAP_PHASE[b]
            for c in range(3):
                q, sk = TAP_PHASE[c]
                for a in taps_x:
                    tap = 9 * a + 3 * b + c
                    hidden = Phases(pack, 0 if a == 1 else 1)[2 * p + q]
                    term = dot(hidden, w2[tap * 128 : (tap + 1) * 128, :])
                    v = 2 * sj + sk
                    totals[v] = totals[v] + term if v in totals else term
        zero = jnp.zeros((NJ, totals[0].shape[1]), F32)

        def later(value):
            return jnp.concatenate([zero, value[: CELLS - NJ]], axis=0)

        inner = totals[2] + later(totals[3])
        inner = jnp.where(iota(inner.shape, 0) % NJ == 0, 0.0, pltpu.roll(inner, 1, axis=0))
        rows = totals[0] + later(totals[1]) + inner
        value = dot(rows.T.astype(BF16), back).reshape(owners, group, CELLS)
        parts[:, part * group : (part + 1) * group] = value.astype(BF16)


def moved_rows(cots, rows_per, order):
    moved = []
    for cot in cots:
        value = dot(cot[...].reshape(-1, CELLS), order).reshape(-1, 2, rows_per, 4 * CELLS)
        moved.append([value[:, s].reshape(-1, 4 * CELLS).astype(BF16) for s in range(2)])
    return [
        [
            jnp.concatenate([m[s][:, v * CELLS : (v + 1) * CELLS] for m in moved], axis=1)
            for v in range(4)
        ]
        for s in range(2)
    ]


def kernel_two(samples, rows_per, *refs):
    packs, cots, refs = refs[:samples], refs[samples : 2 * samples], refs[2 * samples :]
    packed = samples > 1
    if packed:
        ones, outs = refs[:2], refs[2:]
    left = moved_rows(cots, rows_per, cell_order(True))
    height = left[0][0].shape[0]
    for p in range(2):
        for q in range(2):
            right_0, right_1 = [
                jnp.concatenate([Phases(pack, i)[2 * p + q] for pack in packs], axis=0)
                for i in range(2)
            ]
            both = jnp.concatenate([right_0, right_1], axis=1)
            taps = [
                (b, c)
                for b in range(3)
                for c in range(3)
                if TAP_PHASE[b][0] == p and TAP_PHASE[c][0] == q
            ]
            shifts = [2 * TAP_PHASE[b][1] + TAP_PHASE[c][1] for b, c in taps]
            same = dot(jnp.concatenate([left[0][v] for v in shifts], axis=0), both)
            above = dot(jnp.concatenate([left[1][v] for v in shifts], axis=0), right_1)
            for n, (b, c) in enumerate(taps):
                rows = slice(n * height, (n + 1) * height)
                parts = (above[rows], same[rows, 0:128], same[rows, 128:256])
                for a, value in enumerate(parts):
                    to = (9 * a + 3 * b + c) * 128
                    if packed:
                        spread(value.reshape(-1, rows_per, 128), outs, to)
                    else:
                        refs[0][:, to : to + 128] = value
    if packed:
        total = ones[0][...].astype(F32) + ones[1][...].astype(F32)
        spread(total.reshape(-1, rows_per, WIDTH - ONE_AT), outs, ONE_AT)


def spread(value, outs, at):
    kept, near_1, near_2, near_3, lent, own_far = outs
    lanes = slice(at, at + value.shape[2])
    kept[:, lanes] = value[0]
    for n, near in enumerate((near_1, near_2, near_3), 1):
        near[:, lanes] = value[n].astype(BF16)
    for n in range(2):
        own_far[n, :, lanes] = value[4 + 2 * n]
        lent[n, :, lanes] = value[5 + 2 * n].astype(BF16)


def kernel_far(lent, own_far, *outs):
    for n, out in enumerate(outs):
        out[...] = (own_far[n] + lent[n].astype(F32)).astype(BF16)


def kernel_sum(kept, *refs):
    *others, total_out = refs
    total = kept[...]
    for other in others:
        total = total + other[...].astype(F32)
    total_out[...] = total.astype(BF16)


def kernel_join(got, latent):
    slabs, group = got.shape[0], got.shape[1] // 2
    next_ = got[:, group:].astype(F32)
    next_ = jnp.concatenate([jnp.zeros_like(next_[:1]), next_[:-1]], axis=0)
    cells = (got[:, :group].astype(F32) + next_).reshape(-1, CELLS).astype(BF16)
    height = slabs * group
    row, col = iota((height, height), 0), iota((height, height), 1)
    swap = one_hot((row // slabs == col % group) & (row % slabs == col // group))
    latent[...] = dot(swap, cells).reshape(group, slabs, CELLS).astype(BF16)


def kernel_final(pieces, place, *refs):
    parts, (one, two) = refs[:pieces], refs[pieces:]
    rows_per = parts[0].shape[0]
    for k in range(pieces):
        at = pl.multiple_of((place[0] ^ k) * rows_per, rows_per)
        two[pl.ds(at, rows_per), :] = parts[k][:, 0:ONE_AT].astype(F32)
    for k in range(2):
        at = pl.multiple_of(((place[0] ^ k) & 1) * rows_per, rows_per)
        shares = [parts[n][:, ONE_AT:WIDTH].astype(F32) for n in (k, k ^ 2)]
        one[pl.ds(at, rows_per), :] = shares[0] + shares[1]


def call(kernel, out_shape, *args, spaces=None, out_spaces=None, scratch=(), vmem=VMEM_LIMIT):
    spaces, out_spaces = spaces or {}, out_spaces or {}
    single = isinstance(out_shape, jax.ShapeDtypeStruct)

    def spec(n, of):
        return pl.BlockSpec(memory_space=of.get(n, pltpu.VMEM))

    moved = sum(x.size * x.dtype.itemsize for x in args)
    return pl.pallas_call(
        kernel,
        out_shape=out_shape,
        in_specs=[spec(n, spaces) for n in range(len(args))],
        out_specs=spec(0, {}) if single else [spec(n, out_spaces) for n in range(len(out_shape))],
        scratch_shapes=list(scratch),
        cost_estimate=pl.CostEstimate(flops=10**9, bytes_accessed=moved, transcendentals=0),
        compiler_params=pltpu.CompilerParams(vmem_limit_bytes=vmem),
    )(*args)


def shape(dims, dtype):
    return jax.ShapeDtypeStruct(dims, dtype)


def swap_ranks(block, axis, k):
    return lax.ppermute(block, axis, [(i, i ^ k) for i in range(lax.axis_size(axis))])


def first_of(value, *others):
    return lax.optimization_barrier((value, *others))[0]


def from_below(block, axis):
    return lax.ppermute(block, axis, [(i - 1, i) for i in range(1, lax.axis_size(axis))])


def on_device(snapshot, conv_one, conv_two, cotangent):
    slabs, samples = lax.axis_size("space"), lax.axis_size("dp")
    group = cotangent.shape[1]
    shared = samples == 4 and slabs == 8
    pieces = samples if shared else 1
    rows_per = group // pieces

    slab = snapshot[0]
    place, slot = [
        lax.axis_index(axis).astype(jnp.int32).reshape(1) for axis in ("dp", "space")
    ]
    parcels, last = call(
        functools.partial(kernel_parcels, pieces),
        (shape((slabs, 2 * group, CELLS), BF16), shape((1,) + slab.shape[1:], BF16)),
        place,
        slot,
        cotangent[0],
        slab,
        spaces={0: pltpu.SMEM, 1: pltpu.SMEM, 2: pltpu.HBM, 3: pltpu.HBM},
        scratch=[pltpu.VMEM((group, slabs, CELLS), BF16), pltpu.SemaphoreType.DMA((2,))],
        vmem=60 * 1024 * 1024,
    )
    halo = from_below(last, "space")
    cot = lax.all_to_all(parcels, "space", split_axis=0, concat_axis=0, tiled=True)
    pack, slope_t, picked = call(
        kernel_pack,
        (
            shape((PACK, 64, CELLS), BF16),
            shape((2, 4, 128, CELLS), F32),
            shape((5, 5, CELLS, 128), BF16),
        ),
        slab,
        halo,
        conv_one,
        scratch=[pltpu.VMEM((9 * 128, 384), BF16)],
    )
    ones = call(
        functools.partial(kernel_back, pieces, rows_per),
        (shape((64, 864), BF16),) * 2 if shared else (shape((128, 864), F32),),
        place,
        slot,
        slope_t,
        picked,
        conv_two,
        cot,
        spaces={0: pltpu.SMEM, 1: pltpu.SMEM},
        scratch=[pltpu.VMEM((384, 4 * CELLS), BF16)],
    )

    def latent_of(pack):
        return call(kernel_latent, shape((slabs, 2 * group, CELLS), BF16), pack, conv_two)

    def joined(parts):
        got = lax.all_to_all(parts, "space", split_axis=0, concat_axis=0, tiled=True)
        return call(kernel_join, shape((group, slabs, CELLS), BF16), got)[None]

    if not shared:
        two = call(
            functools.partial(kernel_two, 1, rows_per), shape((256, 27 * 128), F32), pack, cot
        )
        one, two = lax.psum((ones[0], two), "dp")
        one = lax.psum_scatter(one, "space", scatter_dimension=0, tiled=True)
        two = lax.psum_scatter(two, "space", scatter_dimension=0, tiled=True)
        return joined(latent_of(pack)), one, two

    across = swap_ranks(pack, "dp", 2)
    beside = swap_ranks(pack, "dp", 1)
    own, *cots = call(
        kernel_pieces,
        (shape((slabs, 2 * rows_per, CELLS), BF16),) * pieces,
        place,
        slot,
        cot,
        spaces={0: pltpu.SMEM, 1: pltpu.SMEM},
    )
    cots = [own] + [swap_ranks(piece, "dp", k) for k, piece in enumerate(cots, 1)]
    parts = latent_of(pack)
    one_block = shape((rows_per, WIDTH), BF16)
    kept, near_1, near_2, near_3, lent, own_far = call(
        functools.partial(kernel_two, samples, rows_per),
        (
            shape((rows_per, WIDTH), F32),
            one_block,
            one_block,
            one_block,
            shape((2, rows_per, WIDTH), BF16),
            shape((2, rows_per, WIDTH), F32),
        ),
        pack,
        beside,
        across,
        swap_ranks(first_of(across, *ones, *cots[1:], parts), "dp", 1),
        *cots,
        ones[0],
        swap_ranks(ones[1], "dp", 1),
    )
    lent = swap_ranks(lent, "space", 1)
    far = call(kernel_far, (one_block, one_block), lent, own_far)
    others = [
        swap_ranks(block, "space", k)
        for k, block in ((1, near_1), (2, near_2), (3, near_3), (4, far[0]), (6, far[1]))
    ]
    latent = joined(first_of(parts, *far))
    total = call(kernel_sum, one_block, kept, *others)
    totals = [swap_ranks(total, "dp", k) if k else total for k in range(pieces)]
    one, two = call(
        functools.partial(kernel_final, pieces),
        (shape((16, 864), F32), shape((32, 27 * 128), F32)),
        place,
        *totals,
        spaces={0: pltpu.SMEM},
    )
    return latent, one, two


def solution(mesh):
    placed = (P("dp", "space", None, None), P(), P(), P("dp", "space", None, None))
    return jax.shard_map(
        on_device,
        mesh=mesh,
        in_specs=placed,
        out_specs=(P("dp", "space", None, None), P("space", None), P("space", None)),
        check_vma=False,
    )
```

```python
import functools

import jax
import jax.numpy as jnp
from jax import lax
from jax.experimental import pallas as pl
from jax.experimental.pallas import tpu as pltpu
from jax.sharding import PartitionSpec as P

F32 = jnp.float32
BF16 = jnp.bfloat16
VMEM_LIMIT = 16 * 1024 * 1024

NJ, NK, CELLS = 16, 8, 128
ONE_AT, WIDTH = 3456, 4320
HIDDEN_AT, PACK = (0, 8), 16
TAP_PHASE = {0: (1, 1), 1: (0, 0), 2: (1, 0)}


def dot(a, b):
    return jnp.dot(a, b, preferred_element_type=F32)


def iota(shape, axis):
    return lax.broadcasted_iota(jnp.int32, shape, axis)


def one_hot(mask):
    return jnp.where(mask, 1.0, 0.0).astype(BF16)


def cell_order(shifted):
    width = CELLS * (4 if shifted else 1)
    row, col = iota((CELLS, width), 0), iota((CELLS, width), 1)
    v, cell = col // CELLS, col % CELLS
    to_j, to_k = cell % NJ + v // 2, cell // NJ + v % 2
    return one_hot((to_k < NK) & (row == to_j * NK + to_k))


def fill_picked(planes, picked):
    row, col = iota((80, 64), 0), iota((80, 64), 1)
    pick = one_hot(col == 4 * (row % NJ) + row // NJ - 1)
    for x, rows in enumerate(planes):
        value = dot(pick, rows).astype(BF16)
        for rho in range(5):
            for k in range(NK):
                picked[x, rho, k * NJ : (k + 1) * NJ] = value[
                    rho * NJ : (rho + 1) * NJ, k * 128 : (k + 1) * 128
                ]


def widen(w1, w_ext):
    for t in range(9):
        base, src = t * 128, t * 96
        zeros = jnp.zeros((128, 128), BF16)
        w_ext[base : base + 64, 0:128] = w1[src + 32 : src + 96, :]
        w_ext[base + 64 : base + 128, 0:128] = zeros[:64]
        w_ext[base : base + 32, 128:256] = zeros[:32]
        w_ext[base + 32 : base + 128, 128:256] = w1[src : src + 96, :]
        w_ext[base : base + 96, 256:384] = zeros[:96]
        w_ext[base + 96 : base + 128, 256:384] = w1[src : src + 32, :]


def fill_hidden(picked, i, w_ext, hidden, slope_t):
    for p in range(2):
        patches = [picked[2 * i + a, 2 * p + b] for a in range(3) for b in range(3)]
        full = dot(jnp.concatenate(patches, axis=1), w_ext[...])
        before = jnp.concatenate(
            [jnp.zeros((NJ, 128), F32), full[: CELLS - NJ, 256:384]], axis=0
        )
        for q, pre in enumerate((full[:, 0:128] + before, full[:, 128:256])):
            logistic = 1.0 / (1.0 + jnp.exp(-pre))
            if hidden is not None:
                hidden[2 * p + q] = (pre * logistic).astype(BF16)
            if slope_t is not None:
                slope = logistic * (1.0 + pre * (1.0 - logistic))
                slope_t[2 * p + q] = slope.T


def kernel_parcels(pieces, _, __, cot_hbm, snap, parcels, halo, cot, sems):
    last = pltpu.make_async_copy(snap.at[pl.ds(3, 1)], halo, sems.at[0])
    whole = pltpu.make_async_copy(cot_hbm, cot, sems.at[1])
    whole.start()
    last.start()
    group, slabs = cot.shape[:2]
    rows_per = group // pieces
    row, col = iota((2 * group * slabs, group * slabs), 0), iota((2 * group * slabs, group * slabs), 1)
    slab = row // (2 * group) + row // rows_per % 2
    channel = row % (2 * group) // (2 * rows_per) * rows_per + row % rows_per
    chosen = one_hot((slab < slabs) & (col == channel * slabs + slab))
    whole.wait()
    flat = cot[...].astype(F32).reshape(-1, CELLS).astype(BF16)
    parcels[...] = dot(chosen, flat).astype(BF16).reshape(slabs, 2 * group, CELLS)
    last.wait()


class Phases:
    def __init__(self, pack, i):
        self.pack, self.at = pack, HIDDEN_AT[i]

    def __setitem__(self, phase, value):
        at = self.at + 2 * phase
        self.pack[at : at + 2] = value.reshape(2, 64, 128)

    def __getitem__(self, phase):
        at = self.at + 2 * phase
        return self.pack[at : at + 2].reshape(CELLS, 128)


def kernel_pack(snap, halo, w1, pack, picked, w_ext):
    widen(w1, w_ext)
    fill_picked([halo[0], snap[0], snap[1], snap[2], snap[3]], picked)
    for i in range(2):
        fill_hidden(picked, i, w_ext, Phases(pack, i), None)


def kernel_pieces(place, slot, cot, *outs):
    height = outs[0].shape[1]
    for k, out in enumerate(outs):
        at = pl.multiple_of((place[0] ^ k) * height, height)
        for n in range(out.shape[0]):
            out[n] = cot[slot[0] ^ n, pl.ds(at, height), :]


def kernel_back(pieces, rows_per, place, slot, snap, halo, w1, w2, cot, *rest):
    *outs, slope_t, picked, w_ext, grad_t = rest
    widen(w1, w_ext)
    fill_picked([halo[0], snap[0], snap[1], snap[2], snap[3]], picked)
    for i in range(2):
        fill_hidden(picked, i, w_ext, None, slope_t.at[i])
    grad_one_share(pieces, rows_per, place, slot, w2, cot, outs, picked, slope_t, grad_t)


def grad_one_share(pieces, rows_per, place, slot, w2, cot, outs, picked, slope_t, grad_t):
    sources = cot.shape[0]
    moved = dot(cot[...].reshape(-1, CELLS), cell_order(True))
    moved = moved.reshape(sources * pieces, 2, rows_per, 4 * CELLS)
    planes = [moved[:, s].reshape(-1, 4 * CELLS).astype(BF16) for s in range(2)]
    for i in range(2):
        for p in range(2):
            for q in range(2):
                total = None
                for a in (1,) if i == 0 else (2, 0):
                    source = planes[1 if a == 0 else 0]
                    for b in (1,) if p == 0 else (2, 0):
                        for c in (1,) if q == 0 else (2, 0):
                            v = 2 * (b == 0) + (c == 0)
                            tap = 9 * a + 3 * b + c
                            term = dot(
                                w2[tap * 128 : (tap + 1) * 128, :],
                                source[:, v * CELLS : (v + 1) * CELLS],
                            )
                            total = term if total is None else total + term
                pre_t = total * slope_t[i, 2 * p + q]
                at = (2 * i + p) * CELLS
                grad_t[q * 128 : (q + 1) * 128, at : at + CELLS] = pre_t.astype(BF16)
                if q == 0:
                    ahead = pltpu.roll(pre_t, CELLS - NJ, axis=1)
                    ahead = jnp.where(iota((128, CELLS), 1) < CELLS - NJ, ahead, 0.0)
                    grad_t[256:384, at : at + CELLS] = ahead.astype(BF16)
    lane = iota((128, 128), 1)
    frames = []
    for t in range(9):
        blocks = [picked[2 * i + t // 3, 2 * p + t % 3] for i in range(2) for p in range(2)]
        full = dot(grad_t[...], jnp.concatenate(blocks, axis=0))
        side = jnp.where(lane < 64, full[0:128], full[256:384])
        side = jnp.where((lane < 64) | (lane >= 96), side, 0.0)
        own = jnp.where(lane < 32, 0.0, full[128:256])
        frames.append(own + pltpu.roll(side, 64, axis=1))
    if pieces == 1:
        for t in range(9):
            outs[0][:, t * 96 : (t + 1) * 96] = frames[t][:, 32:]
        return
    owned = 128 // sources
    share = owned // 2
    row, col = iota((128 // 2, 128), 0), iota((128 // 2, 128), 1)
    frames = [frame.astype(BF16) for frame in frames]
    for k in range(2):
        half = (place[0] ^ k) & 1
        chosen = one_hot(col == (row // share ^ slot[0]) * owned + half * share + row % share)
        for t in range(9):
            value = dot(chosen, frames[t])
            outs[k][:, t * 96 : (t + 1) * 96] = value[:, 32:].astype(BF16)


def kernel_latent(pack, w2, parts):
    owners = parts.shape[0]
    group = parts.shape[1] // 2
    row, col = iota((CELLS, CELLS), 0), iota((CELLS, CELLS), 1)
    back = one_hot((row // NJ == col % NK) & (row % NJ == col // NK))
    for part, taps_x in enumerate(((1, 2), (0,))):
        joined = {}
        for b in range(3):
            p, sj = TAP_PHASE[b]
            for c in range(3):
                q, sk = TAP_PHASE[c]
                for a in taps_x:
                    tap = 9 * a + 3 * b + c
                    hidden = Phases(pack, 0 if a == 1 else 1)[2 * p + q]
                    weights = w2[tap * 128 : (tap + 1) * 128, :]
                    joined.setdefault(2 * sj + sk, []).append((hidden, weights))
        totals = {
            v: dot(
                jnp.concatenate([hidden for hidden, _ in pairs], axis=1),
                jnp.concatenate([weights for _, weights in pairs], axis=0),
            )
            for v, pairs in joined.items()
        }
        zero = jnp.zeros((NJ, totals[0].shape[1]), F32)

        def later(value):
            return jnp.concatenate([zero, value[: CELLS - NJ]], axis=0)

        inner = totals[2] + later(totals[3])
        inner = jnp.where(iota(inner.shape, 0) % NJ == 0, 0.0, pltpu.roll(inner, 1, axis=0))
        rows = totals[0] + later(totals[1]) + inner
        value = dot(rows.T.astype(BF16), back).reshape(owners, group, CELLS)
        parts[:, part * group : (part + 1) * group] = value.astype(BF16)


def moved_rows(cots, rows_per, order):
    moved = []
    for cot in cots:
        value = dot(cot[...].reshape(-1, CELLS), order).reshape(-1, 2, rows_per, 4 * CELLS)
        moved.append([value[:, s].reshape(-1, 4 * CELLS).astype(BF16) for s in range(2)])
    return [
        [
            jnp.concatenate([m[s][:, v * CELLS : (v + 1) * CELLS] for m in moved], axis=1)
            for v in range(4)
        ]
        for s in range(2)
    ]


def kernel_left(rows_per, *refs):
    *cots, out = refs
    for s, values in enumerate(moved_rows(cots, rows_per, cell_order(True))):
        for v, value in enumerate(values):
            out[s, v] = value


def kernel_two(samples, rows_per, *refs):
    packs, left, refs = refs[:samples], refs[samples], refs[samples + 1 :]
    packed = samples > 1
    if packed:
        ones, outs = refs[:2], refs[2:]
    height = left.shape[2]
    for p in range(2):
        for q in range(2):
            right_0, right_1 = [
                jnp.concatenate([Phases(pack, i)[2 * p + q] for pack in packs], axis=0)
                for i in range(2)
            ]
            both = jnp.concatenate([right_0, right_1], axis=1)
            taps = [
                (b, c)
                for b in range(3)
                for c in range(3)
                if TAP_PHASE[b][0] == p and TAP_PHASE[c][0] == q
            ]
            shifts = [2 * TAP_PHASE[b][1] + TAP_PHASE[c][1] for b, c in taps]
            same = dot(jnp.concatenate([left[0, v] for v in shifts], axis=0), both)
            above = dot(jnp.concatenate([left[1, v] for v in shifts], axis=0), right_1)
            for n, (b, c) in enumerate(taps):
                rows = slice(n * height, (n + 1) * height)
                parts = (above[rows], same[rows, 0:128], same[rows, 128:256])
                for a, value in enumerate(parts):
                    to = (9 * a + 3 * b + c) * 128
                    if packed:
                        spread(value.reshape(-1, rows_per, 128), outs, to)
                    else:
                        refs[0][:, to : to + 128] = value
    if packed:
        total = ones[0][...].astype(F32) + ones[1][...].astype(F32)
        spread(total.reshape(-1, rows_per, WIDTH - ONE_AT), outs, ONE_AT)


def spread(value, outs, at):
    kept, near_1, near_2, near_3, lent, own_far = outs
    lanes = slice(at, at + value.shape[2])
    kept[:, lanes] = value[0]
    for n, near in enumerate((near_1, near_2, near_3), 1):
        near[:, lanes] = value[n].astype(BF16)
    for n in range(2):
        own_far[n, :, lanes] = value[4 + 2 * n]
        lent[n, :, lanes] = value[5 + 2 * n].astype(BF16)


def kernel_far(lent, own_far, *outs):
    for n, out in enumerate(outs):
        out[...] = (own_far[n] + lent[n].astype(F32)).astype(BF16)


def kernel_sum(kept, *refs):
    *others, total_out = refs
    total = kept[...]
    for other in others:
        total = total + other[...].astype(F32)
    total_out[...] = total.astype(BF16)


def join(got, latent):
    slabs, group = got.shape[0], got.shape[1] // 2
    next_ = got[:, group:].astype(F32)
    next_ = jnp.concatenate([jnp.zeros_like(next_[:1]), next_[:-1]], axis=0)
    cells = (got[:, :group].astype(F32) + next_).reshape(-1, CELLS).astype(BF16)
    height = slabs * group
    row, col = iota((height, height), 0), iota((height, height), 1)
    swap = one_hot((row // slabs == col % group) & (row % slabs == col // group))
    latent[...] = dot(swap, cells).reshape(group, slabs, CELLS).astype(BF16)


def kernel_final(pieces, place, *refs):
    parts, (got, one, two, latent) = refs[:pieces], refs[pieces:]
    join(got, latent)
    rows_per = parts[0].shape[0]
    for k in range(pieces):
        at = pl.multiple_of((place[0] ^ k) * rows_per, rows_per)
        two[pl.ds(at, rows_per), :] = parts[k][:, 0:ONE_AT].astype(F32)
    for k in range(2):
        at = pl.multiple_of(((place[0] ^ k) & 1) * rows_per, rows_per)
        shares = [parts[n][:, ONE_AT:WIDTH].astype(F32) for n in (k, k ^ 2)]
        one[pl.ds(at, rows_per), :] = shares[0] + shares[1]


def call(kernel, out_shape, *args, spaces=None, out_spaces=None, scratch=(), vmem=VMEM_LIMIT):
    spaces, out_spaces = spaces or {}, out_spaces or {}
    single = isinstance(out_shape, jax.ShapeDtypeStruct)

    def spec(n, of):
        return pl.BlockSpec(memory_space=of.get(n, pltpu.VMEM))

    moved = sum(x.size * x.dtype.itemsize for x in args)
    return pl.pallas_call(
        kernel,
        out_shape=out_shape,
        in_specs=[spec(n, spaces) for n in range(len(args))],
        out_specs=spec(0, {}) if single else [spec(n, out_spaces) for n in range(len(out_shape))],
        scratch_shapes=list(scratch),
        cost_estimate=pl.CostEstimate(flops=10**9, bytes_accessed=moved, transcendentals=0),
        compiler_params=pltpu.CompilerParams(vmem_limit_bytes=vmem),
    )(*args)


def shape(dims, dtype):
    return jax.ShapeDtypeStruct(dims, dtype)


def swap_ranks(block, axis, k):
    return lax.ppermute(block, axis, [(i, i ^ k) for i in range(lax.axis_size(axis))])


def first_of(value, *others):
    return lax.optimization_barrier((value, *others))[0]


def from_below(block, axis):
    return lax.ppermute(block, axis, [(i - 1, i) for i in range(1, lax.axis_size(axis))])


def on_device(snapshot, conv_one, conv_two, cotangent):
    slabs, samples = lax.axis_size("space"), lax.axis_size("dp")
    group = cotangent.shape[1]
    shared = samples == 4 and slabs == 8
    pieces = samples if shared else 1
    rows_per = group // pieces

    slab = snapshot[0]
    place, slot = [
        lax.axis_index(axis).astype(jnp.int32).reshape(1) for axis in ("dp", "space")
    ]
    parcels, last = call(
        functools.partial(kernel_parcels, pieces),
        (shape((slabs, 2 * group, CELLS), BF16), shape((1,) + slab.shape[1:], BF16)),
        place,
        slot,
        cotangent[0],
        slab,
        spaces={0: pltpu.SMEM, 1: pltpu.SMEM, 2: pltpu.HBM, 3: pltpu.HBM},
        scratch=[pltpu.VMEM((group, slabs, CELLS), BF16), pltpu.SemaphoreType.DMA((2,))],
        vmem=60 * 1024 * 1024,
    )
    halo = from_below(last, "space")
    cot = lax.all_to_all(parcels, "space", split_axis=0, concat_axis=0, tiled=True)
    forward = [pltpu.VMEM((5, 5, CELLS, 128), BF16), pltpu.VMEM((9 * 128, 384), BF16)]
    pack = call(
        kernel_pack, shape((PACK, 64, CELLS), BF16), slab, halo, conv_one, scratch=forward
    )
    ones = call(
        functools.partial(kernel_back, pieces, rows_per),
        (shape((64, 864), BF16),) * 2 if shared else (shape((128, 864), F32),),
        place,
        slot,
        slab,
        halo,
        conv_one,
        conv_two,
        cot,
        spaces={0: pltpu.SMEM, 1: pltpu.SMEM},
        scratch=[pltpu.VMEM((2, 4, 128, CELLS), F32), *forward]
        + [pltpu.VMEM((384, 4 * CELLS), BF16)],
    )

    def left_of(height, *cots):
        moved = shape((2, 4, height, len(cots) * CELLS), BF16)
        return call(functools.partial(kernel_left, rows_per), moved, *cots)

    def latent_of(pack):
        return call(kernel_latent, shape((slabs, 2 * group, CELLS), BF16), pack, conv_two)

    def exchanged(parts):
        return lax.all_to_all(parts, "space", split_axis=0, concat_axis=0, tiled=True)

    latent_shape = shape((group, slabs, CELLS), BF16)

    if not shared:
        two = call(
            functools.partial(kernel_two, 1, rows_per),
            shape((256, 27 * 128), F32),
            pack,
            left_of(256, cot),
        )
        one, two = lax.psum((ones[0], two), "dp")
        one = lax.psum_scatter(one, "space", scatter_dimension=0, tiled=True)
        two = lax.psum_scatter(two, "space", scatter_dimension=0, tiled=True)
        return call(join, latent_shape, exchanged(latent_of(pack)))[None], one, two

    across = swap_ranks(pack, "dp", 2)
    beside = swap_ranks(pack, "dp", 1)
    own, *cots = call(
        kernel_pieces,
        (shape((slabs, 2 * rows_per, CELLS), BF16),) * pieces,
        place,
        slot,
        cot,
        spaces={0: pltpu.SMEM, 1: pltpu.SMEM},
    )
    cots = [own] + [swap_ranks(piece, "dp", k) for k, piece in enumerate(cots, 1)]
    parts = latent_of(pack)
    one_block = shape((rows_per, WIDTH), BF16)
    kept, near_1, near_2, near_3, lent, own_far = call(
        functools.partial(kernel_two, samples, rows_per),
        (
            shape((rows_per, WIDTH), F32),
            one_block,
            one_block,
            one_block,
            shape((2, rows_per, WIDTH), BF16),
            shape((2, rows_per, WIDTH), F32),
        ),
        pack,
        beside,
        across,
        swap_ranks(first_of(across, *ones, *cots[1:], parts), "dp", 1),
        left_of(slabs * rows_per, *cots),
        ones[0],
        swap_ranks(ones[1], "dp", 1),
    )
    lent = swap_ranks(lent, "space", 1)
    far = call(kernel_far, (one_block, one_block), lent, own_far)
    others = [
        swap_ranks(block, "space", k)
        for k, block in ((1, near_1), (2, near_2), (3, near_3), (4, far[0]), (6, far[1]))
    ]
    got = exchanged(first_of(parts, *far))
    total = call(kernel_sum, one_block, kept, *others)
    totals = [swap_ranks(total, "dp", k) if k else total for k in range(pieces)]
    one, two, latent = call(
        functools.partial(kernel_final, pieces),
        (shape((16, 864), F32), shape((32, 27 * 128), F32), latent_shape),
        place,
        *totals,
        got,
        spaces={0: pltpu.SMEM},
    )
    return latent[None], one, two


def solution(mesh):
    placed = (P("dp", "space", None, None), P(), P(), P("dp", "space", None, None))
    return jax.shard_map(
        on_device,
        mesh=mesh,
        in_specs=placed,
        out_specs=(P("dp", "space", None, None), P("space", None), P("space", None)),
        check_vma=False,
    )
```

```python
import functools

import jax
import jax.numpy as jnp
from jax import lax
from jax.experimental import pallas as pl
from jax.experimental.pallas import tpu as pltpu
from jax.sharding import PartitionSpec as P

F32 = jnp.float32
BF16 = jnp.bfloat16
VMEM_LIMIT = 16 * 1024 * 1024

NJ, NK, CELLS = 16, 8, 128
ONE_AT, WIDTH = 3456, 4320
HIDDEN_AT, PACK = (0, 8), 16
TAP_PHASE = {0: (1, 1), 1: (0, 0), 2: (1, 0)}


def dot(a, b):
    return jnp.dot(a, b, preferred_element_type=F32)


def iota(shape, axis):
    return lax.broadcasted_iota(jnp.int32, shape, axis)


def one_hot(mask):
    return jnp.where(mask, 1.0, 0.0).astype(BF16)


def cell_order(shifted):
    width = CELLS * (4 if shifted else 1)
    row, col = iota((CELLS, width), 0), iota((CELLS, width), 1)
    v, cell = col // CELLS, col % CELLS
    to_j, to_k = cell % NJ + v // 2, cell // NJ + v % 2
    return one_hot((to_k < NK) & (row == to_j * NK + to_k))


def fill_picked(planes, picked):
    row, col = iota((80, 64), 0), iota((80, 64), 1)
    pick = one_hot(col == 4 * (row % NJ) + row // NJ - 1)
    for x, rows in enumerate(planes):
        value = dot(pick, rows).astype(BF16)
        for rho in range(5):
            for k in range(NK):
                picked[x, rho, k * NJ : (k + 1) * NJ] = value[
                    rho * NJ : (rho + 1) * NJ, k * 128 : (k + 1) * 128
                ]


def widen(w1, w_ext):
    for t in range(9):
        base, src = t * 128, t * 96
        zeros = jnp.zeros((128, 128), BF16)
        w_ext[base : base + 64, 0:128] = w1[src + 32 : src + 96, :]
        w_ext[base + 64 : base + 128, 0:128] = zeros[:64]
        w_ext[base : base + 32, 128:256] = zeros[:32]
        w_ext[base + 32 : base + 128, 128:256] = w1[src : src + 96, :]
        w_ext[base : base + 96, 256:384] = zeros[:96]
        w_ext[base + 96 : base + 128, 256:384] = w1[src : src + 32, :]


def fill_hidden(picked, i, w_ext, hidden, slope_t):
    for p in range(2):
        patches = [picked[2 * i + a, 2 * p + b] for a in range(3) for b in range(3)]
        full = dot(jnp.concatenate(patches, axis=1), w_ext[...])
        before = jnp.concatenate(
            [jnp.zeros((NJ, 128), F32), full[: CELLS - NJ, 256:384]], axis=0
        )
        for q, pre in enumerate((full[:, 0:128] + before, full[:, 128:256])):
            logistic = 1.0 / (1.0 + jnp.exp(-pre))
            if hidden is not None:
                hidden[2 * p + q] = (pre * logistic).astype(BF16)
            if slope_t is not None:
                slope = logistic * (1.0 + pre * (1.0 - logistic))
                slope_t[2 * p + q] = slope.T


def kernel_parcels(pieces, _, __, cot_hbm, snap, parcels, halo, cot, sems):
    last = pltpu.make_async_copy(snap.at[pl.ds(3, 1)], halo, sems.at[0])
    whole = pltpu.make_async_copy(cot_hbm, cot, sems.at[1])
    whole.start()
    last.start()
    group, slabs = cot.shape[:2]
    rows_per = group // pieces
    row, col = iota((2 * group * slabs, group * slabs), 0), iota((2 * group * slabs, group * slabs), 1)
    slab = row // (2 * group) + row // rows_per % 2
    channel = row % (2 * group) // (2 * rows_per) * rows_per + row % rows_per
    chosen = one_hot((slab < slabs) & (col == channel * slabs + slab))
    whole.wait()
    flat = cot[...].astype(F32).reshape(-1, CELLS).astype(BF16)
    parcels[...] = dot(chosen, flat).astype(BF16).reshape(slabs, 2 * group, CELLS)
    last.wait()


class Phases:
    def __init__(self, pack, i):
        self.pack, self.at = pack, HIDDEN_AT[i]

    def __setitem__(self, phase, value):
        at = self.at + 2 * phase
        self.pack[at : at + 2] = value.reshape(2, 64, 128)

    def __getitem__(self, phase):
        at = self.at + 2 * phase
        return self.pack[at : at + 2].reshape(CELLS, 128)


def kernel_pack(snap, halo, w1, pack, picked, w_ext):
    widen(w1, w_ext)
    fill_picked([halo[0], snap[0], snap[1], snap[2], snap[3]], picked)
    for i in range(2):
        fill_hidden(picked, i, w_ext, Phases(pack, i), None)


def kernel_pieces(place, slot, cot, *outs):
    height = outs[0].shape[1]
    for k, out in enumerate(outs):
        at = pl.multiple_of((place[0] ^ k) * height, height)
        for n in range(out.shape[0]):
            out[n] = cot[slot[0] ^ n, pl.ds(at, height), :]


def kernel_back(pieces, rows_per, place, slot, snap, halo, w1, w2, cot, *rest):
    *outs, slope_t, picked, w_ext, grad_t = rest
    widen(w1, w_ext)
    fill_picked([halo[0], snap[0], snap[1], snap[2], snap[3]], picked)
    for i in range(2):
        fill_hidden(picked, i, w_ext, None, slope_t.at[i])
    grad_one_share(pieces, rows_per, place, slot, w2, cot, outs, picked, slope_t, grad_t)


def grad_one_share(pieces, rows_per, place, slot, w2, cot, outs, picked, slope_t, grad_t):
    sources = cot.shape[0]
    moved = dot(cot[...].reshape(-1, CELLS), cell_order(True))
    moved = moved.reshape(sources * pieces, 2, rows_per, 4 * CELLS)
    planes = [moved[:, s].reshape(-1, 4 * CELLS).astype(BF16) for s in range(2)]
    for i in range(2):
        for p in range(2):
            for q in range(2):
                total = None
                for a in (1,) if i == 0 else (2, 0):
                    source = planes[1 if a == 0 else 0]
                    for b in (1,) if p == 0 else (2, 0):
                        for c in (1,) if q == 0 else (2, 0):
                            v = 2 * (b == 0) + (c == 0)
                            tap = 9 * a + 3 * b + c
                            term = dot(
                                w2[tap * 128 : (tap + 1) * 128, :],
                                source[:, v * CELLS : (v + 1) * CELLS],
                            )
                            total = term if total is None else total + term
                pre_t = total * slope_t[i, 2 * p + q]
                at = (2 * i + p) * CELLS
                grad_t[q * 128 : (q + 1) * 128, at : at + CELLS] = pre_t.astype(BF16)
                if q == 0:
                    ahead = pltpu.roll(pre_t, CELLS - NJ, axis=1)
                    ahead = jnp.where(iota((128, CELLS), 1) < CELLS - NJ, ahead, 0.0)
                    grad_t[256:384, at : at + CELLS] = ahead.astype(BF16)
    lane = iota((128, 128), 1)
    frames = []
    for t in range(9):
        blocks = [picked[2 * i + t // 3, 2 * p + t % 3] for i in range(2) for p in range(2)]
        full = dot(grad_t[...], jnp.concatenate(blocks, axis=0))
        side = jnp.where(lane < 64, full[0:128], full[256:384])
        side = jnp.where((lane < 64) | (lane >= 96), side, 0.0)
        own = jnp.where(lane < 32, 0.0, full[128:256])
        frames.append(own + pltpu.roll(side, 64, axis=1))
    if pieces == 1:
        for t in range(9):
            outs[0][:, t * 96 : (t + 1) * 96] = frames[t][:, 32:]
        return
    owned = 128 // sources
    share = owned // 2
    row, col = iota((128 // 2, 128), 0), iota((128 // 2, 128), 1)
    frames = [frame.astype(BF16) for frame in frames]
    for k in range(2):
        half = (place[0] ^ k) & 1
        chosen = one_hot(col == (row // share ^ slot[0]) * owned + half * share + row % share)
        for t in range(9):
            value = dot(chosen, frames[t])
            outs[k][:, t * 96 : (t + 1) * 96] = value[:, 32:].astype(BF16)


def kernel_latent(pack, w2, parts):
    owners = parts.shape[0]
    group = parts.shape[1] // 2
    row, col = iota((CELLS, CELLS), 0), iota((CELLS, CELLS), 1)
    back = one_hot((row // NJ == col % NK) & (row % NJ == col // NK))
    for part, taps_x in enumerate(((1, 2), (0,))):
        joined = {}
        for b in range(3):
            p, sj = TAP_PHASE[b]
            for c in range(3):
                q, sk = TAP_PHASE[c]
                for a in taps_x:
                    tap = 9 * a + 3 * b + c
                    hidden = Phases(pack, 0 if a == 1 else 1)[2 * p + q]
                    weights = w2[tap * 128 : (tap + 1) * 128, :]
                    joined.setdefault(2 * sj + sk, []).append((hidden, weights))
        totals = {
            v: dot(
                jnp.concatenate([hidden for hidden, _ in pairs], axis=1),
                jnp.concatenate([weights for _, weights in pairs], axis=0),
            )
            for v, pairs in joined.items()
        }
        zero = jnp.zeros((NJ, totals[0].shape[1]), F32)

        def later(value):
            return jnp.concatenate([zero, value[: CELLS - NJ]], axis=0)

        inner = totals[2] + later(totals[3])
        inner = jnp.where(iota(inner.shape, 0) % NJ == 0, 0.0, pltpu.roll(inner, 1, axis=0))
        rows = totals[0] + later(totals[1]) + inner
        value = dot(rows.T.astype(BF16), back).reshape(owners, group, CELLS)
        parts[:, part * group : (part + 1) * group] = value.astype(BF16)


def moved_rows(cots, rows_per, order):
    moved = []
    for cot in cots:
        value = dot(cot[...].reshape(-1, CELLS), order).reshape(-1, 2, rows_per, 4 * CELLS)
        moved.append([value[:, s].reshape(-1, 4 * CELLS).astype(BF16) for s in range(2)])
    return [
        [
            jnp.concatenate([m[s][:, v * CELLS : (v + 1) * CELLS] for m in moved], axis=1)
            for v in range(4)
        ]
        for s in range(2)
    ]


def kernel_left(rows_per, *refs):
    *cots, out = refs
    for s, values in enumerate(moved_rows(cots, rows_per, cell_order(True))):
        for v, value in enumerate(values):
            out[s, v] = value


def kernel_two(samples, rows_per, *refs):
    packs, left, refs = refs[:samples], refs[samples], refs[samples + 1 :]
    packed = samples > 1
    if packed:
        ones, outs = refs[:2], refs[2:]
    height = left.shape[2]
    for p in range(2):
        for q in range(2):
            right_0, right_1 = [
                jnp.concatenate([Phases(pack, i)[2 * p + q] for pack in packs], axis=0)
                for i in range(2)
            ]
            both = jnp.concatenate([right_0, right_1], axis=1)
            taps = [
                (b, c)
                for b in range(3)
                for c in range(3)
                if TAP_PHASE[b][0] == p and TAP_PHASE[c][0] == q
            ]
            shifts = [2 * TAP_PHASE[b][1] + TAP_PHASE[c][1] for b, c in taps]
            same = dot(jnp.concatenate([left[0, v] for v in shifts], axis=0), both)
            above = dot(jnp.concatenate([left[1, v] for v in shifts], axis=0), right_1)
            for n, (b, c) in enumerate(taps):
                rows = slice(n * height, (n + 1) * height)
                parts = (above[rows], same[rows, 0:128], same[rows, 128:256])
                for a, value in enumerate(parts):
                    to = (9 * a + 3 * b + c) * 128
                    if packed:
                        spread(value.reshape(-1, rows_per, 128), outs, to)
                    else:
                        refs[0][:, to : to + 128] = value
    if packed:
        total = ones[0][...].astype(F32) + ones[1][...].astype(F32)
        spread(total.reshape(-1, rows_per, WIDTH - ONE_AT), outs, ONE_AT)


def spread(value, outs, at):
    kept, near_1, near_2, near_3, lent, own_far = outs
    lanes = slice(at, at + value.shape[2])
    kept[:, lanes] = value[0]
    for n, near in enumerate((near_1, near_2, near_3), 1):
        near[:, lanes] = value[n].astype(BF16)
    for n in range(2):
        own_far[n, :, lanes] = value[4 + 2 * n]
        lent[n, :, lanes] = value[5 + 2 * n].astype(BF16)


def kernel_far(lent, own_far, *outs):
    for n, out in enumerate(outs):
        out[...] = (own_far[n] + lent[n].astype(F32)).astype(BF16)


def kernel_sum(kept, *refs):
    *others, total_out = refs
    total = kept[...]
    for other in others:
        total = total + other[...].astype(F32)
    total_out[...] = total.astype(BF16)


def join(got, latent):
    slabs, group = got.shape[0], got.shape[1] // 2
    next_ = got[:, group:].astype(F32)
    next_ = jnp.concatenate([jnp.zeros_like(next_[:1]), next_[:-1]], axis=0)
    cells = (got[:, :group].astype(F32) + next_).reshape(-1, CELLS).astype(BF16)
    height = slabs * group
    row, col = iota((height, height), 0), iota((height, height), 1)
    swap = one_hot((row // slabs == col % group) & (row % slabs == col // group))
    latent[...] = dot(swap, cells).reshape(group, slabs, CELLS).astype(BF16)


def kernel_final(pieces, place, *refs):
    parts, (got, one, two, latent) = refs[:pieces], refs[pieces:]
    join(got, latent)
    rows_per = parts[0].shape[0]
    for k in range(pieces):
        at = pl.multiple_of((place[0] ^ k) * rows_per, rows_per)
        two[pl.ds(at, rows_per), :] = parts[k][:, 0:ONE_AT].astype(F32)
    for k in range(2):
        at = pl.multiple_of(((place[0] ^ k) & 1) * rows_per, rows_per)
        shares = [parts[n][:, ONE_AT:WIDTH].astype(F32) for n in (k, k ^ 2)]
        one[pl.ds(at, rows_per), :] = shares[0] + shares[1]


def call(kernel, out_shape, *args, spaces=None, out_spaces=None, scratch=(), vmem=VMEM_LIMIT):
    spaces, out_spaces = spaces or {}, out_spaces or {}
    single = isinstance(out_shape, jax.ShapeDtypeStruct)

    def spec(n, of):
        return pl.BlockSpec(memory_space=of.get(n, pltpu.VMEM))

    moved = sum(x.size * x.dtype.itemsize for x in args)
    return pl.pallas_call(
        kernel,
        out_shape=out_shape,
        in_specs=[spec(n, spaces) for n in range(len(args))],
        out_specs=spec(0, {}) if single else [spec(n, out_spaces) for n in range(len(out_shape))],
        scratch_shapes=list(scratch),
        cost_estimate=pl.CostEstimate(flops=10**9, bytes_accessed=moved, transcendentals=0),
        compiler_params=pltpu.CompilerParams(vmem_limit_bytes=vmem),
    )(*args)


def shape(dims, dtype):
    return jax.ShapeDtypeStruct(dims, dtype)


def swap_ranks(block, axis, k):
    return lax.ppermute(block, axis, [(i, i ^ k) for i in range(lax.axis_size(axis))])


def first_of(value, *others):
    return lax.optimization_barrier((value, *others))[0]


def from_below(block, axis):
    return lax.ppermute(block, axis, [(i - 1, i) for i in range(1, lax.axis_size(axis))])


def on_device(snapshot, conv_one, conv_two, cotangent):
    slabs, samples = lax.axis_size("space"), lax.axis_size("dp")
    group = cotangent.shape[1]
    shared = samples == 4 and slabs == 8
    pieces = samples if shared else 1
    rows_per = group // pieces

    slab = snapshot[0]
    place, slot = [
        lax.axis_index(axis).astype(jnp.int32).reshape(1) for axis in ("dp", "space")
    ]
    parcels, last = call(
        functools.partial(kernel_parcels, pieces),
        (shape((slabs, 2 * group, CELLS), BF16), shape((1,) + slab.shape[1:], BF16)),
        place,
        slot,
        cotangent[0],
        slab,
        spaces={0: pltpu.SMEM, 1: pltpu.SMEM, 2: pltpu.HBM, 3: pltpu.HBM},
        scratch=[pltpu.VMEM((group, slabs, CELLS), BF16), pltpu.SemaphoreType.DMA((2,))],
        vmem=60 * 1024 * 1024,
    )
    halo = from_below(last, "space")
    cot = lax.all_to_all(parcels, "space", split_axis=0, concat_axis=0, tiled=True)
    forward = [pltpu.VMEM((5, 5, CELLS, 128), BF16), pltpu.VMEM((9 * 128, 384), BF16)]
    pack = call(
        kernel_pack, shape((PACK, 64, CELLS), BF16), slab, halo, conv_one, scratch=forward
    )
    ones = call(
        functools.partial(kernel_back, pieces, rows_per),
        (shape((64, 864), BF16),) * 2 if shared else (shape((128, 864), F32),),
        place,
        slot,
        slab,
        halo,
        conv_one,
        conv_two,
        cot,
        spaces={0: pltpu.SMEM, 1: pltpu.SMEM},
        scratch=[pltpu.VMEM((2, 4, 128, CELLS), F32), *forward]
        + [pltpu.VMEM((384, 4 * CELLS), BF16)],
    )

    def left_of(height, *cots):
        moved = shape((2, 4, height, len(cots) * CELLS), BF16)
        return call(functools.partial(kernel_left, rows_per), moved, *cots)

    def latent_of(pack):
        return call(kernel_latent, shape((slabs, 2 * group, CELLS), BF16), pack, conv_two)

    def exchanged(parts):
        return lax.all_to_all(parts, "space", split_axis=0, concat_axis=0, tiled=True)

    latent_shape = shape((group, slabs, CELLS), BF16)

    if not shared:
        two = call(
            functools.partial(kernel_two, 1, rows_per),
            shape((256, 27 * 128), F32),
            pack,
            left_of(256, cot),
        )
        one, two = lax.psum((ones[0], two), "dp")
        one = lax.psum_scatter(one, "space", scatter_dimension=0, tiled=True)
        two = lax.psum_scatter(two, "space", scatter_dimension=0, tiled=True)
        return call(join, latent_shape, exchanged(latent_of(pack)))[None], one, two

    across = swap_ranks(pack, "dp", 2)
    beside = swap_ranks(first_of(pack, cot), "dp", 1)
    own, *cots = call(
        kernel_pieces,
        (shape((slabs, 2 * rows_per, CELLS), BF16),) * pieces,
        place,
        slot,
        cot,
        spaces={0: pltpu.SMEM, 1: pltpu.SMEM},
    )
    cots = [own] + [swap_ranks(piece, "dp", k) for k, piece in enumerate(cots, 1)]
    parts = latent_of(pack)
    one_block = shape((rows_per, WIDTH), BF16)
    kept, near_1, near_2, near_3, lent, own_far = call(
        functools.partial(kernel_two, samples, rows_per),
        (
            shape((rows_per, WIDTH), F32),
            one_block,
            one_block,
            one_block,
            shape((2, rows_per, WIDTH), BF16),
            shape((2, rows_per, WIDTH), F32),
        ),
        pack,
        beside,
        across,
        swap_ranks(first_of(across, *ones, *cots[1:], parts), "dp", 1),
        left_of(slabs * rows_per, *cots),
        ones[0],
        swap_ranks(ones[1], "dp", 1),
    )
    lent = swap_ranks(lent, "space", 1)
    far = call(kernel_far, (one_block, one_block), lent, own_far)
    others = [
        swap_ranks(block, "space", k)
        for k, block in ((1, near_1), (2, near_2), (3, near_3), (4, far[0]), (6, far[1]))
    ]
    got = exchanged(first_of(parts, *far))
    total = call(kernel_sum, one_block, kept, *others)
    totals = [swap_ranks(total, "dp", k) if k else total for k in range(pieces)]
    one, two, latent = call(
        functools.partial(kernel_final, pieces),
        (shape((16, 864), F32), shape((32, 27 * 128), F32), latent_shape),
        place,
        *totals,
        got,
        spaces={0: pltpu.SMEM},
    )
    return latent[None], one, two


def solution(mesh):
    placed = (P("dp", "space", None, None), P(), P(), P("dp", "space", None, None))
    return jax.shard_map(
        on_device,
        mesh=mesh,
        in_specs=placed,
        out_specs=(P("dp", "space", None, None), P("space", None), P("space", None)),
        check_vma=False,
    )
```

```python
import functools

import jax
import jax.numpy as jnp
from jax import lax
from jax.experimental import pallas as pl
from jax.experimental.pallas import tpu as pltpu
from jax.sharding import PartitionSpec as P

F32 = jnp.float32
BF16 = jnp.bfloat16
VMEM_LIMIT = 16 * 1024 * 1024

NJ, NK, CELLS = 16, 8, 128
ONE_AT, WIDTH = 3456, 4320
HIDDEN_AT, PACK = (0, 8), 16
TAP_PHASE = {0: (1, 1), 1: (0, 0), 2: (1, 0)}


def dot(a, b):
    return jnp.dot(a, b, preferred_element_type=F32)


def iota(shape, axis):
    return lax.broadcasted_iota(jnp.int32, shape, axis)


def one_hot(mask):
    return jnp.where(mask, 1.0, 0.0).astype(BF16)


def cell_order(shifted):
    width = CELLS * (4 if shifted else 1)
    row, col = iota((CELLS, width), 0), iota((CELLS, width), 1)
    v, cell = col // CELLS, col % CELLS
    to_j, to_k = cell % NJ + v // 2, cell // NJ + v % 2
    return one_hot((to_k < NK) & (row == to_j * NK + to_k))


def fill_picked(planes, picked):
    row, col = iota((80, 64), 0), iota((80, 64), 1)
    pick = one_hot(col == 4 * (row % NJ) + row // NJ - 1)
    for x, rows in enumerate(planes):
        value = dot(pick, rows).astype(BF16)
        for rho in range(5):
            for k in range(NK):
                picked[x, rho, k * NJ : (k + 1) * NJ] = value[
                    rho * NJ : (rho + 1) * NJ, k * 128 : (k + 1) * 128
                ]


def widen(w1, w_ext):
    for t in range(9):
        base, src = t * 128, t * 96
        zeros = jnp.zeros((128, 128), BF16)
        w_ext[base : base + 64, 0:128] = w1[src + 32 : src + 96, :]
        w_ext[base + 64 : base + 128, 0:128] = zeros[:64]
        w_ext[base : base + 32, 128:256] = zeros[:32]
        w_ext[base + 32 : base + 128, 128:256] = w1[src : src + 96, :]
        w_ext[base : base + 96, 256:384] = zeros[:96]
        w_ext[base + 96 : base + 128, 256:384] = w1[src : src + 32, :]


def fill_hidden(picked, i, w_ext, hidden, slope_t):
    for p in range(2):
        patches = [picked[2 * i + a, 2 * p + b] for a in range(3) for b in range(3)]
        full = dot(jnp.concatenate(patches, axis=1), w_ext[...])
        before = jnp.concatenate(
            [jnp.zeros((NJ, 128), F32), full[: CELLS - NJ, 256:384]], axis=0
        )
        for q, pre in enumerate((full[:, 0:128] + before, full[:, 128:256])):
            logistic = 1.0 / (1.0 + jnp.exp(-pre))
            if hidden is not None:
                hidden[2 * p + q] = (pre * logistic).astype(BF16)
            if slope_t is not None:
                slope = logistic * (1.0 + pre * (1.0 - logistic))
                slope_t[2 * p + q] = slope.T


def kernel_parcels(pieces, _, __, cot_hbm, snap, parcels, halo, cot, sems):
    last = pltpu.make_async_copy(snap.at[pl.ds(3, 1)], halo, sems.at[0])
    whole = pltpu.make_async_copy(cot_hbm, cot, sems.at[1])
    whole.start()
    last.start()
    group, slabs = cot.shape[:2]
    rows_per = group // pieces
    row, col = iota((2 * group * slabs, group * slabs), 0), iota((2 * group * slabs, group * slabs), 1)
    slab = row // (2 * group) + row // rows_per % 2
    channel = row % (2 * group) // (2 * rows_per) * rows_per + row % rows_per
    chosen = one_hot((slab < slabs) & (col == channel * slabs + slab))
    whole.wait()
    flat = cot[...].astype(F32).reshape(-1, CELLS).astype(BF16)
    parcels[...] = dot(chosen, flat).astype(BF16).reshape(slabs, 2 * group, CELLS)
    last.wait()


class Phases:
    def __init__(self, pack, i):
        self.pack, self.at = pack, HIDDEN_AT[i]

    def __setitem__(self, phase, value):
        at = self.at + 2 * phase
        self.pack[at : at + 2] = value.reshape(2, 64, 128)

    def __getitem__(self, phase):
        at = self.at + 2 * phase
        return self.pack[at : at + 2].reshape(CELLS, 128)


def kernel_pack(snap, halo, w1, pack, picked, w_ext):
    widen(w1, w_ext)
    fill_picked([halo[0], snap[0], snap[1], snap[2], snap[3]], picked)
    for i in range(2):
        fill_hidden(picked, i, w_ext, Phases(pack, i), None)


def kernel_pieces(place, slot, cot, *outs):
    height = outs[0].shape[1]
    for k, out in enumerate(outs):
        at = pl.multiple_of((place[0] ^ k) * height, height)
        for n in range(out.shape[0]):
            out[n] = cot[slot[0] ^ n, pl.ds(at, height), :]


def kernel_back(pieces, rows_per, place, slot, snap, halo, w1, w2, cot, *rest):
    *outs, slope_t, picked, w_ext, grad_t = rest
    widen(w1, w_ext)
    fill_picked([halo[0], snap[0], snap[1], snap[2], snap[3]], picked)
    for i in range(2):
        fill_hidden(picked, i, w_ext, None, slope_t.at[i])
    grad_one_share(pieces, rows_per, place, slot, w2, cot, outs, picked, slope_t, grad_t)


def grad_one_share(pieces, rows_per, place, slot, w2, cot, outs, picked, slope_t, grad_t):
    sources = cot.shape[0]
    moved = dot(cot[...].reshape(-1, CELLS), cell_order(True))
    moved = moved.reshape(sources * pieces, 2, rows_per, 4 * CELLS)
    planes = [moved[:, s].reshape(-1, 4 * CELLS).astype(BF16) for s in range(2)]
    for i in range(2):
        for p in range(2):
            for q in range(2):
                total = None
                for a in (1,) if i == 0 else (2, 0):
                    source = planes[1 if a == 0 else 0]
                    for b in (1,) if p == 0 else (2, 0):
                        for c in (1,) if q == 0 else (2, 0):
                            v = 2 * (b == 0) + (c == 0)
                            tap = 9 * a + 3 * b + c
                            term = dot(
                                w2[tap * 128 : (tap + 1) * 128, :],
                                source[:, v * CELLS : (v + 1) * CELLS],
                            )
                            total = term if total is None else total + term
                pre_t = total * slope_t[i, 2 * p + q]
                at = (2 * i + p) * CELLS
                grad_t[q * 128 : (q + 1) * 128, at : at + CELLS] = pre_t.astype(BF16)
                if q == 0:
                    ahead = pltpu.roll(pre_t, CELLS - NJ, axis=1)
                    ahead = jnp.where(iota((128, CELLS), 1) < CELLS - NJ, ahead, 0.0)
                    grad_t[256:384, at : at + CELLS] = ahead.astype(BF16)
    lane = iota((128, 128), 1)
    frames = []
    products = []
    for first in range(0, 9, 2):
        columns = []
        for t in range(first, min(first + 2, 9)):
            blocks = [picked[2 * i + t // 3, 2 * p + t % 3] for i in range(2) for p in range(2)]
            columns.append(jnp.concatenate(blocks, axis=0))
        both = dot(grad_t[...], jnp.concatenate(columns, axis=1))
        products += [both[:, n * 128 : (n + 1) * 128] for n in range(len(columns))]
    for full in products:
        side = jnp.where(lane < 64, full[0:128], full[256:384])
        side = jnp.where((lane < 64) | (lane >= 96), side, 0.0)
        own = jnp.where(lane < 32, 0.0, full[128:256])
        frames.append(own + pltpu.roll(side, 64, axis=1))
    if pieces == 1:
        for t in range(9):
            outs[0][:, t * 96 : (t + 1) * 96] = frames[t][:, 32:]
        return
    owned = 128 // sources
    share = owned // 2
    row, col = iota((128 // 2, 128), 0), iota((128 // 2, 128), 1)
    frames = [frame.astype(BF16) for frame in frames]
    halves = []
    for k in range(2):
        half = (place[0] ^ k) & 1
        halves.append(
            one_hot(col == (row // share ^ slot[0]) * owned + half * share + row % share)
        )
    chosen = jnp.concatenate(halves, axis=0)
    for first in range(0, 9, 2):
        value = dot(chosen, jnp.concatenate(frames[first : first + 2], axis=1))
        for t in range(first, min(first + 2, 9)):
            at = (t - first) * 128 + 32
            for k in range(2):
                part = value[k * 64 : (k + 1) * 64, at : at + 96]
                outs[k][:, t * 96 : (t + 1) * 96] = part.astype(BF16)


def kernel_latent(pack, w2, parts):
    owners = parts.shape[0]
    group = parts.shape[1] // 2
    row, col = iota((CELLS, CELLS), 0), iota((CELLS, CELLS), 1)
    back = one_hot((row // NJ == col % NK) & (row % NJ == col // NK))
    for part, taps_x in enumerate(((1, 2), (0,))):
        joined = {}
        for b in range(3):
            p, sj = TAP_PHASE[b]
            for c in range(3):
                q, sk = TAP_PHASE[c]
                for a in taps_x:
                    tap = 9 * a + 3 * b + c
                    hidden = Phases(pack, 0 if a == 1 else 1)[2 * p + q]
                    weights = w2[tap * 128 : (tap + 1) * 128, :]
                    joined.setdefault(2 * sj + sk, []).append((hidden, weights))
        totals = {
            v: dot(
                jnp.concatenate([hidden for hidden, _ in pairs], axis=1),
                jnp.concatenate([weights for _, weights in pairs], axis=0),
            )
            for v, pairs in joined.items()
        }
        zero = jnp.zeros((NJ, totals[0].shape[1]), F32)

        def later(value):
            return jnp.concatenate([zero, value[: CELLS - NJ]], axis=0)

        inner = totals[2] + later(totals[3])
        inner = jnp.where(iota(inner.shape, 0) % NJ == 0, 0.0, pltpu.roll(inner, 1, axis=0))
        rows = totals[0] + later(totals[1]) + inner
        value = dot(rows.T.astype(BF16), back).reshape(owners, group, CELLS)
        parts[:, part * group : (part + 1) * group] = value.astype(BF16)


def moved_rows(cots, rows_per, order):
    moved = []
    for cot in cots:
        value = dot(cot[...].reshape(-1, CELLS), order).reshape(-1, 2, rows_per, 4 * CELLS)
        moved.append([value[:, s].reshape(-1, 4 * CELLS).astype(BF16) for s in range(2)])
    return [
        [
            jnp.concatenate([m[s][:, v * CELLS : (v + 1) * CELLS] for m in moved], axis=1)
            for v in range(4)
        ]
        for s in range(2)
    ]


def kernel_left(rows_per, *refs):
    *cots, out = refs
    for s, values in enumerate(moved_rows(cots, rows_per, cell_order(True))):
        for v, value in enumerate(values):
            out[s, v] = value


def kernel_two(samples, rows_per, *refs):
    packs, left, refs = refs[:samples], refs[samples], refs[samples + 1 :]
    packed = samples > 1
    if packed:
        ones, outs = refs[:2], refs[2:]
    height = left.shape[2]
    for p in range(2):
        for q in range(2):
            right_0, right_1 = [
                jnp.concatenate([Phases(pack, i)[2 * p + q] for pack in packs], axis=0)
                for i in range(2)
            ]
            both = jnp.concatenate([right_0, right_1], axis=1)
            taps = [
                (b, c)
                for b in range(3)
                for c in range(3)
                if TAP_PHASE[b][0] == p and TAP_PHASE[c][0] == q
            ]
            shifts = [2 * TAP_PHASE[b][1] + TAP_PHASE[c][1] for b, c in taps]
            same = dot(jnp.concatenate([left[0, v] for v in shifts], axis=0), both)
            above = dot(jnp.concatenate([left[1, v] for v in shifts], axis=0), right_1)
            for n, (b, c) in enumerate(taps):
                rows = slice(n * height, (n + 1) * height)
                parts = (above[rows], same[rows, 0:128], same[rows, 128:256])
                for a, value in enumerate(parts):
                    to = (9 * a + 3 * b + c) * 128
                    if packed:
                        spread(value.reshape(-1, rows_per, 128), outs, to)
                    else:
                        refs[0][:, to : to + 128] = value
    if packed:
        total = ones[0][...].astype(F32) + ones[1][...].astype(F32)
        spread(total.reshape(-1, rows_per, WIDTH - ONE_AT), outs, ONE_AT)


def spread(value, outs, at):
    kept, near_1, near_2, near_3, lent, own_far = outs
    lanes = slice(at, at + value.shape[2])
    kept[:, lanes] = value[0]
    for n, near in enumerate((near_1, near_2, near_3), 1):
        near[:, lanes] = value[n].astype(BF16)
    for n in range(2):
        own_far[n, :, lanes] = value[4 + 2 * n]
        lent[n, :, lanes] = value[5 + 2 * n].astype(BF16)


def kernel_far(lent, own_far, *outs):
    for n, out in enumerate(outs):
        out[...] = (own_far[n] + lent[n].astype(F32)).astype(BF16)


def kernel_sum(kept, *refs):
    *others, total_out = refs
    total = kept[...]
    for other in others:
        total = total + other[...].astype(F32)
    total_out[...] = total.astype(BF16)


def join(got, latent):
    slabs, group = got.shape[0], got.shape[1] // 2
    next_ = got[:, group:].astype(F32)
    next_ = jnp.concatenate([jnp.zeros_like(next_[:1]), next_[:-1]], axis=0)
    cells = (got[:, :group].astype(F32) + next_).reshape(-1, CELLS).astype(BF16)
    height = slabs * group
    row, col = iota((height, height), 0), iota((height, height), 1)
    swap = one_hot((row // slabs == col % group) & (row % slabs == col // group))
    latent[...] = dot(swap, cells).reshape(group, slabs, CELLS).astype(BF16)


def kernel_final(pieces, place, *refs):
    parts, (got, one, two, latent) = refs[:pieces], refs[pieces:]
    join(got, latent)
    rows_per = parts[0].shape[0]
    for k in range(pieces):
        at = pl.multiple_of((place[0] ^ k) * rows_per, rows_per)
        two[pl.ds(at, rows_per), :] = parts[k][:, 0:ONE_AT].astype(F32)
    for k in range(2):
        at = pl.multiple_of(((place[0] ^ k) & 1) * rows_per, rows_per)
        shares = [parts[n][:, ONE_AT:WIDTH].astype(F32) for n in (k, k ^ 2)]
        one[pl.ds(at, rows_per), :] = shares[0] + shares[1]


def call(kernel, out_shape, *args, spaces=None, out_spaces=None, scratch=(), vmem=VMEM_LIMIT):
    spaces, out_spaces = spaces or {}, out_spaces or {}
    single = isinstance(out_shape, jax.ShapeDtypeStruct)

    def spec(n, of):
        return pl.BlockSpec(memory_space=of.get(n, pltpu.VMEM))

    moved = sum(x.size * x.dtype.itemsize for x in args)
    return pl.pallas_call(
        kernel,
        out_shape=out_shape,
        in_specs=[spec(n, spaces) for n in range(len(args))],
        out_specs=spec(0, {}) if single else [spec(n, out_spaces) for n in range(len(out_shape))],
        scratch_shapes=list(scratch),
        cost_estimate=pl.CostEstimate(flops=10**9, bytes_accessed=moved, transcendentals=0),
        compiler_params=pltpu.CompilerParams(vmem_limit_bytes=vmem),
    )(*args)


def shape(dims, dtype):
    return jax.ShapeDtypeStruct(dims, dtype)


def swap_ranks(block, axis, k):
    return lax.ppermute(block, axis, [(i, i ^ k) for i in range(lax.axis_size(axis))])


def first_of(value, *others):
    return lax.optimization_barrier((value, *others))[0]


def from_below(block, axis):
    return lax.ppermute(block, axis, [(i - 1, i) for i in range(1, lax.axis_size(axis))])


def on_device(snapshot, conv_one, conv_two, cotangent):
    slabs, samples = lax.axis_size("space"), lax.axis_size("dp")
    group = cotangent.shape[1]
    shared = samples == 4 and slabs == 8
    pieces = samples if shared else 1
    rows_per = group // pieces

    slab = snapshot[0]
    place, slot = [
        lax.axis_index(axis).astype(jnp.int32).reshape(1) for axis in ("dp", "space")
    ]
    parcels, last = call(
        functools.partial(kernel_parcels, pieces),
        (shape((slabs, 2 * group, CELLS), BF16), shape((1,) + slab.shape[1:], BF16)),
        place,
        slot,
        cotangent[0],
        slab,
        spaces={0: pltpu.SMEM, 1: pltpu.SMEM, 2: pltpu.HBM, 3: pltpu.HBM},
        scratch=[pltpu.VMEM((group, slabs, CELLS), BF16), pltpu.SemaphoreType.DMA((2,))],
        vmem=60 * 1024 * 1024,
    )
    halo = from_below(last, "space")
    cot = lax.all_to_all(parcels, "space", split_axis=0, concat_axis=0, tiled=True)
    forward = [pltpu.VMEM((5, 5, CELLS, 128), BF16), pltpu.VMEM((9 * 128, 384), BF16)]
    pack = call(
        kernel_pack, shape((PACK, 64, CELLS), BF16), slab, halo, conv_one, scratch=forward
    )
    ones = call(
        functools.partial(kernel_back, pieces, rows_per),
        (shape((64, 864), BF16),) * 2 if shared else (shape((128, 864), F32),),
        place,
        slot,
        slab,
        halo,
        conv_one,
        conv_two,
        cot,
        spaces={0: pltpu.SMEM, 1: pltpu.SMEM},
        scratch=[pltpu.VMEM((2, 4, 128, CELLS), F32), *forward]
        + [pltpu.VMEM((384, 4 * CELLS), BF16)],
    )

    def left_of(height, *cots):
        moved = shape((2, 4, height, len(cots) * CELLS), BF16)
        return call(functools.partial(kernel_left, rows_per), moved, *cots)

    def latent_of(pack):
        return call(kernel_latent, shape((slabs, 2 * group, CELLS), BF16), pack, conv_two)

    def exchanged(parts):
        return lax.all_to_all(parts, "space", split_axis=0, concat_axis=0, tiled=True)

    latent_shape = shape((group, slabs, CELLS), BF16)

    if not shared:
        two = call(
            functools.partial(kernel_two, 1, rows_per),
            shape((256, 27 * 128), F32),
            pack,
            left_of(256, cot),
        )
        one, two = lax.psum((ones[0], two), "dp")
        one = lax.psum_scatter(one, "space", scatter_dimension=0, tiled=True)
        two = lax.psum_scatter(two, "space", scatter_dimension=0, tiled=True)
        return call(join, latent_shape, exchanged(latent_of(pack)))[None], one, two

    across = swap_ranks(pack, "dp", 2)
    beside = swap_ranks(first_of(pack, cot), "dp", 1)
    own, *cots = call(
        kernel_pieces,
        (shape((slabs, 2 * rows_per, CELLS), BF16),) * pieces,
        place,
        slot,
        cot,
        spaces={0: pltpu.SMEM, 1: pltpu.SMEM},
    )
    cots = [own] + [swap_ranks(piece, "dp", k) for k, piece in enumerate(cots, 1)]
    parts = latent_of(pack)
    one_block = shape((rows_per, WIDTH), BF16)
    kept, near_1, near_2, near_3, lent, own_far = call(
        functools.partial(kernel_two, samples, rows_per),
        (
            shape((rows_per, WIDTH), F32),
            one_block,
            one_block,
            one_block,
            shape((2, rows_per, WIDTH), BF16),
            shape((2, rows_per, WIDTH), F32),
        ),
        pack,
        beside,
        across,
        swap_ranks(first_of(across, *ones, *cots[1:], parts), "dp", 1),
        left_of(slabs * rows_per, *cots),
        ones[0],
        swap_ranks(ones[1], "dp", 1),
    )
    lent = swap_ranks(lent, "space", 1)
    far = call(kernel_far, (one_block, one_block), lent, own_far)
    others = [
        swap_ranks(block, "space", k)
        for k, block in ((1, near_1), (2, near_2), (3, near_3), (4, far[0]), (6, far[1]))
    ]
    got = exchanged(first_of(parts, *far))
    total = call(kernel_sum, one_block, kept, *others)
    totals = [swap_ranks(total, "dp", k) if k else total for k in range(pieces)]
    one, two, latent = call(
        functools.partial(kernel_final, pieces),
        (shape((16, 864), F32), shape((32, 27 * 128), F32), latent_shape),
        place,
        *totals,
        got,
        spaces={0: pltpu.SMEM},
    )
    return latent[None], one, two


def solution(mesh):
    placed = (P("dp", "space", None, None), P(), P(), P("dp", "space", None, None))
    return jax.shard_map(
        on_device,
        mesh=mesh,
        in_specs=placed,
        out_specs=(P("dp", "space", None, None), P("space", None), P("space", None)),
        check_vma=False,
    )
```

```python
import functools

import jax
import jax.numpy as jnp
from jax import lax
from jax.experimental import pallas as pl
from jax.experimental.pallas import tpu as pltpu
from jax.sharding import PartitionSpec as P

F32 = jnp.float32
BF16 = jnp.bfloat16
VMEM_LIMIT = 16 * 1024 * 1024

NJ, NK, CELLS = 16, 8, 128
ONE_AT, WIDTH = 3456, 4320
HIDDEN_AT, PACK = (0, 8), 16
TAP_PHASE = {0: (1, 1), 1: (0, 0), 2: (1, 0)}


def dot(a, b):
    return jnp.dot(a, b, preferred_element_type=F32)


def iota(shape, axis):
    return lax.broadcasted_iota(jnp.int32, shape, axis)


def one_hot(mask):
    return jnp.where(mask, 1.0, 0.0).astype(BF16)


def cell_order(shifted):
    width = CELLS * (4 if shifted else 1)
    row, col = iota((CELLS, width), 0), iota((CELLS, width), 1)
    v, cell = col // CELLS, col % CELLS
    to_j, to_k = cell % NJ + v // 2, cell // NJ + v % 2
    return one_hot((to_k < NK) & (row == to_j * NK + to_k))


def fill_picked(planes, picked):
    row, col = iota((80, 64), 0), iota((80, 64), 1)
    pick = one_hot(col == 4 * (row % NJ) + row // NJ - 1)
    for x, rows in enumerate(planes):
        value = dot(pick, rows).astype(BF16)
        for rho in range(5):
            for k in range(NK):
                picked[x, rho, k * NJ : (k + 1) * NJ] = value[
                    rho * NJ : (rho + 1) * NJ, k * 128 : (k + 1) * 128
                ]


def widen(w1, w_ext):
    for t in range(9):
        base, src = t * 128, t * 96
        zeros = jnp.zeros((128, 128), BF16)
        w_ext[base : base + 64, 0:128] = w1[src + 32 : src + 96, :]
        w_ext[base + 64 : base + 128, 0:128] = zeros[:64]
        w_ext[base : base + 32, 128:256] = zeros[:32]
        w_ext[base + 32 : base + 128, 128:256] = w1[src : src + 96, :]
        w_ext[base : base + 96, 256:384] = zeros[:96]
        w_ext[base + 96 : base + 128, 256:384] = w1[src : src + 32, :]


def fill_hidden(picked, i, w_ext, hidden, slope_t):
    for p in range(2):
        patches = [picked[2 * i + a, 2 * p + b] for a in range(3) for b in range(3)]
        full = dot(jnp.concatenate(patches, axis=1), w_ext[...])
        before = jnp.concatenate(
            [jnp.zeros((NJ, 128), F32), full[: CELLS - NJ, 256:384]], axis=0
        )
        for q, pre in enumerate((full[:, 0:128] + before, full[:, 128:256])):
            logistic = 1.0 / (1.0 + jnp.exp(-pre))
            if hidden is not None:
                hidden[2 * p + q] = (pre * logistic).astype(BF16)
            if slope_t is not None:
                slope = logistic * (1.0 + pre * (1.0 - logistic))
                slope_t[2 * p + q] = slope.T


def kernel_parcels(pieces, _, __, cot_hbm, snap, parcels, halo, cot, sems):
    last = pltpu.make_async_copy(snap.at[pl.ds(3, 1)], halo, sems.at[0])
    whole = pltpu.make_async_copy(cot_hbm, cot, sems.at[1])
    whole.start()
    last.start()
    group, slabs = cot.shape[:2]
    rows_per = group // pieces
    row, col = iota((group * slabs, group * slabs), 0), iota((group * slabs, group * slabs), 1)
    chosen = one_hot(col == row % group * slabs + row // group)
    whole.wait()
    flat = cot[...].astype(F32).reshape(-1, CELLS).astype(BF16)
    here = dot(chosen, flat).reshape(slabs, pieces, 1, rows_per, CELLS)
    next_ = jnp.concatenate([here[1:], jnp.zeros_like(here[:1])], axis=0)
    pair = jnp.concatenate([here, next_], axis=2)
    parcels[...] = pair.reshape(slabs, 2 * group, CELLS).astype(BF16)
    last.wait()


class Phases:
    def __init__(self, pack, i):
        self.pack, self.at = pack, HIDDEN_AT[i]

    def __setitem__(self, phase, value):
        at = self.at + 2 * phase
        self.pack[at : at + 2] = value.reshape(2, 64, 128)

    def __getitem__(self, phase):
        at = self.at + 2 * phase
        return self.pack[at : at + 2].reshape(CELLS, 128)


def kernel_pack(snap, halo, w1, pack, picked, w_ext):
    widen(w1, w_ext)
    fill_picked([halo[0], snap[0], snap[1], snap[2], snap[3]], picked)
    for i in range(2):
        fill_hidden(picked, i, w_ext, Phases(pack, i), None)


def kernel_pieces(place, slot, cot, *outs):
    height = outs[0].shape[1]
    for k, out in enumerate(outs):
        at = pl.multiple_of((place[0] ^ k) * height, height)
        for n in range(out.shape[0]):
            out[n] = cot[slot[0] ^ n, pl.ds(at, height), :]


def kernel_back(pieces, rows_per, place, slot, snap, halo, w1, w2, cot, *rest):
    *outs, slope_t, picked, w_ext, grad_t = rest
    widen(w1, w_ext)
    fill_picked([halo[0], snap[0], snap[1], snap[2], snap[3]], picked)
    for i in range(2):
        fill_hidden(picked, i, w_ext, None, slope_t.at[i])
    grad_one_share(pieces, rows_per, place, slot, w2, cot, outs, picked, slope_t, grad_t)


def grad_one_share(pieces, rows_per, place, slot, w2, cot, outs, picked, slope_t, grad_t):
    sources = cot.shape[0]
    moved = dot(cot[...].reshape(-1, CELLS), cell_order(True))
    moved = moved.reshape(sources * pieces, 2, rows_per, 4 * CELLS)
    planes = [moved[:, s].reshape(-1, 4 * CELLS).astype(BF16) for s in range(2)]
    for i in range(2):
        for p in range(2):
            for q in range(2):
                total = None
                for a in (1,) if i == 0 else (2, 0):
                    source = planes[1 if a == 0 else 0]
                    for b in (1,) if p == 0 else (2, 0):
                        for c in (1,) if q == 0 else (2, 0):
                            v = 2 * (b == 0) + (c == 0)
                            tap = 9 * a + 3 * b + c
                            term = dot(
                                w2[tap * 128 : (tap + 1) * 128, :],
                                source[:, v * CELLS : (v + 1) * CELLS],
                            )
                            total = term if total is None else total + term
                pre_t = total * slope_t[i, 2 * p + q]
                at = (2 * i + p) * CELLS
                grad_t[q * 128 : (q + 1) * 128, at : at + CELLS] = pre_t.astype(BF16)
                if q == 0:
                    ahead = pltpu.roll(pre_t, CELLS - NJ, axis=1)
                    ahead = jnp.where(iota((128, CELLS), 1) < CELLS - NJ, ahead, 0.0)
                    grad_t[256:384, at : at + CELLS] = ahead.astype(BF16)
    lane = iota((128, 128), 1)
    frames = []
    products = []
    for first in range(0, 9, 2):
        columns = []
        for t in range(first, min(first + 2, 9)):
            blocks = [picked[2 * i + t // 3, 2 * p + t % 3] for i in range(2) for p in range(2)]
            columns.append(jnp.concatenate(blocks, axis=0))
        both = dot(grad_t[...], jnp.concatenate(columns, axis=1))
        products += [both[:, n * 128 : (n + 1) * 128] for n in range(len(columns))]
    for full in products:
        side = jnp.where(lane < 64, full[0:128], full[256:384])
        side = jnp.where((lane < 64) | (lane >= 96), side, 0.0)
        own = jnp.where(lane < 32, 0.0, full[128:256])
        frames.append(own + pltpu.roll(side, 64, axis=1))
    if pieces == 1:
        for t in range(9):
            outs[0][:, t * 96 : (t + 1) * 96] = frames[t][:, 32:]
        return
    owned = 128 // sources
    share = owned // 2
    row, col = iota((128 // 2, 128), 0), iota((128 // 2, 128), 1)
    frames = [frame.astype(BF16) for frame in frames]
    halves = []
    for k in range(2):
        half = (place[0] ^ k) & 1
        halves.append(
            one_hot(col == (row // share ^ slot[0]) * owned + half * share + row % share)
        )
    chosen = jnp.concatenate(halves, axis=0)
    for first in range(0, 9, 2):
        value = dot(chosen, jnp.concatenate(frames[first : first + 2], axis=1))
        for t in range(first, min(first + 2, 9)):
            at = (t - first) * 128 + 32
            for k in range(2):
                part = value[k * 64 : (k + 1) * 64, at : at + 96]
                outs[k][:, t * 96 : (t + 1) * 96] = part.astype(BF16)


def kernel_latent(pack, w2, parts):
    owners = parts.shape[0]
    group = parts.shape[1] // 2
    row, col = iota((CELLS, CELLS), 0), iota((CELLS, CELLS), 1)
    back = one_hot((row // NJ == col % NK) & (row % NJ == col // NK))
    for part, taps_x in enumerate(((1, 2), (0,))):
        joined = {}
        for b in range(3):
            p, sj = TAP_PHASE[b]
            for c in range(3):
                q, sk = TAP_PHASE[c]
                for a in taps_x:
                    tap = 9 * a + 3 * b + c
                    hidden = Phases(pack, 0 if a == 1 else 1)[2 * p + q]
                    weights = w2[tap * 128 : (tap + 1) * 128, :]
                    joined.setdefault(2 * sj + sk, []).append((hidden, weights))
        totals = {
            v: dot(
                jnp.concatenate([hidden for hidden, _ in pairs], axis=1),
                jnp.concatenate([weights for _, weights in pairs], axis=0),
            )
            for v, pairs in joined.items()
        }
        zero = jnp.zeros((NJ, totals[0].shape[1]), F32)

        def later(value):
            return jnp.concatenate([zero, value[: CELLS - NJ]], axis=0)

        inner = totals[2] + later(totals[3])
        inner = jnp.where(iota(inner.shape, 0) % NJ == 0, 0.0, pltpu.roll(inner, 1, axis=0))
        rows = totals[0] + later(totals[1]) + inner
        value = dot(rows.T.astype(BF16), back).reshape(owners, group, CELLS)
        parts[:, part * group : (part + 1) * group] = value.astype(BF16)


def moved_rows(cots, rows_per, order):
    moved = []
    for cot in cots:
        value = dot(cot[...].reshape(-1, CELLS), order).reshape(-1, 2, rows_per, 4 * CELLS)
        moved.append([value[:, s].reshape(-1, 4 * CELLS).astype(BF16) for s in range(2)])
    return [
        [
            jnp.concatenate([m[s][:, v * CELLS : (v + 1) * CELLS] for m in moved], axis=1)
            for v in range(4)
        ]
        for s in range(2)
    ]


def kernel_left(rows_per, *refs):
    *cots, out = refs
    for s, values in enumerate(moved_rows(cots, rows_per, cell_order(True))):
        for v, value in enumerate(values):
            out[s, v] = value


def kernel_two(samples, rows_per, *refs):
    packs, left, refs = refs[:samples], refs[samples], refs[samples + 1 :]
    packed = samples > 1
    if packed:
        ones, outs = refs[:2], refs[2:]
    height = left.shape[2]
    for p in range(2):
        for q in range(2):
            right_0, right_1 = [
                jnp.concatenate([Phases(pack, i)[2 * p + q] for pack in packs], axis=0)
                for i in range(2)
            ]
            both = jnp.concatenate([right_0, right_1], axis=1)
            taps = [
                (b, c)
                for b in range(3)
                for c in range(3)
                if TAP_PHASE[b][0] == p and TAP_PHASE[c][0] == q
            ]
            shifts = [2 * TAP_PHASE[b][1] + TAP_PHASE[c][1] for b, c in taps]
            same = dot(jnp.concatenate([left[0, v] for v in shifts], axis=0), both)
            above = dot(jnp.concatenate([left[1, v] for v in shifts], axis=0), right_1)
            for n, (b, c) in enumerate(taps):
                rows = slice(n * height, (n + 1) * height)
                parts = (above[rows], same[rows, 0:128], same[rows, 128:256])
                for a, value in enumerate(parts):
                    to = (9 * a + 3 * b + c) * 128
                    if packed:
                        spread(value.reshape(-1, rows_per, 128), outs, to)
                    else:
                        refs[0][:, to : to + 128] = value
    if packed:
        total = ones[0][...].astype(F32) + ones[1][...].astype(F32)
        spread(total.reshape(-1, rows_per, WIDTH - ONE_AT), outs, ONE_AT)


def spread(value, outs, at):
    kept, near_1, near_2, near_3, lent, own_far = outs
    lanes = slice(at, at + value.shape[2])
    kept[:, lanes] = value[0]
    for n, near in enumerate((near_1, near_2, near_3), 1):
        near[:, lanes] = value[n].astype(BF16)
    for n in range(2):
        own_far[n, :, lanes] = value[4 + 2 * n]
        lent[n, :, lanes] = value[5 + 2 * n].astype(BF16)


def kernel_far(lent, own_far, *outs):
    for n, out in enumerate(outs):
        out[...] = (own_far[n] + lent[n].astype(F32)).astype(BF16)


def kernel_sum(kept, *refs):
    *others, total_out = refs
    total = kept[...]
    for other in others:
        total = total + other[...].astype(F32)
    total_out[...] = total.astype(BF16)


def join(got, latent):
    slabs, group = got.shape[0], got.shape[1] // 2
    next_ = got[:, group:].astype(F32)
    next_ = jnp.concatenate([jnp.zeros_like(next_[:1]), next_[:-1]], axis=0)
    cells = (got[:, :group].astype(F32) + next_).reshape(-1, CELLS).astype(BF16)
    height = slabs * group
    row, col = iota((height, height), 0), iota((height, height), 1)
    swap = one_hot((row // slabs == col % group) & (row % slabs == col // group))
    latent[...] = dot(swap, cells).reshape(group, slabs, CELLS).astype(BF16)


def kernel_final(pieces, place, *refs):
    parts, (got, one, two, latent) = refs[:pieces], refs[pieces:]
    join(got, latent)
    rows_per = parts[0].shape[0]
    for k in range(pieces):
        at = pl.multiple_of((place[0] ^ k) * rows_per, rows_per)
        two[pl.ds(at, rows_per), :] = parts[k][:, 0:ONE_AT].astype(F32)
    for k in range(2):
        at = pl.multiple_of(((place[0] ^ k) & 1) * rows_per, rows_per)
        shares = [parts[n][:, ONE_AT:WIDTH].astype(F32) for n in (k, k ^ 2)]
        one[pl.ds(at, rows_per), :] = shares[0] + shares[1]


def call(kernel, out_shape, *args, spaces=None, out_spaces=None, scratch=(), vmem=VMEM_LIMIT):
    spaces, out_spaces = spaces or {}, out_spaces or {}
    single = isinstance(out_shape, jax.ShapeDtypeStruct)

    def spec(n, of):
        return pl.BlockSpec(memory_space=of.get(n, pltpu.VMEM))

    moved = sum(x.size * x.dtype.itemsize for x in args)
    return pl.pallas_call(
        kernel,
        out_shape=out_shape,
        in_specs=[spec(n, spaces) for n in range(len(args))],
        out_specs=spec(0, {}) if single else [spec(n, out_spaces) for n in range(len(out_shape))],
        scratch_shapes=list(scratch),
        cost_estimate=pl.CostEstimate(flops=10**9, bytes_accessed=moved, transcendentals=0),
        compiler_params=pltpu.CompilerParams(vmem_limit_bytes=vmem),
    )(*args)


def shape(dims, dtype):
    return jax.ShapeDtypeStruct(dims, dtype)


def swap_ranks(block, axis, k):
    return lax.ppermute(block, axis, [(i, i ^ k) for i in range(lax.axis_size(axis))])


def first_of(value, *others):
    return lax.optimization_barrier((value, *others))[0]


def from_below(block, axis):
    return lax.ppermute(block, axis, [(i - 1, i) for i in range(1, lax.axis_size(axis))])


def on_device(snapshot, conv_one, conv_two, cotangent):
    slabs, samples = lax.axis_size("space"), lax.axis_size("dp")
    group = cotangent.shape[1]
    shared = samples == 4 and slabs == 8
    pieces = samples if shared else 1
    rows_per = group // pieces

    slab = snapshot[0]
    place, slot = [
        lax.axis_index(axis).astype(jnp.int32).reshape(1) for axis in ("dp", "space")
    ]
    parcels, last = call(
        functools.partial(kernel_parcels, pieces),
        (shape((slabs, 2 * group, CELLS), BF16), shape((1,) + slab.shape[1:], BF16)),
        place,
        slot,
        cotangent[0],
        slab,
        spaces={0: pltpu.SMEM, 1: pltpu.SMEM, 2: pltpu.HBM, 3: pltpu.HBM},
        scratch=[pltpu.VMEM((group, slabs, CELLS), BF16), pltpu.SemaphoreType.DMA((2,))],
        vmem=62 * 1024 * 1024,
    )
    halo = from_below(last, "space")
    cot = lax.all_to_all(parcels, "space", split_axis=0, concat_axis=0, tiled=True)
    forward = [pltpu.VMEM((5, 5, CELLS, 128), BF16), pltpu.VMEM((9 * 128, 384), BF16)]
    pack = call(
        kernel_pack, shape((PACK, 64, CELLS), BF16), slab, halo, conv_one, scratch=forward
    )
    ones = call(
        functools.partial(kernel_back, pieces, rows_per),
        (shape((64, 864), BF16),) * 2 if shared else (shape((128, 864), F32),),
        place,
        slot,
        slab,
        halo,
        conv_one,
        conv_two,
        cot,
        spaces={0: pltpu.SMEM, 1: pltpu.SMEM},
        scratch=[pltpu.VMEM((2, 4, 128, CELLS), F32), *forward]
        + [pltpu.VMEM((384, 4 * CELLS), BF16)],
    )

    def left_of(height, *cots):
        moved = shape((2, 4, height, len(cots) * CELLS), BF16)
        return call(functools.partial(kernel_left, rows_per), moved, *cots)

    def latent_of(pack):
        return call(kernel_latent, shape((slabs, 2 * group, CELLS), BF16), pack, conv_two)

    def exchanged(parts):
        return lax.all_to_all(parts, "space", split_axis=0, concat_axis=0, tiled=True)

    latent_shape = shape((group, slabs, CELLS), BF16)

    if not shared:
        two = call(
            functools.partial(kernel_two, 1, rows_per),
            shape((256, 27 * 128), F32),
            pack,
            left_of(256, cot),
        )
        one, two = lax.psum((ones[0], two), "dp")
        one = lax.psum_scatter(one, "space", scatter_dimension=0, tiled=True)
        two = lax.psum_scatter(two, "space", scatter_dimension=0, tiled=True)
        return call(join, latent_shape, exchanged(latent_of(pack)))[None], one, two

    across = swap_ranks(pack, "dp", 2)
    beside = swap_ranks(first_of(pack, cot), "dp", 1)
    own, *cots = call(
        kernel_pieces,
        (shape((slabs, 2 * rows_per, CELLS), BF16),) * pieces,
        place,
        slot,
        cot,
        spaces={0: pltpu.SMEM, 1: pltpu.SMEM},
    )
    cots = [own] + [swap_ranks(piece, "dp", k) for k, piece in enumerate(cots, 1)]
    parts = latent_of(pack)
    one_block = shape((rows_per, WIDTH), BF16)
    kept, near_1, near_2, near_3, lent, own_far = call(
        functools.partial(kernel_two, samples, rows_per),
        (
            shape((rows_per, WIDTH), F32),
            one_block,
            one_block,
            one_block,
            shape((2, rows_per, WIDTH), BF16),
            shape((2, rows_per, WIDTH), F32),
        ),
        pack,
        beside,
        across,
        swap_ranks(first_of(across, *ones, *cots[1:], parts), "dp", 1),
        left_of(slabs * rows_per, *cots),
        ones[0],
        swap_ranks(ones[1], "dp", 1),
    )
    lent = swap_ranks(lent, "space", 1)
    far = call(kernel_far, (one_block, one_block), lent, own_far)
    others = [
        swap_ranks(block, "space", k)
        for k, block in ((1, near_1), (2, near_2), (3, near_3), (4, far[0]), (6, far[1]))
    ]
    got = exchanged(first_of(parts, *far))
    total = call(kernel_sum, one_block, kept, *others)
    totals = [swap_ranks(total, "dp", k) if k else total for k in range(pieces)]
    one, two, latent = call(
        functools.partial(kernel_final, pieces),
        (shape((16, 864), F32), shape((32, 27 * 128), F32), latent_shape),
        place,
        *totals,
        got,
        spaces={0: pltpu.SMEM},
    )
    return latent[None], one, two


def solution(mesh):
    placed = (P("dp", "space", None, None), P(), P(), P("dp", "space", None, None))
    return jax.shard_map(
        on_device,
        mesh=mesh,
        in_specs=placed,
        out_specs=(P("dp", "space", None, None), P("space", None), P("space", None)),
        check_vma=False,
    )
```

```python
import functools

import jax
import jax.numpy as jnp
from jax import lax
from jax.experimental import pallas as pl
from jax.experimental.pallas import tpu as pltpu
from jax.sharding import PartitionSpec as P

F32 = jnp.float32
BF16 = jnp.bfloat16
VMEM_LIMIT = 16 * 1024 * 1024

NJ, NK, CELLS = 16, 8, 128
ONE_AT, WIDTH = 3456, 4320
HIDDEN_AT, PACK = (0, 8), 16
TAP_PHASE = {0: (1, 1), 1: (0, 0), 2: (1, 0)}


def dot(a, b):
    return jnp.dot(a, b, preferred_element_type=F32)


def iota(shape, axis):
    return lax.broadcasted_iota(jnp.int32, shape, axis)


def one_hot(mask):
    return jnp.where(mask, 1.0, 0.0).astype(BF16)


def cell_order(shifted):
    width = CELLS * (4 if shifted else 1)
    row, col = iota((CELLS, width), 0), iota((CELLS, width), 1)
    v, cell = col // CELLS, col % CELLS
    to_j, to_k = cell % NJ + v // 2, cell // NJ + v % 2
    return one_hot((to_k < NK) & (row == to_j * NK + to_k))


def fill_picked(planes, picked):
    row, col = iota((80, 64), 0), iota((80, 64), 1)
    pick = one_hot(col == 4 * (row % NJ) + row // NJ - 1)
    for x, rows in enumerate(planes):
        value = dot(pick, rows).astype(BF16)
        for rho in range(5):
            for k in range(NK):
                picked[x, rho, k * NJ : (k + 1) * NJ] = value[
                    rho * NJ : (rho + 1) * NJ, k * 128 : (k + 1) * 128
                ]


def widen(w1, w_ext):
    for t in range(9):
        base, src = t * 128, t * 96
        zeros = jnp.zeros((128, 128), BF16)
        w_ext[base : base + 64, 0:128] = w1[src + 32 : src + 96, :]
        w_ext[base + 64 : base + 128, 0:128] = zeros[:64]
        w_ext[base : base + 32, 128:256] = zeros[:32]
        w_ext[base + 32 : base + 128, 128:256] = w1[src : src + 96, :]
        w_ext[base : base + 96, 256:384] = zeros[:96]
        w_ext[base + 96 : base + 128, 256:384] = w1[src : src + 32, :]


def fill_hidden(picked, i, w_ext, hidden, slope_t):
    rows = []
    for p in range(2):
        patches = [picked[2 * i + a, 2 * p + b] for a in range(3) for b in range(3)]
        rows.append(jnp.concatenate(patches, axis=1))
    product = dot(jnp.concatenate(rows, axis=0), w_ext[...])
    for p in range(2):
        full = product[p * CELLS : (p + 1) * CELLS]
        before = jnp.concatenate(
            [jnp.zeros((NJ, 128), F32), full[: CELLS - NJ, 256:384]], axis=0
        )
        for q, pre in enumerate((full[:, 0:128] + before, full[:, 128:256])):
            logistic = 1.0 / (1.0 + jnp.exp(-pre))
            if hidden is not None:
                hidden[2 * p + q] = (pre * logistic).astype(BF16)
            if slope_t is not None:
                slope = logistic * (1.0 + pre * (1.0 - logistic))
                slope_t[2 * p + q] = slope.T


def kernel_parcels(pieces, _, __, cot_hbm, snap, parcels, halo, cot, sems):
    last = pltpu.make_async_copy(snap.at[pl.ds(3, 1)], halo, sems.at[0])
    whole = pltpu.make_async_copy(cot_hbm, cot, sems.at[1])
    whole.start()
    last.start()
    group, slabs = cot.shape[:2]
    rows_per = group // pieces
    row, col = iota((2 * group * slabs, group * slabs), 0), iota((2 * group * slabs, group * slabs), 1)
    slab = row // (2 * group) + row // rows_per % 2
    channel = row % (2 * group) // (2 * rows_per) * rows_per + row % rows_per
    chosen = one_hot((slab < slabs) & (col == channel * slabs + slab))
    whole.wait()
    flat = cot[...].astype(F32).reshape(-1, CELLS).astype(BF16)
    parcels[...] = dot(chosen, flat).astype(BF16).reshape(slabs, 2 * group, CELLS)
    last.wait()


class Phases:
    def __init__(self, pack, i):
        self.pack, self.at = pack, HIDDEN_AT[i]

    def __setitem__(self, phase, value):
        at = self.at + 2 * phase
        self.pack[at : at + 2] = value.reshape(2, 64, 128)

    def __getitem__(self, phase):
        at = self.at + 2 * phase
        return self.pack[at : at + 2].reshape(CELLS, 128)


def kernel_pack(snap, halo, w1, pack, picked, w_ext):
    widen(w1, w_ext)
    fill_picked([halo[0], snap[0], snap[1], snap[2], snap[3]], picked)
    for i in range(2):
        fill_hidden(picked, i, w_ext, Phases(pack, i), None)


def kernel_pieces(place, slot, cot, *outs):
    height = outs[0].shape[1]
    for k, out in enumerate(outs):
        at = pl.multiple_of((place[0] ^ k) * height, height)
        for n in range(out.shape[0]):
            out[n] = cot[slot[0] ^ n, pl.ds(at, height), :]


def kernel_back(pieces, rows_per, place, slot, snap, halo, w1, w2, cot, *rest):
    *outs, slope_t, picked, w_ext, grad_t = rest
    widen(w1, w_ext)
    fill_picked([halo[0], snap[0], snap[1], snap[2], snap[3]], picked)
    for i in range(2):
        fill_hidden(picked, i, w_ext, None, slope_t.at[i])
    grad_one_share(pieces, rows_per, place, slot, w2, cot, outs, picked, slope_t, grad_t)


def grad_one_share(pieces, rows_per, place, slot, w2, cot, outs, picked, slope_t, grad_t):
    sources = cot.shape[0]
    moved = dot(cot[...].reshape(-1, CELLS), cell_order(True))
    moved = moved.reshape(sources * pieces, 2, rows_per, 4 * CELLS)
    planes = [moved[:, s].reshape(-1, 4 * CELLS).astype(BF16) for s in range(2)]
    for i in range(2):
        for p in range(2):
            for q in range(2):
                total = None
                for a in (1,) if i == 0 else (2, 0):
                    source = planes[1 if a == 0 else 0]
                    for b in (1,) if p == 0 else (2, 0):
                        for c in (1,) if q == 0 else (2, 0):
                            v = 2 * (b == 0) + (c == 0)
                            tap = 9 * a + 3 * b + c
                            term = dot(
                                w2[tap * 128 : (tap + 1) * 128, :],
                                source[:, v * CELLS : (v + 1) * CELLS],
                            )
                            total = term if total is None else total + term
                pre_t = total * slope_t[i, 2 * p + q]
                at = (2 * i + p) * CELLS
                grad_t[q * 128 : (q + 1) * 128, at : at + CELLS] = pre_t.astype(BF16)
                if q == 0:
                    ahead = pltpu.roll(pre_t, CELLS - NJ, axis=1)
                    ahead = jnp.where(iota((128, CELLS), 1) < CELLS - NJ, ahead, 0.0)
                    grad_t[256:384, at : at + CELLS] = ahead.astype(BF16)
    lane = iota((128, 128), 1)
    frames = []
    products = []
    for first in range(0, 9, 2):
        columns = []
        for t in range(first, min(first + 2, 9)):
            blocks = [picked[2 * i + t // 3, 2 * p + t % 3] for i in range(2) for p in range(2)]
            columns.append(jnp.concatenate(blocks, axis=0))
        both = dot(grad_t[...], jnp.concatenate(columns, axis=1))
        products += [both[:, n * 128 : (n + 1) * 128] for n in range(len(columns))]
    for full in products:
        side = jnp.where(lane < 64, full[0:128], full[256:384])
        frames.append(full[128:256] + pltpu.roll(side, 64, axis=1))
    if pieces == 1:
        for t in range(9):
            outs[0][:, t * 96 : (t + 1) * 96] = frames[t][:, 32:]
        return
    owned = 128 // sources
    share = owned // 2
    row, col = iota((128 // 2, 128), 0), iota((128 // 2, 128), 1)
    frames = [frame.astype(BF16) for frame in frames]
    halves = []
    for k in range(2):
        half = (place[0] ^ k) & 1
        halves.append(
            one_hot(col == (row // share ^ slot[0]) * owned + half * share + row % share)
        )
    chosen = jnp.concatenate(halves, axis=0)
    for first in range(0, 9, 2):
        value = dot(chosen, jnp.concatenate(frames[first : first + 2], axis=1))
        for t in range(first, min(first + 2, 9)):
            at = (t - first) * 128 + 32
            for k in range(2):
                part = value[k * 64 : (k + 1) * 64, at : at + 96]
                outs[k][:, t * 96 : (t + 1) * 96] = part.astype(BF16)


def kernel_latent(pack, w2, parts):
    owners = parts.shape[0]
    group = parts.shape[1] // 2
    row, col = iota((CELLS, CELLS), 0), iota((CELLS, CELLS), 1)
    back = one_hot((row // NJ == col % NK) & (row % NJ == col // NK))
    for part, taps_x in enumerate(((1, 2), (0,))):
        joined = {}
        for b in range(3):
            p, sj = TAP_PHASE[b]
            for c in range(3):
                q, sk = TAP_PHASE[c]
                for a in taps_x:
                    tap = 9 * a + 3 * b + c
                    hidden = Phases(pack, 0 if a == 1 else 1)[2 * p + q]
                    weights = w2[tap * 128 : (tap + 1) * 128, :]
                    joined.setdefault(2 * sj + sk, []).append((hidden, weights))
        totals = {
            v: dot(
                jnp.concatenate([hidden for hidden, _ in pairs], axis=1),
                jnp.concatenate([weights for _, weights in pairs], axis=0),
            )
            for v, pairs in joined.items()
        }
        zero = jnp.zeros((NJ, totals[0].shape[1]), F32)

        def later(value):
            return jnp.concatenate([zero, value[: CELLS - NJ]], axis=0)

        inner = totals[2] + later(totals[3])
        inner = jnp.where(iota(inner.shape, 0) % NJ == 0, 0.0, pltpu.roll(inner, 1, axis=0))
        rows = totals[0] + later(totals[1]) + inner
        value = dot(rows.T.astype(BF16), back).reshape(owners, group, CELLS)
        parts[:, part * group : (part + 1) * group] = value.astype(BF16)


def moved_rows(cots, rows_per, order):
    moved = []
    for cot in cots:
        value = dot(cot[...].reshape(-1, CELLS), order).reshape(-1, 2, rows_per, 4 * CELLS)
        moved.append([value[:, s].reshape(-1, 4 * CELLS).astype(BF16) for s in range(2)])
    return [
        [
            jnp.concatenate([m[s][:, v * CELLS : (v + 1) * CELLS] for m in moved], axis=1)
            for v in range(4)
        ]
        for s in range(2)
    ]


def kernel_left(rows_per, *refs):
    *cots, out = refs
    for s, values in enumerate(moved_rows(cots, rows_per, cell_order(True))):
        for v, value in enumerate(values):
            out[s, v] = value


def kernel_two(samples, rows_per, *refs):
    packs, left, refs = refs[:samples], refs[samples], refs[samples + 1 :]
    packed = samples > 1
    if packed:
        ones, outs = refs[:2], refs[2:]
    height = left.shape[2]
    for p in range(2):
        for q in range(2):
            right_0, right_1 = [
                jnp.concatenate([Phases(pack, i)[2 * p + q] for pack in packs], axis=0)
                for i in range(2)
            ]
            both = jnp.concatenate([right_0, right_1], axis=1)
            taps = [
                (b, c)
                for b in range(3)
                for c in range(3)
                if TAP_PHASE[b][0] == p and TAP_PHASE[c][0] == q
            ]
            shifts = [2 * TAP_PHASE[b][1] + TAP_PHASE[c][1] for b, c in taps]
            same = dot(jnp.concatenate([left[0, v] for v in shifts], axis=0), both)
            above = dot(jnp.concatenate([left[1, v] for v in shifts], axis=0), right_1)
            for n, (b, c) in enumerate(taps):
                rows = slice(n * height, (n + 1) * height)
                parts = (above[rows], same[rows, 0:128], same[rows, 128:256])
                for a, value in enumerate(parts):
                    to = (9 * a + 3 * b + c) * 128
                    if packed:
                        spread(value.reshape(-1, rows_per, 128), outs, to)
                    else:
                        refs[0][:, to : to + 128] = value
    if packed:
        total = ones[0][...].astype(F32) + ones[1][...].astype(F32)
        spread(total.reshape(-1, rows_per, WIDTH - ONE_AT), outs, ONE_AT)


def spread(value, outs, at):
    kept, near_1, near_2, near_3, lent, own_far = outs
    lanes = slice(at, at + value.shape[2])
    kept[:, lanes] = value[0]
    for n, near in enumerate((near_1, near_2, near_3), 1):
        near[:, lanes] = value[n].astype(BF16)
    for n in range(2):
        own_far[n, :, lanes] = value[4 + 2 * n]
        lent[n, :, lanes] = value[5 + 2 * n].astype(BF16)


def kernel_far(lent, own_far, *outs):
    for n, out in enumerate(outs):
        out[...] = (own_far[n] + lent[n].astype(F32)).astype(BF16)


def kernel_sum(kept, *refs):
    *others, total_out = refs
    total = kept[...]
    for other in others:
        total = total + other[...].astype(F32)
    total_out[...] = total.astype(BF16)


def join(got, latent):
    slabs, group = got.shape[0], got.shape[1] // 2
    next_ = got[:, group:].astype(F32)
    next_ = jnp.concatenate([jnp.zeros_like(next_[:1]), next_[:-1]], axis=0)
    cells = (got[:, :group].astype(F32) + next_).reshape(-1, CELLS).astype(BF16)
    height = slabs * group
    row, col = iota((height, height), 0), iota((height, height), 1)
    swap = one_hot((row // slabs == col % group) & (row % slabs == col // group))
    latent[...] = dot(swap, cells).reshape(group, slabs, CELLS).astype(BF16)


def kernel_final(pieces, place, *refs):
    parts, (got, one, two, latent) = refs[:pieces], refs[pieces:]
    join(got, latent)
    rows_per = parts[0].shape[0]
    for k in range(pieces):
        at = pl.multiple_of((place[0] ^ k) * rows_per, rows_per)
        two[pl.ds(at, rows_per), :] = parts[k][:, 0:ONE_AT].astype(F32)
    for k in range(2):
        at = pl.multiple_of(((place[0] ^ k) & 1) * rows_per, rows_per)
        shares = [parts[n][:, ONE_AT:WIDTH].astype(F32) for n in (k, k ^ 2)]
        one[pl.ds(at, rows_per), :] = shares[0] + shares[1]


def call(kernel, out_shape, *args, spaces=None, out_spaces=None, scratch=(), vmem=VMEM_LIMIT):
    spaces, out_spaces = spaces or {}, out_spaces or {}
    single = isinstance(out_shape, jax.ShapeDtypeStruct)

    def spec(n, of):
        return pl.BlockSpec(memory_space=of.get(n, pltpu.VMEM))

    moved = sum(x.size * x.dtype.itemsize for x in args)
    return pl.pallas_call(
        kernel,
        out_shape=out_shape,
        in_specs=[spec(n, spaces) for n in range(len(args))],
        out_specs=spec(0, {}) if single else [spec(n, out_spaces) for n in range(len(out_shape))],
        scratch_shapes=list(scratch),
        cost_estimate=pl.CostEstimate(flops=10**9, bytes_accessed=moved, transcendentals=0),
        compiler_params=pltpu.CompilerParams(vmem_limit_bytes=vmem),
    )(*args)


def shape(dims, dtype):
    return jax.ShapeDtypeStruct(dims, dtype)


def swap_ranks(block, axis, k):
    return lax.ppermute(block, axis, [(i, i ^ k) for i in range(lax.axis_size(axis))])


def first_of(value, *others):
    return lax.optimization_barrier((value, *others))[0]


def from_below(block, axis):
    return lax.ppermute(block, axis, [(i - 1, i) for i in range(1, lax.axis_size(axis))])


def on_device(snapshot, conv_one, conv_two, cotangent):
    slabs, samples = lax.axis_size("space"), lax.axis_size("dp")
    group = cotangent.shape[1]
    shared = samples == 4 and slabs == 8
    pieces = samples if shared else 1
    rows_per = group // pieces

    slab = snapshot[0]
    place, slot = [
        lax.axis_index(axis).astype(jnp.int32).reshape(1) for axis in ("dp", "space")
    ]
    parcels, last = call(
        functools.partial(kernel_parcels, pieces),
        (shape((slabs, 2 * group, CELLS), BF16), shape((1,) + slab.shape[1:], BF16)),
        place,
        slot,
        cotangent[0],
        slab,
        spaces={0: pltpu.SMEM, 1: pltpu.SMEM, 2: pltpu.HBM, 3: pltpu.HBM},
        scratch=[pltpu.VMEM((group, slabs, CELLS), BF16), pltpu.SemaphoreType.DMA((2,))],
        vmem=60 * 1024 * 1024,
    )
    halo = from_below(last, "space")
    cot = lax.all_to_all(parcels, "space", split_axis=0, concat_axis=0, tiled=True)
    forward = [pltpu.VMEM((5, 5, CELLS, 128), BF16), pltpu.VMEM((9 * 128, 384), BF16)]
    pack = call(
        kernel_pack, shape((PACK, 64, CELLS), BF16), slab, halo, conv_one, scratch=forward
    )
    ones = call(
        functools.partial(kernel_back, pieces, rows_per),
        (shape((64, 864), BF16),) * 2 if shared else (shape((128, 864), F32),),
        place,
        slot,
        slab,
        halo,
        conv_one,
        conv_two,
        cot,
        spaces={0: pltpu.SMEM, 1: pltpu.SMEM},
        scratch=[pltpu.VMEM((2, 4, 128, CELLS), F32), *forward]
        + [pltpu.VMEM((384, 4 * CELLS), BF16)],
    )

    def left_of(height, *cots):
        moved = shape((2, 4, height, len(cots) * CELLS), BF16)
        return call(functools.partial(kernel_left, rows_per), moved, *cots)

    def latent_of(pack):
        return call(kernel_latent, shape((slabs, 2 * group, CELLS), BF16), pack, conv_two)

    def exchanged(parts):
        return lax.all_to_all(parts, "space", split_axis=0, concat_axis=0, tiled=True)

    latent_shape = shape((group, slabs, CELLS), BF16)

    if not shared:
        two = call(
            functools.partial(kernel_two, 1, rows_per),
            shape((256, 27 * 128), F32),
            pack,
            left_of(256, cot),
        )
        one, two = lax.psum((ones[0], two), "dp")
        one = lax.psum_scatter(one, "space", scatter_dimension=0, tiled=True)
        two = lax.psum_scatter(two, "space", scatter_dimension=0, tiled=True)
        return call(join, latent_shape, exchanged(latent_of(pack)))[None], one, two

    across = swap_ranks(pack, "dp", 2)
    beside = swap_ranks(first_of(pack, cot), "dp", 1)
    own, *cots = call(
        kernel_pieces,
        (shape((slabs, 2 * rows_per, CELLS), BF16),) * pieces,
        place,
        slot,
        cot,
        spaces={0: pltpu.SMEM, 1: pltpu.SMEM},
    )
    cots = [own] + [swap_ranks(piece, "dp", k) for k, piece in enumerate(cots, 1)]
    parts = latent_of(pack)
    one_block = shape((rows_per, WIDTH), BF16)
    kept, near_1, near_2, near_3, lent, own_far = call(
        functools.partial(kernel_two, samples, rows_per),
        (
            shape((rows_per, WIDTH), F32),
            one_block,
            one_block,
            one_block,
            shape((2, rows_per, WIDTH), BF16),
            shape((2, rows_per, WIDTH), F32),
        ),
        pack,
        beside,
        across,
        swap_ranks(first_of(across, *ones, *cots[1:], parts), "dp", 1),
        left_of(slabs * rows_per, *cots),
        ones[0],
        swap_ranks(ones[1], "dp", 1),
    )
    lent = swap_ranks(lent, "space", 1)
    far = call(kernel_far, (one_block, one_block), lent, own_far)
    others = [
        swap_ranks(block, "space", k)
        for k, block in ((1, near_1), (2, near_2), (3, near_3), (4, far[0]), (6, far[1]))
    ]
    got = exchanged(first_of(parts, *far))
    total = call(kernel_sum, one_block, kept, *others)
    totals = [swap_ranks(total, "dp", k) if k else total for k in range(pieces)]
    one, two, latent = call(
        functools.partial(kernel_final, pieces),
        (shape((16, 864), F32), shape((32, 27 * 128), F32), latent_shape),
        place,
        *totals,
        got,
        spaces={0: pltpu.SMEM},
    )
    return latent[None], one, two


def solution(mesh):
    placed = (P("dp", "space", None, None), P(), P(), P("dp", "space", None, None))
    return jax.shard_map(
        on_device,
        mesh=mesh,
        in_specs=placed,
        out_specs=(P("dp", "space", None, None), P("space", None), P("space", None)),
        check_vma=False,
    )
```

```python
import functools

import jax
import jax.numpy as jnp
from jax import lax
from jax.experimental import pallas as pl
from jax.experimental.pallas import tpu as pltpu
from jax.sharding import PartitionSpec as P

F32 = jnp.float32
BF16 = jnp.bfloat16
VMEM_LIMIT = 16 * 1024 * 1024

NJ, NK, CELLS = 16, 8, 128
ONE_AT, WIDTH = 3456, 4320
HIDDEN_AT, PACK = (0, 8), 16
TAP_PHASE = {0: (1, 1), 1: (0, 0), 2: (1, 0)}


def dot(a, b):
    return jnp.dot(a, b, preferred_element_type=F32)


def iota(shape, axis):
    return lax.broadcasted_iota(jnp.int32, shape, axis)


def one_hot(mask):
    return jnp.where(mask, 1.0, 0.0).astype(BF16)


def cell_order(shifted):
    width = CELLS * (4 if shifted else 1)
    row, col = iota((CELLS, width), 0), iota((CELLS, width), 1)
    v, cell = col // CELLS, col % CELLS
    to_j, to_k = cell % NJ + v // 2, cell // NJ + v % 2
    return one_hot((to_k < NK) & (row == to_j * NK + to_k))


def fill_picked(planes, picked):
    row, col = iota((80, 64), 0), iota((80, 64), 1)
    pick = one_hot(col == 4 * (row % NJ) + row // NJ - 1)
    for x, rows in enumerate(planes):
        value = dot(pick, rows).astype(BF16)
        for rho in range(5):
            for k in range(NK):
                picked[x, rho, k * NJ : (k + 1) * NJ] = value[
                    rho * NJ : (rho + 1) * NJ, k * 128 : (k + 1) * 128
                ]


def widen(w1, w_ext):
    for t in range(9):
        base, src = t * 128, t * 96
        zeros = jnp.zeros((128, 128), BF16)
        w_ext[base : base + 64, 0:128] = w1[src + 32 : src + 96, :]
        w_ext[base + 64 : base + 128, 0:128] = zeros[:64]
        w_ext[base : base + 32, 128:256] = zeros[:32]
        w_ext[base + 32 : base + 128, 128:256] = w1[src : src + 96, :]
        w_ext[base : base + 96, 256:384] = zeros[:96]
        w_ext[base + 96 : base + 128, 256:384] = w1[src : src + 32, :]


def fill_hidden(picked, i, w_ext, hidden, slope_t):
    rows = []
    for p in range(2):
        patches = [picked[2 * i + a, 2 * p + b] for a in range(3) for b in range(3)]
        rows.append(jnp.concatenate(patches, axis=1))
    product = dot(jnp.concatenate(rows, axis=0), w_ext[...])
    for p in range(2):
        full = product[p * CELLS : (p + 1) * CELLS]
        before = jnp.concatenate(
            [jnp.zeros((NJ, 128), F32), full[: CELLS - NJ, 256:384]], axis=0
        )
        for q, pre in enumerate((full[:, 0:128] + before, full[:, 128:256])):
            logistic = 1.0 / (1.0 + jnp.exp(-pre))
            if hidden is not None:
                hidden[2 * p + q] = (pre * logistic).astype(BF16)
            if slope_t is not None:
                slope = logistic * (1.0 + pre * (1.0 - logistic))
                slope_t[2 * p + q] = slope.T


def kernel_parcels(pieces, _, __, cot_hbm, snap, parcels, halo, cot, sems):
    last = pltpu.make_async_copy(snap.at[pl.ds(3, 1)], halo, sems.at[0])
    whole = pltpu.make_async_copy(cot_hbm, cot, sems.at[1])
    whole.start()
    last.start()
    group, slabs = cot.shape[:2]
    rows_per = group // pieces
    row, col = iota((group * slabs, group * slabs), 0), iota((group * slabs, group * slabs), 1)
    chosen = one_hot(col == row % group * slabs + row // group)
    whole.wait()
    flat = cot[...].astype(F32).reshape(-1, CELLS).astype(BF16)
    here = dot(chosen, flat).reshape(slabs, pieces, 1, rows_per, CELLS)
    next_ = jnp.concatenate([here[1:], jnp.zeros_like(here[:1])], axis=0)
    pair = jnp.concatenate([here, next_], axis=2)
    parcels[...] = pair.reshape(slabs, 2 * group, CELLS).astype(BF16)
    last.wait()


class Phases:
    def __init__(self, pack, i):
        self.pack, self.at = pack, HIDDEN_AT[i]

    def __setitem__(self, phase, value):
        at = self.at + 2 * phase
        self.pack[at : at + 2] = value.reshape(2, 64, 128)

    def __getitem__(self, phase):
        at = self.at + 2 * phase
        return self.pack[at : at + 2].reshape(CELLS, 128)


def kernel_pack(snap, halo, w1, pack, picked, w_ext):
    widen(w1, w_ext)
    fill_picked([halo[0], snap[0], snap[1], snap[2], snap[3]], picked)
    for i in range(2):
        fill_hidden(picked, i, w_ext, Phases(pack, i), None)


def kernel_pieces(place, slot, cot, *outs):
    height = outs[0].shape[1]
    for k, out in enumerate(outs):
        at = pl.multiple_of((place[0] ^ k) * height, height)
        for n in range(out.shape[0]):
            out[n] = cot[slot[0] ^ n, pl.ds(at, height), :]


def kernel_back(pieces, rows_per, place, slot, snap, halo, w1, w2, cot, *rest):
    *outs, slope_t, picked, w_ext, grad_t = rest
    widen(w1, w_ext)
    fill_picked([halo[0], snap[0], snap[1], snap[2], snap[3]], picked)
    for i in range(2):
        fill_hidden(picked, i, w_ext, None, slope_t.at[i])
    grad_one_share(pieces, rows_per, place, slot, w2, cot, outs, picked, slope_t, grad_t)


def grad_one_share(pieces, rows_per, place, slot, w2, cot, outs, picked, slope_t, grad_t):
    sources = cot.shape[0]
    moved = dot(cot[...].reshape(-1, CELLS), cell_order(True))
    moved = moved.reshape(sources * pieces, 2, rows_per, 4 * CELLS)
    planes = [moved[:, s].reshape(-1, 4 * CELLS).astype(BF16) for s in range(2)]
    for i in range(2):
        for p in range(2):
            for q in range(2):
                total = None
                for a in (1,) if i == 0 else (2, 0):
                    source = planes[1 if a == 0 else 0]
                    for b in (1,) if p == 0 else (2, 0):
                        for c in (1,) if q == 0 else (2, 0):
                            v = 2 * (b == 0) + (c == 0)
                            tap = 9 * a + 3 * b + c
                            term = dot(
                                w2[tap * 128 : (tap + 1) * 128, :],
                                source[:, v * CELLS : (v + 1) * CELLS],
                            )
                            total = term if total is None else total + term
                pre_t = total * slope_t[i, 2 * p + q]
                at = (2 * i + p) * CELLS
                grad_t[q * 128 : (q + 1) * 128, at : at + CELLS] = pre_t.astype(BF16)
                if q == 0:
                    ahead = pltpu.roll(pre_t, CELLS - NJ, axis=1)
                    ahead = jnp.where(iota((128, CELLS), 1) < CELLS - NJ, ahead, 0.0)
                    grad_t[256:384, at : at + CELLS] = ahead.astype(BF16)
    lane = iota((128, 128), 1)
    frames = []
    products = []
    for first in range(0, 9, 2):
        columns = []
        for t in range(first, min(first + 2, 9)):
            blocks = [picked[2 * i + t // 3, 2 * p + t % 3] for i in range(2) for p in range(2)]
            columns.append(jnp.concatenate(blocks, axis=0))
        both = dot(grad_t[...], jnp.concatenate(columns, axis=1))
        products += [both[:, n * 128 : (n + 1) * 128] for n in range(len(columns))]
    for full in products:
        side = jnp.where(lane < 64, full[0:128], full[256:384])
        frames.append(full[128:256] + pltpu.roll(side, 64, axis=1))
    if pieces == 1:
        for t in range(9):
            outs[0][:, t * 96 : (t + 1) * 96] = frames[t][:, 32:]
        return
    owned = 128 // sources
    share = owned // 2
    row, col = iota((128 // 2, 128), 0), iota((128 // 2, 128), 1)
    frames = [frame.astype(BF16) for frame in frames]
    halves = []
    for k in range(2):
        half = (place[0] ^ k) & 1
        halves.append(
            one_hot(col == (row // share ^ slot[0]) * owned + half * share + row % share)
        )
    chosen = jnp.concatenate(halves, axis=0)
    for first in range(0, 9, 2):
        value = dot(chosen, jnp.concatenate(frames[first : first + 2], axis=1))
        for t in range(first, min(first + 2, 9)):
            at = (t - first) * 128 + 32
            for k in range(2):
                part = value[k * 64 : (k + 1) * 64, at : at + 96]
                outs[k][:, t * 96 : (t + 1) * 96] = part.astype(BF16)


def kernel_latent(pack, w2, parts):
    owners = parts.shape[0]
    group = parts.shape[1] // 2
    row, col = iota((CELLS, CELLS), 0), iota((CELLS, CELLS), 1)
    back = one_hot((row // NJ == col % NK) & (row % NJ == col // NK))
    for part, taps_x in enumerate(((1, 2), (0,))):
        joined = {}
        for b in range(3):
            p, sj = TAP_PHASE[b]
            for c in range(3):
                q, sk = TAP_PHASE[c]
                for a in taps_x:
                    tap = 9 * a + 3 * b + c
                    hidden = Phases(pack, 0 if a == 1 else 1)[2 * p + q]
                    weights = w2[tap * 128 : (tap + 1) * 128, :]
                    joined.setdefault(2 * sj + sk, []).append((hidden, weights))
        totals = {
            v: dot(
                jnp.concatenate([hidden for hidden, _ in pairs], axis=1),
                jnp.concatenate([weights for _, weights in pairs], axis=0),
            )
            for v, pairs in joined.items()
        }
        zero = jnp.zeros((NJ, totals[0].shape[1]), F32)

        def later(value):
            return jnp.concatenate([zero, value[: CELLS - NJ]], axis=0)

        inner = totals[2] + later(totals[3])
        inner = jnp.where(iota(inner.shape, 0) % NJ == 0, 0.0, pltpu.roll(inner, 1, axis=0))
        rows = totals[0] + later(totals[1]) + inner
        value = dot(rows.T.astype(BF16), back).reshape(owners, group, CELLS)
        parts[:, part * group : (part + 1) * group] = value.astype(BF16)


def moved_rows(cots, rows_per, order):
    moved = []
    for cot in cots:
        value = dot(cot[...].reshape(-1, CELLS), order).reshape(-1, 2, rows_per, 4 * CELLS)
        moved.append([value[:, s].reshape(-1, 4 * CELLS).astype(BF16) for s in range(2)])
    return [
        [
            jnp.concatenate([m[s][:, v * CELLS : (v + 1) * CELLS] for m in moved], axis=1)
            for v in range(4)
        ]
        for s in range(2)
    ]


def kernel_left(rows_per, *refs):
    *cots, out = refs
    for s, values in enumerate(moved_rows(cots, rows_per, cell_order(True))):
        for v, value in enumerate(values):
            out[s, v] = value


def kernel_two(samples, rows_per, *refs):
    packs, left, refs = refs[:samples], refs[samples], refs[samples + 1 :]
    packed = samples > 1
    if packed:
        ones, outs = refs[:2], refs[2:]
    height = left.shape[2]
    for p in range(2):
        for q in range(2):
            right_0, right_1 = [
                jnp.concatenate([Phases(pack, i)[2 * p + q] for pack in packs], axis=0)
                for i in range(2)
            ]
            both = jnp.concatenate([right_0, right_1], axis=1)
            taps = [
                (b, c)
                for b in range(3)
                for c in range(3)
                if TAP_PHASE[b][0] == p and TAP_PHASE[c][0] == q
            ]
            shifts = [2 * TAP_PHASE[b][1] + TAP_PHASE[c][1] for b, c in taps]
            same = dot(jnp.concatenate([left[0, v] for v in shifts], axis=0), both)
            above = dot(jnp.concatenate([left[1, v] for v in shifts], axis=0), right_1)
            for n, (b, c) in enumerate(taps):
                rows = slice(n * height, (n + 1) * height)
                parts = (above[rows], same[rows, 0:128], same[rows, 128:256])
                for a, value in enumerate(parts):
                    to = (9 * a + 3 * b + c) * 128
                    if packed:
                        spread(value.reshape(-1, rows_per, 128), outs, to)
                    else:
                        refs[0][:, to : to + 128] = value
    if packed:
        total = ones[0][...].astype(F32) + ones[1][...].astype(F32)
        spread(total.reshape(-1, rows_per, WIDTH - ONE_AT), outs, ONE_AT)


def spread(value, outs, at):
    kept, near_1, near_2, near_3, lent, own_far = outs
    lanes = slice(at, at + value.shape[2])
    kept[:, lanes] = value[0]
    for n, near in enumerate((near_1, near_2, near_3), 1):
        near[:, lanes] = value[n].astype(BF16)
    for n in range(2):
        own_far[n, :, lanes] = value[4 + 2 * n]
        lent[n, :, lanes] = value[5 + 2 * n].astype(BF16)


def kernel_far(lent, own_far, *outs):
    for n, out in enumerate(outs):
        out[...] = (own_far[n] + lent[n].astype(F32)).astype(BF16)


def kernel_sum(kept, *refs):
    *others, total_out = refs
    total = kept[...]
    for other in others:
        total = total + other[...].astype(F32)
    total_out[...] = total.astype(BF16)


def join(got, latent):
    slabs, group = got.shape[0], got.shape[1] // 2
    next_ = got[:, group:].astype(F32)
    next_ = jnp.concatenate([jnp.zeros_like(next_[:1]), next_[:-1]], axis=0)
    cells = (got[:, :group].astype(F32) + next_).reshape(-1, CELLS).astype(BF16)
    height = slabs * group
    row, col = iota((height, height), 0), iota((height, height), 1)
    swap = one_hot((row // slabs == col % group) & (row % slabs == col // group))
    latent[...] = dot(swap, cells).reshape(group, slabs, CELLS).astype(BF16)


def kernel_final(pieces, place, *refs):
    parts, (got, one, two, latent) = refs[:pieces], refs[pieces:]
    join(got, latent)
    rows_per = parts[0].shape[0]
    for k in range(pieces):
        at = pl.multiple_of((place[0] ^ k) * rows_per, rows_per)
        two[pl.ds(at, rows_per), :] = parts[k][:, 0:ONE_AT].astype(F32)
    for k in range(2):
        at = pl.multiple_of(((place[0] ^ k) & 1) * rows_per, rows_per)
        shares = [parts[n][:, ONE_AT:WIDTH].astype(F32) for n in (k, k ^ 2)]
        one[pl.ds(at, rows_per), :] = shares[0] + shares[1]


def call(kernel, out_shape, *args, spaces=None, out_spaces=None, scratch=(), vmem=VMEM_LIMIT):
    spaces, out_spaces = spaces or {}, out_spaces or {}
    single = isinstance(out_shape, jax.ShapeDtypeStruct)

    def spec(n, of):
        return pl.BlockSpec(memory_space=of.get(n, pltpu.VMEM))

    moved = sum(x.size * x.dtype.itemsize for x in args)
    return pl.pallas_call(
        kernel,
        out_shape=out_shape,
        in_specs=[spec(n, spaces) for n in range(len(args))],
        out_specs=spec(0, {}) if single else [spec(n, out_spaces) for n in range(len(out_shape))],
        scratch_shapes=list(scratch),
        cost_estimate=pl.CostEstimate(flops=10**9, bytes_accessed=moved, transcendentals=0),
        compiler_params=pltpu.CompilerParams(vmem_limit_bytes=vmem),
    )(*args)


def shape(dims, dtype):
    return jax.ShapeDtypeStruct(dims, dtype)


def swap_ranks(block, axis, k):
    return lax.ppermute(block, axis, [(i, i ^ k) for i in range(lax.axis_size(axis))])


def first_of(value, *others):
    return lax.optimization_barrier((value, *others))[0]


def from_below(block, axis):
    return lax.ppermute(block, axis, [(i - 1, i) for i in range(1, lax.axis_size(axis))])


def on_device(snapshot, conv_one, conv_two, cotangent):
    slabs, samples = lax.axis_size("space"), lax.axis_size("dp")
    group = cotangent.shape[1]
    shared = samples == 4 and slabs == 8
    pieces = samples if shared else 1
    rows_per = group // pieces

    slab = snapshot[0]
    place, slot = [
        lax.axis_index(axis).astype(jnp.int32).reshape(1) for axis in ("dp", "space")
    ]
    parcels, last = call(
        functools.partial(kernel_parcels, pieces),
        (shape((slabs, 2 * group, CELLS), BF16), shape((1,) + slab.shape[1:], BF16)),
        place,
        slot,
        cotangent[0],
        slab,
        spaces={0: pltpu.SMEM, 1: pltpu.SMEM, 2: pltpu.HBM, 3: pltpu.HBM},
        scratch=[pltpu.VMEM((group, slabs, CELLS), BF16), pltpu.SemaphoreType.DMA((2,))],
        vmem=60 * 1024 * 1024,
    )
    halo = from_below(last, "space")
    cot = lax.all_to_all(parcels, "space", split_axis=0, concat_axis=0, tiled=True)
    forward = [pltpu.VMEM((5, 5, CELLS, 128), BF16), pltpu.VMEM((9 * 128, 384), BF16)]
    pack = call(
        kernel_pack, shape((PACK, 64, CELLS), BF16), slab, halo, conv_one, scratch=forward
    )
    ones = call(
        functools.partial(kernel_back, pieces, rows_per),
        (shape((64, 864), BF16),) * 2 if shared else (shape((128, 864), F32),),
        place,
        slot,
        slab,
        halo,
        conv_one,
        conv_two,
        cot,
        spaces={0: pltpu.SMEM, 1: pltpu.SMEM},
        scratch=[pltpu.VMEM((2, 4, 128, CELLS), F32), *forward]
        + [pltpu.VMEM((384, 4 * CELLS), BF16)],
    )

    def left_of(height, *cots):
        moved = shape((2, 4, height, len(cots) * CELLS), BF16)
        return call(functools.partial(kernel_left, rows_per), moved, *cots)

    def latent_of(pack):
        return call(kernel_latent, shape((slabs, 2 * group, CELLS), BF16), pack, conv_two)

    def exchanged(parts):
        return lax.all_to_all(parts, "space", split_axis=0, concat_axis=0, tiled=True)

    latent_shape = shape((group, slabs, CELLS), BF16)

    if not shared:
        two = call(
            functools.partial(kernel_two, 1, rows_per),
            shape((256, 27 * 128), F32),
            pack,
            left_of(256, cot),
        )
        one, two = lax.psum((ones[0], two), "dp")
        one = lax.psum_scatter(one, "space", scatter_dimension=0, tiled=True)
        two = lax.psum_scatter(two, "space", scatter_dimension=0, tiled=True)
        return call(join, latent_shape, exchanged(latent_of(pack)))[None], one, two

    across = swap_ranks(pack, "dp", 2)
    beside = swap_ranks(first_of(pack, cot), "dp", 1)
    own, *cots = call(
        kernel_pieces,
        (shape((slabs, 2 * rows_per, CELLS), BF16),) * pieces,
        place,
        slot,
        cot,
        spaces={0: pltpu.SMEM, 1: pltpu.SMEM},
    )
    cots = [own] + [swap_ranks(piece, "dp", k) for k, piece in enumerate(cots, 1)]
    parts = latent_of(pack)
    one_block = shape((rows_per, WIDTH), BF16)
    kept, near_1, near_2, near_3, lent, own_far = call(
        functools.partial(kernel_two, samples, rows_per),
        (
            shape((rows_per, WIDTH), F32),
            one_block,
            one_block,
            one_block,
            shape((2, rows_per, WIDTH), BF16),
            shape((2, rows_per, WIDTH), F32),
        ),
        pack,
        beside,
        across,
        swap_ranks(first_of(across, *ones, *cots[1:], parts), "dp", 1),
        left_of(slabs * rows_per, *cots),
        ones[0],
        swap_ranks(ones[1], "dp", 1),
    )
    lent = swap_ranks(lent, "space", 1)
    far = call(kernel_far, (one_block, one_block), lent, own_far)
    others = [
        swap_ranks(block, "space", k)
        for k, block in ((1, near_1), (2, near_2), (3, near_3), (4, far[0]), (6, far[1]))
    ]
    got = exchanged(first_of(parts, *far))
    total = call(kernel_sum, one_block, kept, *others)
    totals = [swap_ranks(total, "dp", k) if k else total for k in range(pieces)]
    one, two, latent = call(
        functools.partial(kernel_final, pieces),
        (shape((16, 864), F32), shape((32, 27 * 128), F32), latent_shape),
        place,
        *totals,
        got,
        spaces={0: pltpu.SMEM},
    )
    return latent[None], one, two


def solution(mesh):
    placed = (P("dp", "space", None, None), P(), P(), P("dp", "space", None, None))
    return jax.shard_map(
        on_device,
        mesh=mesh,
        in_specs=placed,
        out_specs=(P("dp", "space", None, None), P("space", None), P("space", None)),
        check_vma=False,
    )
```
